32 devices in a mesh: dp: 16 (over z, x, core), tensor: 2 (over y).
Axes of the slice: x: 2, y: 2, z: 4, core: 2. Of those that a mesh axis runs over, the one named last changes fastest.
Arguments:
- hidden: bfloat16 [7168, 768], P('dp'), may hold values from -6 to 6
- encoder: bfloat16 [16, 1500, 768], P('dp'), may hold values from -6 to 6
- text_len: int32 [16], P('dp'), may hold values from 56 to 448, as said below
- audio_len: int32 [16], P('dp'), may hold values from 375 to 1500, as said below
- corpus_weight: float32 [16], P('dp'), may hold values from 0.5 to 2
- cotangent: bfloat16 [7168, 768], P('dp'), may hold values from -6 to 6
- norm_gain: float32 [3, 768], replicated, may hold values from 0.5 to 1.5
- norm_bias: float32 [3, 768], replicated, may hold values from -1.5 to 1.5
- self_proj: bfloat16 [3, 768, 768], P(None, None, 'tensor'), may hold values from -0.21875 to 0.21875
- self_bias: float32 [2, 768], P(None, 'tensor'), may hold values from -1.5 to 1.5
- cross_proj: bfloat16 [3, 768, 768], P(None, None, 'tensor'), may hold values from -0.21875 to 0.21875
- cross_bias: float32 [2, 768], P(None, 'tensor'), may hold values from -1.5 to 1.5
- out_proj: bfloat16 [2, 768, 768], P(None, 'tensor'), may hold values from -1.75 to 1.75
- out_bias: float32 [2, 768], replicated, may hold values from -1.5 to 1.5
- fc1_weight: bfloat16 [768, 3072], P(None, 'tensor'), may hold values from -0.21875 to 0.21875
- fc1_bias: float32 [3072], P('tensor'), may hold values from -1.5 to 1.5
- fc2_weight: bfloat16 [3072, 768], P('tensor'), may hold values from -0.109375 to 0.109375
- fc2_bias: float32 [768], replicated, may hold values from -1.5 to 1.5
Outputs:
- output: bfloat16 [7168, 768], P('dp')
- grad_hidden: bfloat16 [7168, 768], P('dp')
- grad_encoder: float32 [16, 1500, 768], P('dp')
- norm_gain_grad: float32 [3, 768], replicated
- norm_bias_grad: float32 [3, 768], replicated
- self_proj_grad: float32 [3, 768, 768], P(None, None, 'tensor')
- self_bias_grad: float32 [2, 768], P(None, 'tensor')
- cross_proj_grad: float32 [3, 768, 768], P(None, None, 'tensor')
- cross_bias_grad: float32 [2, 768], P(None, 'tensor')
- out_proj_grad: float32 [2, 768, 768], P(None, 'tensor')
- out_bias_grad: float32 [2, 768], replicated
- fc1_weight_grad: float32 [768, 3072], P(None, 'tensor')
- fc1_bias_grad: float32 [3072], P('tensor')
- fc2_weight_grad: float32 [3072, 768], P('tensor')
- fc2_bias_grad: float32 [768], replicated
The draws below stay inside these ranges and needn't reach their ends.
Inputs may be any that keep to these rules, and one draw needn't show every extreme that they name: `text_len`: one sequence of the batch has all 448 tokens. `audio_len`: one sequence of the batch has all 1500 frames.
All inputs are finite; a program needn't handle non-finite values.
Results may differ from the reference program's by a relative error of at most 0.023.
The reference program's roundings to bfloat16 on the way count: a program that leaves them out, or rounds other values in their place, can miss the bound.
Values sent between devices are 32-bit elements; how exact they have to be, the bound alone decides.
No kernel may reach another device: no remote copies, remote signals or barrier semaphores. Data moves between devices by JAX's collectives and lax.ppermute only.
A program may use at most 256 MiB of HBM per device.

```python
import math
import jax
import jax.numpy as jnp
from jax import lax

D = 768
HEADS = 12
HEAD_DIM = 64
FF = 3072
FRAMES = 1500
SEQ = 448
SEQS_DEV = 1
BATCH = 16
TOKENS = 7168


def draw_text_len(key, part):
    key = jax.random.fold_in(key, 11)
    pick_key, length_key = jax.random.split(key)
    lengths = jax.random.randint(length_key, (BATCH,), SEQ // 8, SEQ + 1)
    chosen = jax.random.randint(pick_key, (), 0, BATCH)
    return jnp.where(jnp.arange(BATCH) == chosen, SEQ, lengths).astype(jnp.int32)


def draw_audio_len(key, part):
    key = jax.random.fold_in(key, 23)
    pick_key, length_key = jax.random.split(key)
    lengths = jax.random.randint(length_key, (BATCH,), FRAMES // 4, FRAMES + 1)
    chosen = jax.random.randint(pick_key, (), 0, BATCH)
    return jnp.where(jnp.arange(BATCH) == chosen, FRAMES, lengths).astype(jnp.int32)


def steps_of(stream_key, shape, cuts, smallest, largest):
    def one(position, shards_of):
        draws = jax.random.uniform(jax.random.fold_in(jax.random.fold_in(stream_key, 6), position), (shards_of,), jnp.float32, smallest / len(cuts), largest / len(cuts))
        return jnp.repeat(jnp.exp(draws), shape[position] // shards_of).reshape((-1,) + (1,) * (len(shape) - position - 1))

    factor_of = one(*cuts[0])
    for cut in cuts[1:]:
        factor_of = factor_of * one(*cut)
    return factor_of


def scatter_about(rng, extent, width, limit, cuts=(), kind=jnp.bfloat16):
    entries = width * jax.random.normal(rng, extent, jnp.float32)
    if cuts:
        entries = entries * steps_of(rng, extent, cuts, -0.22, 0.18)
    return jnp.clip(entries, -limit, limit).astype(kind)


def setup_inputs(seed: int = 0) -> dict:
    key_list = jax.random.split(jax.random.key(seed), 19)
    return {
        "hidden": scatter_about(key_list[0], (TOKENS, D), 1.0, 6.0, ((0, 16),)),
        "encoder": scatter_about(key_list[1], (BATCH, FRAMES, D), 1.0, 6.0, ((0, 16),)),
        "text_len": draw_text_len(jax.random.fold_in(key_list[18], 71), 0),
        "audio_len": draw_audio_len(jax.random.fold_in(key_list[18], 71), 0),
        "corpus_weight": jnp.clip(jnp.exp(math.log(2.0) - 1.3862944 * jax.random.uniform(key_list[4], (BATCH,), jnp.float32) ** steps_of(key_list[4], (BATCH,), ((0, 16),), -0.2, 0.2)), 0.5, 2.0),
        "cotangent": scatter_about(key_list[5], (TOKENS, D), 1.0, 6.0, ((0, 16),)),
        "norm_gain": jnp.clip(1.0 + 0.1 * jax.random.normal(key_list[6], (3, D), jnp.float32), 0.5, 1.5),
        "norm_bias": scatter_about(key_list[7], (3, D), 0.3, 1.5, (), jnp.float32),
        "self_proj": scatter_about(key_list[8], (3, D, D), D ** -0.5, 0.21875, ((2, 2),)),
        "self_bias": scatter_about(key_list[9], (2, D), 0.3, 1.5, ((1, 2),), jnp.float32),
        "cross_proj": scatter_about(key_list[10], (3, D, D), D ** -0.5, 0.21875, ((2, 2),)),
        "cross_bias": scatter_about(key_list[11], (2, D), 0.3, 1.5, ((1, 2),), jnp.float32),
        "out_proj": scatter_about(key_list[12], (2, D, D), (max(D // 64, 4)) ** -0.5, 1.75, ((1, 2),)),
        "out_bias": scatter_about(key_list[13], (2, D), 0.3, 1.5, (), jnp.float32),
        "fc1_weight": scatter_about(key_list[14], (D, FF), D ** -0.5, 0.21875, ((1, 2),)),
        "fc1_bias": scatter_about(key_list[15], (FF,), 0.3, 1.5, ((0, 2),), jnp.float32),
        "fc2_weight": scatter_about(key_list[16], (FF, D), FF ** -0.5, 0.109375, ((0, 2),)),
        "fc2_bias": scatter_about(key_list[17], (D,), 0.3, 1.5, (), jnp.float32),
    }


@jax.custom_vjp
def low(v):
    return lax.optimization_barrier(v.astype(jnp.bfloat16)).astype(jnp.float32)

@jax.custom_vjp
def low_back(v):
    return v

def low_keep(v):
    return (low(v), None)

def low_pass(kept, grad):
    return (grad,)

def back_keep(v):
    return (v, None)

def back_low(kept, grad):
    return (low(grad),)
low.defvjp(low_keep, low_pass)
low_back.defvjp(back_keep, back_low)
epsilon = 1e-05
masked_value = -1e+30
highest = lax.Precision.HIGHEST

def layer_norm(values, gain, shift):
    mean_value = lax.optimization_barrier(jnp.mean(values, axis=-1, keepdims=True))
    centered = values - mean_value
    variance = lax.optimization_barrier(jnp.mean(centered * centered, axis=-1, keepdims=True))
    return centered * lax.rsqrt(variance + epsilon) * gain + shift

def project(values, matrix):
    return jnp.einsum('...d,de->...e', values, matrix, precision=highest)

def attend(queries, keys_all, values_all, allowed):
    queries = queries.reshape(queries.shape[:-1] + (HEADS, HEAD_DIM))
    keys_all = keys_all.reshape(keys_all.shape[:-1] + (HEADS, HEAD_DIM))
    values_all = values_all.reshape(values_all.shape[:-1] + (HEADS, HEAD_DIM))
    scores = low_back(jnp.einsum('sqhc,skhc->shqk', queries, keys_all, precision=highest))
    scores = jnp.where(allowed[:, None], scores, masked_value)
    weights = jax.nn.softmax(scores, axis=-1)
    mixed = jnp.einsum('shqk,skhc->sqhc', low(weights), values_all, precision=highest)
    return low(low_back(mixed.reshape(mixed.shape[:2] + (D,))))

def block_forward(params, hidden, encoder, text_len, audio_len):
    norm_gain, norm_bias, self_proj, self_bias, cross_proj, cross_bias, out_proj, out_bias, fc1_weight, fc1_bias, fc2_weight, fc2_bias = params
    scale = HEAD_DIM ** (-0.5)
    sequences = hidden.shape[0]
    places = jnp.arange(SEQ)
    frame_places = jnp.arange(FRAMES)
    self_allowed = (places[None, :, None] >= places[None, None, :]) & (places[None, None, :] < text_len[:, None, None])
    cross_allowed = jnp.broadcast_to(frame_places[None, None, :] < audio_len[:, None, None], (sequences, SEQ, FRAMES))
    normed = low(layer_norm(hidden, norm_gain[0], norm_bias[0]))
    queries = low(low_back((project(normed, self_proj[0]) + self_bias[0]) * scale))
    keys_all = low(low_back(project(normed, self_proj[1])))
    values_all = low(low_back(project(normed, self_proj[2]) + self_bias[1]))
    heads = attend(queries, keys_all, values_all, self_allowed)
    first = hidden + low_back(project(heads, out_proj[0])) + out_bias[0]
    normed = low(layer_norm(first, norm_gain[1], norm_bias[1]))
    queries = low(low_back((project(normed, cross_proj[0]) + cross_bias[0]) * scale))
    keys_all = low(low_back(project(encoder, cross_proj[1])))
    values_all = low(low_back(project(encoder, cross_proj[2]) + cross_bias[1]))
    heads = attend(queries, keys_all, values_all, cross_allowed)
    second = first + low_back(project(heads, out_proj[1])) + out_bias[1]
    normed = low(layer_norm(second, norm_gain[2], norm_bias[2]))
    inner = low(jax.nn.gelu(low_back(project(normed, fc1_weight) + fc1_bias), approximate=False))
    return second + low_back(project(inner, fc2_weight)) + fc2_bias

def reference(hidden, encoder, text_len, audio_len, corpus_weight, cotangent, norm_gain, norm_bias, self_proj, self_bias, cross_proj, cross_bias, out_proj, out_bias, fc1_weight, fc1_bias, fc2_weight, fc2_bias):
    params = tuple((array.astype(jnp.float32) for array in (norm_gain, norm_bias, self_proj, self_bias, cross_proj, cross_bias, out_proj, out_bias, fc1_weight, fc1_bias, fc2_weight, fc2_bias)))
    batch_size = text_len.shape[0]
    groups = batch_size // SEQS_DEV
    hidden_groups = hidden.astype(jnp.float32).reshape(groups, SEQS_DEV, SEQ, D)
    encoder_groups = encoder.astype(jnp.float32).reshape(groups, SEQS_DEV, FRAMES, D)
    text_groups = text_len.reshape(groups, SEQS_DEV)
    audio_groups = audio_len.reshape(groups, SEQS_DEV)
    places = jnp.arange(SEQ)
    live = (places[None, :] < text_len[:, None]).astype(jnp.float32) * corpus_weight.astype(jnp.float32)[:, None]
    seed_grad = (cotangent.astype(jnp.float32).reshape(batch_size, SEQ, D) * live[:, :, None]).reshape(groups, SEQS_DEV, SEQ, D)

    def whole(params_all, hidden_all, encoder_all):
        checked = jax.checkpoint(block_forward)

        def one_group(carry, pieces):
            return (carry, checked(params_all, pieces[0], pieces[1], pieces[2], pieces[3]))
        return lax.scan(one_group, None, (hidden_all, encoder_all, text_groups, audio_groups))[1]
    result, pullback = jax.vjp(whole, params, hidden_groups, encoder_groups)
    grads, grad_hidden, grad_encoder = pullback(seed_grad)
    return (result.reshape(batch_size * SEQ, D).astype(jnp.bfloat16), grad_hidden.reshape(batch_size * SEQ, D).astype(jnp.bfloat16), grad_encoder.reshape(batch_size, FRAMES, D), grads[0], grads[1], grads[2], grads[3], grads[4], grads[5], grads[6], grads[7], grads[8], grads[9], grads[10], grads[11])
```

```python
from functools import partial

import jax
import jax.numpy as jnp
import numpy as np
from jax import lax
from jax.experimental import pallas as pl
from jax.experimental.pallas import tpu as pltpu
from jax.sharding import PartitionSpec as P

HEAD_DIM = 64
SCALE = HEAD_DIM ** (-0.5)
PAIR = 2 * HEAD_DIM
LANES = 128
epsilon = 1e-05
masked_value = -1e30
f32 = jnp.float32
bf16 = jnp.bfloat16


def dot(a, b, ca, cb):
    return lax.dot_general(a, b, (((ca,), (cb,)), ((), ())), preferred_element_type=f32)


def norm_forward(values, gain, shift):
    centered = values - jnp.mean(values, axis=-1, keepdims=True)
    inverse = lax.rsqrt(jnp.mean(centered * centered, axis=-1, keepdims=True) + epsilon)
    unit = centered * inverse
    return (unit * gain + shift, unit, inverse)


def norm_backward(incoming, unit, inverse, gain):
    scaled = incoming * gain
    scaled_mean = jnp.mean(scaled, axis=-1, keepdims=True)
    along_unit = jnp.mean(scaled * unit, axis=-1, keepdims=True)
    return inverse * (scaled - scaled_mean - unit * along_unit)


def lane_masks(rows):
    lanes = lax.broadcasted_iota(jnp.int32, (rows, PAIR), 1)
    return lanes < HEAD_DIM


def allowed_of(length, rows, columns, causal):
    places = lax.broadcasted_iota(jnp.int32, (rows, columns), 1)
    allowed = places < length
    if causal:
        allowed = allowed & (places <= lax.broadcasted_iota(jnp.int32, (rows, columns), 0))
    return allowed


def attend_forward_kernel(causal, length_ref, q_ref, k_ref, v_ref, heads_ref, weights_ref, inverse_ref):
    rows, columns = q_ref.shape[0], k_ref.shape[0]
    length = length_ref[0]
    first_lanes = lane_masks(rows)
    if causal:
        allowed = allowed_of(length, rows, columns, True)
    else:
        places = lax.broadcasted_iota(jnp.int32, (1, columns), 1)
        shift = jnp.where(places < length, 0.0, masked_value)
    q = q_ref[...]
    k = k_ref[...]
    v = v_ref[...]
    mixed = []
    inverses = []
    for head in range(2):
        mine = first_lanes if head == 0 else jnp.logical_not(first_lanes)
        scores = dot(jnp.where(mine, q, jnp.zeros_like(q)), k, 1, 1)
        if causal:
            scores = jnp.where(allowed, scores, masked_value)
        else:
            scores = scores + shift
        largest = jnp.max(scores, axis=-1, keepdims=True)
        weights = jnp.exp(scores - largest)
        inverse = 1.0 / jnp.sum(weights, axis=-1, keepdims=True)
        weights = weights.astype(bf16)
        weights_ref[head] = weights
        mixed.append(dot(weights, v, 1, 0) * inverse)
        inverses.append(inverse)
    heads_ref[...] = jnp.where(first_lanes, mixed[0], mixed[1]).astype(bf16)
    inverse_ref[...] = jnp.where(first_lanes, inverses[0], inverses[1])


def attend_forward(length, q, k, v, causal):
    rows, width = q.shape
    columns = k.shape[0]
    pairs = width // PAIR
    return pl.pallas_call(
        partial(attend_forward_kernel, causal),
        grid=(pairs,),
        in_specs=[
            pl.BlockSpec(memory_space=pltpu.SMEM),
            pl.BlockSpec((rows, PAIR), lambda p: (0, p)),
            pl.BlockSpec((columns, PAIR), lambda p: (0, p)),
            pl.BlockSpec((columns, PAIR), lambda p: (0, p)),
        ],
        out_specs=[
            pl.BlockSpec((rows, PAIR), lambda p: (0, p)),
            pl.BlockSpec((2, rows, columns), lambda p: (p, 0, 0)),
            pl.BlockSpec((rows, PAIR), lambda p: (0, p)),
        ],
        out_shape=[
            jax.ShapeDtypeStruct((rows, width), bf16),
            jax.ShapeDtypeStruct((2 * pairs, rows, columns), bf16),
            jax.ShapeDtypeStruct((rows, width), f32),
        ],
        compiler_params=pltpu.CompilerParams(vmem_limit_bytes=40 * 1024 * 1024),
        cost_estimate=pl.CostEstimate(
            flops=4 * rows * columns * width * 3,
            bytes_accessed=4 * pairs * rows * columns,
            transcendentals=2 * pairs * rows * columns,
        ),
        name="attend_fwd_causal" if causal else "attend_fwd_cross",
    )(length, q, k, v)


def attend_backward_kernel(q_ref, k_ref, v_ref, weights_ref, inverse_ref, heads_ref, grad_ref, dq_ref, dk_ref, dv_ref):
    rows = q_ref.shape[0]
    first_lanes = lane_masks(rows)
    q = q_ref[...]
    k = k_ref[...]
    v = v_ref[...]
    grad = (grad_ref[...].astype(f32) * inverse_ref[...]).astype(bf16)
    along = grad.astype(f32) * heads_ref[...].astype(f32)
    dq = []
    dk = None
    dv = None
    for head in range(2):
        mine = first_lanes if head == 0 else jnp.logical_not(first_lanes)
        grad_one = jnp.where(mine, grad, jnp.zeros_like(grad))
        q_one = jnp.where(mine, q, jnp.zeros_like(q))
        row_terms = jnp.sum(jnp.where(mine, along, 0.0), axis=-1, keepdims=True)
        weights = weights_ref[head]
        grad_probs = dot(grad_one, v, 1, 1)
        grad_scores = (weights.astype(f32) * (grad_probs - row_terms)).astype(bf16)
        dv_one = dot(grad_one, weights, 0, 0)
        dk_one = dot(q_one, grad_scores, 0, 0)
        dq.append(dot(grad_scores, k, 1, 0))
        dk = dk_one if dk is None else dk + dk_one
        dv = dv_one if dv is None else dv + dv_one
    dq_ref[...] = (jnp.where(first_lanes, dq[0], dq[1]) * SCALE).astype(bf16)
    dk_ref[...] = dk.astype(bf16)
    dv_ref[...] = dv.astype(bf16)


def attend_backward(q, k, v, weights, inverse, heads, grad):
    rows, width = q.shape
    columns = k.shape[0]
    pairs = width // PAIR
    row_block = pl.BlockSpec((rows, PAIR), lambda p: (0, p))
    column_block = pl.BlockSpec((columns, PAIR), lambda p: (0, p))
    flipped = pl.BlockSpec((PAIR, columns), lambda p: (p, 0))
    return pl.pallas_call(
        attend_backward_kernel,
        grid=(pairs,),
        in_specs=[
            row_block,
            column_block,
            column_block,
            pl.BlockSpec((2, rows, columns), lambda p: (p, 0, 0)),
            row_block,
            row_block,
            row_block,
        ],
        out_specs=[row_block, flipped, flipped],
        out_shape=[
            jax.ShapeDtypeStruct((rows, width), bf16),
            jax.ShapeDtypeStruct((width, columns), bf16),
            jax.ShapeDtypeStruct((width, columns), bf16),
        ],
        compiler_params=pltpu.CompilerParams(vmem_limit_bytes=40 * 1024 * 1024),
        cost_estimate=pl.CostEstimate(
            flops=8 * rows * columns * width * 3,
            bytes_accessed=4 * pairs * rows * columns,
            transcendentals=0,
        ),
        name="attend_bwd",
    )(q, k, v, weights, inverse, heads, grad)


def join_kernel(axis, side_ref, own_ref, other_ref, whole_ref):
    own = own_ref[0].astype(f32)
    other = other_ref[0]
    first = side_ref[0] == 0
    low = jnp.where(first, own, other).astype(bf16)
    high = jnp.where(first, other, own).astype(bf16)
    extent = own.shape[axis - 1]
    if axis == 2:
        whole_ref[0, :, :extent] = low
        whole_ref[0, :, extent:] = high
    else:
        whole_ref[0, :extent, :] = low
        whole_ref[0, extent:, :] = high


def join_halves(side, own, other, axis):
    count, rows, columns = own.shape
    shape = (rows, 2 * columns) if axis == 2 else (2 * rows, columns)
    return pl.pallas_call(
        partial(join_kernel, axis),
        grid=(count,),
        in_specs=[
            pl.BlockSpec(memory_space=pltpu.SMEM),
            pl.BlockSpec((1, rows, columns), lambda p: (p, 0, 0)),
            pl.BlockSpec((1, rows, columns), lambda p: (p, 0, 0)),
        ],
        out_specs=pl.BlockSpec((1,) + shape, lambda p: (p, 0, 0)),
        out_shape=jax.ShapeDtypeStruct((count,) + shape, bf16),
        name="join_halves",
    )(side, own, other)


def swap(value):
    return lax.ppermute(value, "tensor", [(0, 1), (1, 0)])


def sum_tensor(value):
    if lax.axis_size("tensor") == 2:
        return value + swap(value)
    return lax.psum(value, "tensor")


def scatter_sum(arrays):
    members = lax.axis_size("dp")
    bits = members.bit_length() - 1
    me = lax.axis_index("dp")
    parts = [a.reshape((2,) * bits + (a.shape[0] // members, a.shape[1])) for a in arrays]
    total = None
    for bit in range(bits):
        axis = bits - 1 - bit
        side = (me >> bit) & 1
        pairs = [(i, i ^ (1 << bit)) for i in range(members)]
        mine = [lax.dynamic_index_in_dim(a, side, axis, keepdims=True) for a in parts]
        theirs = [lax.dynamic_index_in_dim(a, 1 - side, axis, keepdims=True) for a in parts]
        if len(parts) > 1:
            mine = [jnp.concatenate(mine, axis=-2)]
            theirs = [jnp.concatenate(theirs, axis=-2)]
        total = mine[0] + lax.ppermute(theirs[0], "dp", pairs)
        parts = [total]
    return total.reshape(total.shape[-2:])


def gather_parts(share, counts):
    whole = lax.all_gather(share, "dp", axis=0, tiled=False)
    pieces = []
    offset = 0
    for count in counts:
        pieces.append(whole[:, offset : offset + count].reshape(-1, share.shape[1]))
        offset += count
    return pieces


def column_blocks(value, width):
    blocks = value.shape[1] // width
    if blocks == 1:
        return value
    return jnp.concatenate([value[:, i * width : (i + 1) * width] for i in range(blocks)], axis=0)


def from_column_blocks(value, blocks):
    if blocks == 1:
        return value
    rows = value.shape[0] // blocks
    return jnp.concatenate([value[i * rows : (i + 1) * rows] for i in range(blocks)], axis=1)


def per_device(
    hidden,
    encoder,
    text_len,
    audio_len,
    corpus_weight,
    cotangent,
    norm_gain,
    norm_bias,
    self_proj,
    self_bias,
    cross_proj,
    cross_bias,
    out_proj,
    out_bias,
    fc1_weight,
    fc1_bias,
    fc2_weight,
    fc2_bias,
):
    sequences, frames, width = encoder.shape
    length = hidden.shape[0]
    members = lax.axis_size("dp")
    me = lax.axis_index("dp")
    side = lax.axis_index("tensor")
    half = self_proj.shape[2]
    padded = -(-frames // 256) * 256

    proj_rows = cross_proj.reshape(-1, half)
    out_rows = out_proj[1]
    proj_count = proj_rows.shape[0] // members
    out_count = out_rows.shape[0] // members
    out_part = lax.dynamic_slice_in_dim(out_rows, me * out_count, out_count, 0)
    part = jnp.concatenate(
        [
            lax.dynamic_slice_in_dim(proj_rows, me * proj_count, proj_count, 0).astype(f32),
            column_blocks(out_part, half).astype(f32),
            cross_bias,
        ],
        axis=0,
    )
    part = swap(part)
    sent = proj_count + 2 * out_count
    other_bias = part[sent:]
    gathered = lax.all_gather(part[:sent], "dp", axis=0, tiled=False)

    residual = hidden.astype(f32)
    normed, unit_self, inverse_self = norm_forward(residual, norm_gain[0], norm_bias[0])
    normed_self = normed.astype(bf16)
    query_self = ((dot(normed_self, self_proj[0], 1, 0) + self_bias[0]) * SCALE).astype(bf16)
    keys_self = dot(normed_self, self_proj[1], 1, 0).astype(bf16)
    values_self = (dot(normed_self, self_proj[2], 1, 0) + self_bias[1]).astype(bf16)
    heads_self, weights_self, totals_self = attend_forward(text_len, query_self, keys_self, values_self, True)
    partial_self = dot(heads_self, out_proj[0], 1, 0)
    first = residual + sum_tensor(partial_self) + out_bias[0]

    other_out = from_column_blocks(
        gathered[:, proj_count:].reshape(members, 2, out_count, half).swapaxes(0, 1).reshape(-1, half), 2
    )
    here = side.astype(jnp.int32).reshape(1)
    full_proj = join_halves(here, cross_proj, gathered[:, :proj_count].reshape(cross_proj.shape), 2)
    full_out = join_halves(here, out_proj[1:], other_out[None], 1)[0]
    full_bias = jnp.where(
        side == 0,
        jnp.concatenate([cross_bias, other_bias], axis=1),
        jnp.concatenate([other_bias, cross_bias], axis=1),
    )
    frames_in = jnp.pad(encoder.reshape(frames, width), ((0, padded - frames), (0, 0)))
    keys_cross = dot(frames_in, full_proj[1], 1, 0).astype(bf16)
    values_cross = (dot(frames_in, full_proj[2], 1, 0) + full_bias[1]).astype(bf16)

    normed, unit_cross, inverse_cross = norm_forward(first, norm_gain[1], norm_bias[1])
    normed_cross = normed.astype(bf16)
    query_cross = ((dot(normed_cross, full_proj[0], 1, 0) + full_bias[0]) * SCALE).astype(bf16)
    heads_cross, weights_cross, totals_cross = attend_forward(
        audio_len, query_cross, keys_cross, values_cross, False
    )
    second = first + dot(heads_cross, full_out, 1, 0) + out_bias[1]

    normed, unit_mlp, inverse_mlp = norm_forward(second, norm_gain[2], norm_bias[2])
    normed_mlp = normed.astype(bf16)
    pre_act = dot(normed_mlp, fc1_weight, 1, 0) + fc1_bias
    inner = jax.nn.gelu(pre_act, approximate=False).astype(bf16)
    partial_mlp = dot(inner, fc2_weight, 1, 0)

    live = jnp.where(jnp.arange(length) < text_len[0], corpus_weight[0], 0.0).reshape(-1, 1)
    grad_y = cotangent.astype(f32) * live
    grad_low = grad_y.astype(bf16)
    grad_inner = dot(grad_low, fc2_weight, 1, 1)
    _, gelu_back = jax.vjp(partial(jax.nn.gelu, approximate=False), pre_act)
    grad_pre = gelu_back(grad_inner)[0].astype(bf16)
    grad_normed = sum_tensor(dot(grad_pre, fc1_weight, 1, 1))
    fc2_weight_grad = dot(inner, grad_low, 0, 0)
    fc1_weight_grad = dot(normed_mlp, grad_pre, 0, 0)
    fc1_bias_grad = jnp.sum(grad_pre.astype(f32), axis=0)
    fc2_bias_grad = jnp.sum(grad_y, axis=0)
    fc1_blocks = fc1_weight_grad.shape[1] // width
    mlp_share = scatter_sum([fc2_weight_grad, column_blocks(fc1_weight_grad, width)])
    fc2_count = fc2_weight_grad.shape[0] // members
    fc2_weight_grad, fc1_rows = gather_parts(mlp_share, [fc2_count, mlp_share.shape[0] - fc2_count])
    fc1_weight_grad = from_column_blocks(fc1_rows, fc1_blocks)

    gain_mlp = jnp.sum(grad_normed * unit_mlp, axis=0)
    shift_mlp = jnp.sum(grad_normed, axis=0)
    grad_second = grad_y + norm_backward(grad_normed, unit_mlp, inverse_mlp, norm_gain[2])
    result = second + sum_tensor(partial_mlp) + fc2_bias

    second_low = grad_second.astype(bf16)
    grad_heads = dot(second_low, full_out, 1, 1).astype(bf16)
    grad_query, grad_keys, grad_values = attend_backward(
        query_cross, keys_cross, values_cross, weights_cross, totals_cross, heads_cross, grad_heads
    )
    grad_normed = dot(grad_query, full_proj[0], 1, 1)
    gain_cross = jnp.sum(grad_normed * unit_cross, axis=0)
    shift_cross = jnp.sum(grad_normed, axis=0)
    grad_first = grad_second + norm_backward(grad_normed, unit_cross, inverse_cross, norm_gain[1])

    own_heads = lax.dynamic_slice_in_dim(heads_cross, side * half, half, 1)
    own_query = lax.dynamic_slice_in_dim(grad_query, side * half, half, 1)
    own_keys = lax.dynamic_slice_in_dim(grad_keys, side * half, half, 0)
    own_values = lax.dynamic_slice_in_dim(grad_values, side * half, half, 0)
    out_cross_grad = dot(own_heads, second_low, 0, 0)
    cross_proj_grad = jnp.concatenate(
        [
            dot(normed_cross, own_query, 0, 0),
            dot(frames_in, own_keys, 0, 1),
            dot(frames_in, own_values, 0, 1),
        ],
        axis=0,
    )
    cross_bias_grad = jnp.stack(
        [jnp.sum(own_query.astype(f32), axis=0), jnp.sum(own_values.astype(f32), axis=1)]
    )
    out_cross_bias = jnp.sum(grad_second, axis=0)
    cross_share = scatter_sum([cross_proj_grad, column_blocks(out_cross_grad, half)])
    proj_grad_count = cross_proj_grad.shape[0] // members
    cross_rows, out_cross_rows = gather_parts(cross_share, [proj_grad_count, cross_share.shape[0] - proj_grad_count])
    grad_encoder = (
        dot(grad_keys, full_proj[1], 0, 1) + dot(grad_values, full_proj[2], 0, 1)
    )[:frames].reshape(encoder.shape)

    first_low = grad_first.astype(bf16)
    grad_heads = dot(first_low, out_proj[0], 1, 1).astype(bf16)
    grad_query, grad_keys, grad_values = attend_backward(
        query_self, keys_self, values_self, weights_self, totals_self, heads_self, grad_heads
    )
    normed_part = (
        dot(grad_query, self_proj[0], 1, 1)
        + dot(grad_keys, self_proj[1], 0, 1)
        + dot(grad_values, self_proj[2], 0, 1)
    )
    norm_part = swap(
        jnp.stack([jnp.sum(normed_part * unit_self, axis=0), jnp.sum(normed_part, axis=0)])
    ) + jnp.stack([jnp.sum(normed_part * unit_self, axis=0), jnp.sum(normed_part, axis=0)])
    gain_self, shift_self = norm_part[0], norm_part[1]
    self_proj_grad = jnp.concatenate(
        [
            dot(normed_self, grad_query, 0, 0),
            dot(normed_self, grad_keys, 0, 1),
            dot(normed_self, grad_values, 0, 1),
        ],
        axis=0,
    )
    self_bias_grad = jnp.stack(
        [jnp.sum(grad_query.astype(f32), axis=0), jnp.sum(grad_values.astype(f32), axis=1)]
    )
    out_self_grad = dot(heads_self, first_low, 0, 0)
    out_self_bias = jnp.sum(grad_first, axis=0)

    small = (
        jnp.stack([gain_self, gain_cross, gain_mlp]),
        jnp.stack([shift_self, shift_cross, shift_mlp]),
        self_bias_grad,
        cross_bias_grad,
        jnp.stack([out_self_bias, out_cross_bias]),
        fc1_bias_grad,
        fc2_bias_grad,
    )
    flat = jnp.concatenate([item.reshape(-1) for item in small])
    unit_rows = 8 * members
    small_rows = -(-flat.shape[0] // (half * unit_rows)) * unit_rows
    flat = jnp.pad(flat, (0, small_rows * half - flat.shape[0])).reshape(small_rows, half)
    self_share = scatter_sum([self_proj_grad, column_blocks(out_self_grad, half), flat])
    out_grad_count = out_self_grad.shape[0] * 2 // members
    self_rows, out_self_rows, flat = gather_parts(
        self_share, [proj_grad_count, out_grad_count, small_rows // members]
    )
    grad_normed = sum_tensor(normed_part)
    grad_hidden = (grad_first + norm_backward(grad_normed, unit_self, inverse_self, norm_gain[0])).astype(bf16)

    flat = flat.reshape(-1)
    small_out = []
    offset = 0
    for item in small:
        small_out.append(flat[offset : offset + item.size].reshape(item.shape))
        offset += item.size
    return (
        result.astype(bf16),
        grad_hidden,
        grad_encoder,
        small_out[0],
        small_out[1],
        self_rows.reshape(self_proj.shape),
        small_out[2],
        cross_rows.reshape(cross_proj.shape),
        small_out[3],
        jnp.stack([from_column_blocks(out_self_rows, 2), from_column_blocks(out_cross_rows, 2)]),
        small_out[4],
        fc1_weight_grad,
        small_out[5],
        fc2_weight_grad,
        small_out[6],
    )


def solution(mesh):
    placed = (
        P("dp", None),
        P("dp", None, None),
        P("dp"),
        P("dp"),
        P("dp"),
        P("dp", None),
        P(),
        P(),
        P(None, None, "tensor"),
        P(None, "tensor"),
        P(None, None, "tensor"),
        P(None, "tensor"),
        P(None, "tensor", None),
        P(),
        P(None, "tensor"),
        P("tensor"),
        P("tensor", None),
        P(),
    )
    return jax.shard_map(
        per_device,
        mesh=mesh,
        in_specs=placed,
        out_specs=(
            P("dp", None),
            P("dp", None),
            P("dp", None, None),
            P(),
            P(),
            P(None, None, "tensor"),
            P(None, "tensor"),
            P(None, None, "tensor"),
            P(None, "tensor"),
            P(None, "tensor", None),
            P(),
            P(None, "tensor"),
            P("tensor"),
            P("tensor", None),
            P(),
        ),
        check_vma=False,
    )
```

```python
from functools import partial

import jax
import jax.numpy as jnp
from jax import lax
from jax.experimental import pallas as pl
from jax.experimental.pallas import tpu as pltpu
from jax.sharding import PartitionSpec as P

HEAD_DIM = 64
SCALE = HEAD_DIM ** (-0.5)
PAIR = 2 * HEAD_DIM
FF_BLOCK = 256
FRAME_BLOCK = 256
VMEM_LIMIT = 58 * 1024 * 1024
COST_SHARE = 64
epsilon = 1e-05
masked_value = -1e30
f32 = jnp.float32
bf16 = jnp.bfloat16


def dot(a, b, ca, cb):
    return lax.dot_general(a, b, (((ca,), (cb,)), ((), ())), preferred_element_type=f32)


def shaped(shape, dtype):
    return jax.ShapeDtypeStruct(shape, dtype)


class Source:
    def __init__(self, ref, held, sems, first_sem, pieces):
        self.held, self.shape, self.dtype = held, held.shape, held.dtype
        self.size = held.shape[0] // pieces
        self.ref, self.sems, self.first_sem = ref, sems, first_sem
        self.copies = [None] * pieces
        self.pending = [True] * pieces

    def fetch(self, *pieces):
        for piece in pieces or range(len(self.copies)):
            if self.copies[piece] is None:
                here = pl.ds(piece * self.size, self.size)
                self.copies[piece] = pltpu.make_async_copy(
                    self.ref.at[here], self.held.at[here], self.sems.at[self.first_sem + piece]
                )
                self.copies[piece].start()

    def wait(self, piece):
        if self.pending[piece]:
            self.fetch(piece)
            self.pending[piece] = False
            self.copies[piece].wait()

    def __getitem__(self, index):
        if len(self.copies) > 1 and isinstance(index, int):
            self.wait(index // self.size)
        else:
            for piece in range(len(self.copies)):
                self.wait(piece)
        return self.held[index]


class Sink:
    def __init__(self, ref, held, sems, first_sem, pieces):
        self.held, self.shape, self.dtype = held, held.shape, held.dtype
        self.size = held.shape[0] // pieces
        self.copies = []
        self.sent = []
        for i in range(pieces):
            here = pl.ds(i * self.size, self.size)
            self.copies.append(pltpu.make_async_copy(held.at[here], ref.at[here], sems.at[first_sem + i]))
            self.sent.append(False)

    def __getitem__(self, index):
        return self.held[index]

    def __setitem__(self, index, value):
        self.held[index] = value

    def send(self, piece=0):
        self.sent[piece] = True
        self.copies[piece].start()


def call(kernel, name, out_shape, flops, early, scalars, *arrays):
    arrays = [a if isinstance(a, tuple) else (a, 1) for a in arrays]
    outs = [o if isinstance(o, tuple) else (o, 1) for o in out_shape]
    in_pieces = [pieces for _, pieces in arrays]
    out_pieces = [pieces for _, pieces in outs]
    arrays = [a for a, _ in arrays]
    outs = [o for o, _ in outs]
    moved = sum(a.size * a.dtype.itemsize for a in (*arrays, *outs))

    def body(*refs):
        refs = list(refs)
        scalar_refs = [refs.pop(0) for _ in scalars]
        in_refs = [refs.pop(0) for _ in arrays]
        out_refs = [refs.pop(0) for _ in outs]
        in_held = [refs.pop(0) for _ in arrays]
        out_held = [refs.pop(0) for _ in outs]
        in_sems, out_sems = refs
        sources = []
        for i, (ref, held) in enumerate(zip(in_refs, in_held)):
            sources.append(Source(ref, held, in_sems, sum(in_pieces[:i]), in_pieces[i]))
        sinks = []
        for i, (ref, held) in enumerate(zip(out_refs, out_held)):
            sinks.append(Sink(ref, held, out_sems, sum(out_pieces[:i]), out_pieces[i]))
        for source in sources[:early]:
            source.fetch()
        kernel(*scalar_refs, *sources, *sinks)
        for source in sources:
            for piece in range(len(source.copies)):
                if source.copies[piece] is not None:
                    source.wait(piece)
        for sink in sinks:
            for piece, sent in enumerate(sink.sent):
                if not sent:
                    sink.send(piece)
        for sink in sinks:
            for copy in sink.copies:
                copy.wait()

    anywhere = pl.BlockSpec(memory_space=pl.ANY)
    return pl.pallas_call(
        body,
        in_specs=[pl.BlockSpec(memory_space=pltpu.SMEM)] * len(scalars) + [anywhere] * len(arrays),
        out_specs=[anywhere] * len(outs),
        out_shape=outs,
        scratch_shapes=[pltpu.VMEM(a.shape, a.dtype) for a in (*arrays, *outs)]
        + [pltpu.SemaphoreType.DMA((sum(in_pieces),)), pltpu.SemaphoreType.DMA((sum(out_pieces),))],
        compiler_params=pltpu.CompilerParams(vmem_limit_bytes=VMEM_LIMIT),
        cost_estimate=pl.CostEstimate(flops=flops // COST_SHARE, bytes_accessed=moved // COST_SHARE, transcendentals=0),
        name=name,
    )(*scalars, *arrays)


def lanes_of(pair):
    return slice(pair * PAIR, (pair + 1) * PAIR)


def add_up(terms):
    total = terms[0]
    for term in terms[1:]:
        total = total + term
    return total


def norm_unit(values):
    centered = values - jnp.mean(values, axis=-1, keepdims=True)
    inverse = lax.rsqrt(jnp.mean(centered * centered, axis=-1, keepdims=True) + epsilon)
    return centered * inverse, inverse


def norm_backward(incoming, unit, inverse, gain):
    scaled = incoming * gain
    scaled_mean = jnp.mean(scaled, axis=-1, keepdims=True)
    along_unit = jnp.mean(scaled * unit, axis=-1, keepdims=True)
    return inverse * (scaled - scaled_mean - unit * along_unit)


def column_sum(values):
    return jnp.sum(values, axis=0, keepdims=True)


def live_gradient(cotangent, text_len, corpus_weight):
    places = lax.broadcasted_iota(jnp.int32, (cotangent.shape[0], 1), 0)
    live = jnp.where(places < text_len, corpus_weight, 0.0)
    return cotangent.astype(f32) * live


def lane_masks(rows):
    return lax.broadcasted_iota(jnp.int32, (rows, PAIR), 1) < HEAD_DIM


def pair_forward(length, causal, q, k, v, weights_ref, start):
    rows, columns = q.shape[0], k.shape[0]
    first_lanes = lane_masks(rows)
    if causal:
        places = lax.broadcasted_iota(jnp.int32, (rows, columns), 1)
        allowed = (places < length) & (places <= lax.broadcasted_iota(jnp.int32, (rows, columns), 0))
    else:
        places = lax.broadcasted_iota(jnp.int32, (1, columns), 1)
        shift = jnp.where(places < length, 0.0, masked_value)
    scores = []
    for head in range(2):
        mine = first_lanes if head == 0 else jnp.logical_not(first_lanes)
        raw = dot(jnp.where(mine, q, jnp.zeros_like(q)), k, 1, 1)
        scores.append(jnp.where(allowed, raw, masked_value) if causal else raw + shift)
    inverses = []
    for head in range(2):
        largest = jnp.max(scores[head], axis=-1, keepdims=True)
        weights = jnp.exp(scores[head] - largest)
        inverses.append(1.0 / jnp.sum(weights, axis=-1, keepdims=True))
        weights_ref[start + head] = weights.astype(bf16)
    mixed = [dot(weights_ref[start + head], v, 1, 0) for head in range(2)]
    inverse = jnp.where(first_lanes, inverses[0], inverses[1])
    return (jnp.where(first_lanes, mixed[0], mixed[1]) * inverse).astype(bf16), inverse


def pair_backward(q, k, v, weights_ref, start, inverse, heads, grad_heads):
    first_lanes = lane_masks(q.shape[0])
    grad = (grad_heads.astype(f32) * inverse).astype(bf16)
    along = grad.astype(f32) * heads.astype(f32)
    dq = []
    dk = None
    dv = None
    for head in range(2):
        mine = first_lanes if head == 0 else jnp.logical_not(first_lanes)
        grad_one = jnp.where(mine, grad, jnp.zeros_like(grad))
        q_one = jnp.where(mine, q, jnp.zeros_like(q))
        row_terms = jnp.sum(jnp.where(mine, along, 0.0), axis=-1, keepdims=True)
        weights = weights_ref[start + head]
        grad_probs = dot(grad_one, v, 1, 1)
        grad_scores = (weights.astype(f32) * (grad_probs - row_terms)).astype(bf16)
        dv_one = dot(grad_one, weights, 0, 0)
        dk_one = dot(q_one, grad_scores, 0, 0)
        dq.append(dot(grad_scores, k, 1, 0))
        dk = dk_one if dk is None else dk + dk_one
        dv = dv_one if dv is None else dv + dv_one
    dq = (jnp.where(first_lanes, dq[0], dq[1]) * SCALE).astype(bf16)
    return dq, dk.astype(bf16), dv.astype(bf16)


def row_sums(values):
    return dot(jnp.ones((8, values.shape[1]), bf16), values, 1, 1)


def self_forward_kernel(
    length_ref, hidden_ref, gain_ref, shift_ref, proj_ref, bias_ref, out_ref,
    normed_ref, q_ref, k_ref, v_ref, weights_ref, inverse_ref, heads_ref, partial_ref,
):
    unit, _ = norm_unit(hidden_ref[...].astype(f32))
    normed = (unit * gain_ref[0:1, :] + shift_ref[0:1, :]).astype(bf16)
    normed_ref[...] = normed
    normed_ref.send()
    out_ref.fetch(0)
    q_ref[...] = ((dot(normed, proj_ref[0], 1, 0) + bias_ref[0:1]) * SCALE).astype(bf16)
    k_ref[...] = dot(normed, proj_ref[1], 1, 0).astype(bf16)
    v_ref[...] = (dot(normed, proj_ref[2], 1, 0) + bias_ref[1:2]).astype(bf16)
    q_ref.send()
    k_ref.send()
    v_ref.send()
    for pair in range(q_ref.shape[1] // PAIR):
        lanes = lanes_of(pair)
        heads, inverse = pair_forward(
            length_ref[0], True, q_ref[:, lanes], k_ref[:, lanes], v_ref[:, lanes], weights_ref, 2 * pair
        )
        weights_ref.send(pair)
        heads_ref[:, lanes] = heads
        inverse_ref[:, lanes] = inverse
    heads_ref.send()
    inverse_ref.send()
    partial_ref[...] = dot(heads_ref[...], out_ref[0], 1, 0)


def self_forward(text_len, hidden, gain, shift, proj, bias, out_proj):
    rows, width = hidden.shape
    half = proj.shape[2]
    return call(
        self_forward_kernel,
        "self_forward",
        [
            shaped((rows, width), bf16),
            shaped((rows, half), bf16),
            shaped((rows, half), bf16),
            shaped((rows, half), bf16),
            (shaped((half // HEAD_DIM, rows, rows), bf16), half // PAIR),
            shaped((rows, half), f32),
            shaped((rows, half), bf16),
            shaped((rows, width), f32),
        ],
        8 * rows * width * half + 12 * rows * rows * half,
        6,
        (text_len,),
        hidden, gain, shift, (proj, 3), bias, (out_proj, 2),
    )


def cross_own_kernel(
    length_ref, received_ref, partial_ref, hidden_ref, out_bias_ref, gain_ref, shift_ref,
    proj_ref, bias_ref, k_ref, v_ref, out_ref,
    first_ref, normed_ref, q_ref, weights_ref, inverse_ref, heads_ref, term_ref,
):
    first = hidden_ref[...].astype(f32) + (partial_ref[...] + received_ref[...]) + out_bias_ref[0:1, :]
    first_ref[...] = first
    first_ref.send()
    proj_ref.fetch(0)
    bias_ref.fetch()
    k_ref.fetch()
    v_ref.fetch()
    out_ref.fetch(1)
    unit, _ = norm_unit(first)
    normed = (unit * gain_ref[1:2, :] + shift_ref[1:2, :]).astype(bf16)
    normed_ref[...] = normed
    normed_ref.send()
    q_ref[...] = ((dot(normed, proj_ref[0], 1, 0) + bias_ref[0:1]) * SCALE).astype(bf16)
    q_ref.send()
    for pair in range(q_ref.shape[1] // PAIR):
        lanes = lanes_of(pair)
        heads, inverse = pair_forward(
            length_ref[0], False, q_ref[:, lanes], k_ref[:, lanes], v_ref[:, lanes], weights_ref, 2 * pair
        )
        weights_ref.send(pair)
        heads_ref[:, lanes] = heads
        inverse_ref[:, lanes] = inverse
    heads_ref.send()
    inverse_ref.send()
    term_ref[...] = dot(heads_ref[...], out_ref[1], 1, 0)


def cross_own(audio_len, hidden, partial_self, received, out_bias, gain, shift, proj, bias, k, v, out_proj):
    rows, width = hidden.shape
    columns, half = k.shape
    return call(
        cross_own_kernel,
        "cross_own",
        [
            shaped((rows, width), f32),
            shaped((rows, width), bf16),
            shaped((rows, half), bf16),
            (shaped((half // HEAD_DIM, rows, columns), bf16), half // PAIR),
            shaped((rows, half), f32),
            shaped((rows, half), bf16),
            shaped((rows, width), f32),
        ],
        4 * rows * width * half + 12 * rows * columns * half,
        6,
        (audio_len,),
        received, partial_self, hidden, out_bias, gain, shift, (proj, 3), bias, k, v, (out_proj, 2),
    )


def cross_other_kernel(
    length_ref, gathered_ref, normed_ref, frames_ref, bias_ref,
    q_ref, k_ref, v_ref, weights_ref, inverse_ref, heads_ref, term_ref, wq_ref, wk_ref, wv_ref, wo_ref,
):
    width, half = wq_ref.shape
    for i, ref in enumerate((wq_ref, wk_ref, wv_ref)):
        ref[...] = gathered_ref[i * width : (i + 1) * width, :].astype(bf16)
        ref.send()
    for i in range(width // half):
        start = 3 * width + i * half
        wo_ref[:, i * half : (i + 1) * half] = gathered_ref[start : start + half, :].astype(bf16)
    wo_ref.send()
    q_ref[...] = ((dot(normed_ref[...], wq_ref[...], 1, 0) + bias_ref[0:1]) * SCALE).astype(bf16)
    k_ref[...] = dot(frames_ref[...], wk_ref[...], 1, 0).astype(bf16)
    v_ref[...] = (dot(frames_ref[...], wv_ref[...], 1, 0) + bias_ref[1:2]).astype(bf16)
    q_ref.send()
    k_ref.send()
    v_ref.send()
    for pair in range(half // PAIR):
        lanes = lanes_of(pair)
        heads, inverse = pair_forward(
            length_ref[0], False, q_ref[:, lanes], k_ref[:, lanes], v_ref[:, lanes], weights_ref, 2 * pair
        )
        weights_ref.send(pair)
        heads_ref[:, lanes] = heads
        inverse_ref[:, lanes] = inverse
    heads_ref.send()
    inverse_ref.send()
    term_ref[...] = dot(heads_ref[...], wo_ref[...], 1, 0)


def cross_other(audio_len, normed, frames_in, gathered, bias):
    rows, width = normed.shape
    columns = frames_in.shape[0]
    half = gathered.shape[1]
    proj = shaped((width, half), bf16)
    return call(
        cross_other_kernel,
        "cross_other",
        [
            shaped((rows, half), bf16),
            shaped((columns, half), bf16),
            shaped((columns, half), bf16),
            (shaped((half // HEAD_DIM, rows, columns), bf16), half // PAIR),
            shaped((rows, half), f32),
            shaped((rows, half), bf16),
            shaped((rows, width), f32),
            proj,
            proj,
            proj,
            shaped((half, width), bf16),
        ],
        4 * rows * width * half + 4 * columns * width * half + 12 * rows * columns * half,
        4,
        (audio_len,),
        gathered, normed, frames_in, bias,
    )


def error_function(x):
    x = jnp.clip(x, -4.0, 4.0)
    square = x * x
    top = jnp.full_like(x, -2.72614225801306e-10)
    for c in (
        2.77068142495902e-08,
        -2.10102402082508e-06,
        -5.69250639462346e-05,
        -7.34990630326855e-04,
        -2.95459980854025e-03,
        -1.60960333262415e-02,
    ):
        top = top * square + c
    bottom = jnp.full_like(x, -1.45660718464996e-05)
    for c in (-2.13374055278905e-04, -1.68282697438203e-03, -7.37332916720468e-03, -1.42647390514189e-02):
        bottom = bottom * square + c
    return x * top / bottom


def feed_forward_kernel(
    length_ref, weight_ref, own_ref, other_ref, first_ref, out_bias_ref, gain_ref, shift_ref,
    fc1_ref, fc1_bias_ref, cotangent_ref, fc2_ref,
    second_ref, normed_grad_ref, grads_ref, mlp_ref, fc1_bias_grad_ref, fc2_bias_grad_ref,
):
    second = first_ref[...] + (own_ref[...] + other_ref[...]) + out_bias_ref[1:2, :]
    second_ref[...] = second
    second_ref.send()
    for source in (fc1_ref, fc1_bias_ref, cotangent_ref, fc2_ref):
        source.fetch()
    unit, _ = norm_unit(second)
    normed = (unit * gain_ref[2:3, :] + shift_ref[2:3, :]).astype(bf16)
    grad_y = live_gradient(cotangent_ref[...], length_ref[0], weight_ref[0])
    fc2_bias_grad_ref[...] = column_sum(grad_y)
    grad = grad_y.astype(bf16)
    units, width = fc2_ref.shape
    for start in range(0, units, FF_BLOCK):
        here = slice(start, start + FF_BLOCK)
        fc1 = fc1_ref[:, here]
        pre = dot(normed, fc1, 1, 0) + fc1_bias_ref[:, here]
        cdf = 0.5 * (1.0 + error_function(pre * 0.7071067811865476))
        inner = (pre * cdf).astype(bf16)
        slope = cdf + pre * (0.3989422804014327 * jnp.exp(-0.5 * pre * pre))
        fc2 = fc2_ref[here, :]
        grad_pre = (dot(grad, fc2, 1, 1) * slope).astype(bf16)
        fc1_bias_grad_ref[:, here] = column_sum(grad_pre.astype(f32))
        grads_ref[here, :] = dot(inner, grad, 0, 0)
        block = units + (start // width) * width
        grads_ref[block : block + width, start % width : start % width + FF_BLOCK] = dot(normed, grad_pre, 0, 0)
        mlp_term = dot(inner, fc2, 1, 0)
        normed_term = dot(grad_pre, fc1, 1, 1)
        if start == 0:
            mlp_ref[...] = mlp_term
            normed_grad_ref[...] = normed_term
        else:
            mlp_ref[...] += mlp_term
            normed_grad_ref[...] += normed_term
        if (start + FF_BLOCK) % width == 0:
            grads_ref.send(start // width)
            grads_ref.send((units + start) // width)


def feed_forward(text_len, corpus_weight, first, own, other, out_bias, gain, shift, cotangent, fc1, fc1_bias, fc2):
    rows, width = first.shape
    units = fc2.shape[0]
    full = shaped((rows, width), f32)
    return call(
        feed_forward_kernel,
        "feed_forward",
        [
            full,
            full,
            (shaped((2 * units, width), f32), 2 * units // width),
            full,
            shaped((1, units), f32),
            shaped((1, width), f32),
        ],
        12 * rows * width * units,
        6,
        (text_len, corpus_weight),
        own, other, first, out_bias, gain, shift, fc1, fc1_bias, cotangent, fc2,
    )


def projection_grads(core, normed, source, low, dq, dk, dv, heads, theirs_ref, mine_ref):
    part = theirs_ref.shape[1]
    for out_ref, side in ((theirs_ref, 1 - core), (mine_ref, core)):
        here = pl.ds(pl.multiple_of(side * part, PAIR), part)
        piece = source[:, here]
        out_ref[0] = dot(normed[:, here], dq[...], 0, 0)
        out_ref[1] = dot(piece, dk[...], 0, 1)
        out_ref[2] = dot(piece, dv[...], 0, 1)
        out_ref[3] = dot(heads[...], low[:, here], 0, 0)
        out_ref.send()


def cross_own_back_kernel(
    length_ref, weight_ref, core_ref, received_ref, partial_ref, second_ref, cotangent_ref, gain_ref,
    out_ref, q_ref, k_ref, v_ref, inverse_ref, heads_ref, weights_ref, proj_ref, normed_ref, frames_ref,
    grad_second_ref, low_ref, gain_grad_ref, shift_grad_ref, bias_grad_ref,
    dq_ref, dk_ref, dv_ref, term_ref, dq_sum_ref, dv_sum_ref, theirs_ref, mine_ref,
):
    incoming = partial_ref[...] + received_ref[...]
    unit, inverse = norm_unit(second_ref[...])
    gain_grad_ref[...] = column_sum(incoming * unit)
    shift_grad_ref[...] = column_sum(incoming)
    grad_second = live_gradient(cotangent_ref[...], length_ref[0], weight_ref[0]) + norm_backward(
        incoming, unit, inverse, gain_ref[2:3, :]
    )
    grad_second_ref[...] = grad_second
    out_ref.fetch(1)
    for source in (q_ref, k_ref, v_ref, inverse_ref, heads_ref, weights_ref):
        source.fetch()
    proj_ref.fetch(0)
    normed_ref.fetch()
    frames_ref.fetch()
    grad_second_ref.send()
    low = grad_second.astype(bf16)
    low_ref[...] = low
    low_ref.send()
    bias_grad_ref[...] = column_sum(grad_second)
    grad_heads = dot(low, out_ref[1], 1, 1).astype(bf16)
    for pair in range(q_ref.shape[1] // PAIR):
        lanes = lanes_of(pair)
        dq, dk, dv = pair_backward(
            q_ref[:, lanes], k_ref[:, lanes], v_ref[:, lanes], weights_ref, 2 * pair,
            inverse_ref[:, lanes], heads_ref[:, lanes], grad_heads[:, lanes],
        )
        dq_ref[:, lanes] = dq
        dk_ref[lanes, :] = dk
        dv_ref[lanes, :] = dv
    dk_ref.send()
    dv_ref.send()
    projection_grads(
        core_ref[0], normed_ref, frames_ref, low_ref, dq_ref, dk_ref, dv_ref, heads_ref, theirs_ref, mine_ref
    )
    term_ref[...] = dot(dq_ref[...], proj_ref[0], 1, 1)
    dq_sum_ref[...] = column_sum(dq_ref[...].astype(f32))
    dv_sum_ref[...] = row_sums(dv_ref[...])


def cross_own_back(
    text_len, corpus_weight, core, cotangent, second, partial_normed, received, gain, out_proj, proj,
    q, k, v, weights, inverse, heads, normed, frames_in,
):
    rows, width = second.shape
    columns, half = k.shape
    vector = shaped((1, width), f32)
    grads = shaped((4, width // 2, half), f32)
    return call(
        cross_own_back_kernel,
        "cross_own_back",
        [
            shaped((rows, width), f32),
            shaped((rows, width), bf16),
            vector,
            vector,
            vector,
            shaped((rows, half), bf16),
            shaped((half, columns), bf16),
            shaped((half, columns), bf16),
            shaped((rows, width), f32),
            shaped((1, half), f32),
            shaped((8, half), f32),
            grads,
            grads,
        ],
        8 * rows * width * half + 4 * columns * width * half + 24 * rows * columns * half,
        5,
        (text_len, corpus_weight, core),
        received, partial_normed, second, cotangent, gain, (out_proj, 2), q, k, v, inverse, heads,
        (weights, half // PAIR), (proj, 3), normed, frames_in,
    )


def other_back_kernel(
    core_ref, low_in_ref, wo_ref, q_ref, k_ref, v_ref, inverse_ref, heads_ref, weights_ref, wq_ref,
    own_term_ref, first_ref, grad_second_ref, gain_ref,
    out_ref, self_q_ref, self_k_ref, self_v_ref, self_inverse_ref, self_heads_ref, self_weights_ref,
    proj_ref, hidden_ref, normed_ref,
    dk_ref, dv_ref, grad_first_ref, gain_grad_ref, shift_grad_ref, bias_grad_ref,
    term_ref, theirs_ref, mine_ref, self_gain_grad_ref, self_shift_grad_ref, dq_sum_ref, dv_sum_ref,
    low_ref, self_dq_ref, self_dk_ref, self_dv_ref,
):
    grad_heads = dot(low_in_ref[...], wo_ref[...], 1, 1).astype(bf16)
    for source in (wq_ref, own_term_ref, first_ref, grad_second_ref, gain_ref):
        source.fetch()
    out_ref.fetch(0)
    for source in (
        self_q_ref, self_k_ref, self_v_ref, self_inverse_ref, self_heads_ref, self_weights_ref, proj_ref,
        hidden_ref, normed_ref,
    ):
        source.fetch()
    pairs = q_ref.shape[1] // PAIR
    dqs = []
    for pair in range(pairs):
        lanes = lanes_of(pair)
        dq, dk, dv = pair_backward(
            q_ref[:, lanes], k_ref[:, lanes], v_ref[:, lanes], weights_ref, 2 * pair,
            inverse_ref[:, lanes], heads_ref[:, lanes], grad_heads[:, lanes],
        )
        dqs.append(dq)
        dk_ref[lanes, :] = dk
        dv_ref[lanes, :] = dv
    dk_ref.send()
    dv_ref.send()
    incoming = own_term_ref[...] + dot(jnp.concatenate(dqs, axis=1), wq_ref[...], 1, 1)
    unit, inverse = norm_unit(first_ref[...])
    gain_grad_ref[...] = column_sum(incoming * unit)
    shift_grad_ref[...] = column_sum(incoming)
    grad_first = grad_second_ref[...] + norm_backward(incoming, unit, inverse, gain_ref[1:2, :])
    grad_first_ref[...] = grad_first
    grad_first_ref.send()
    low = grad_first.astype(bf16)
    low_ref[...] = low
    bias_grad_ref[...] = column_sum(grad_first)

    grad_heads = dot(low, out_ref[0], 1, 1).astype(bf16)
    for pair in range(pairs):
        lanes = lanes_of(pair)
        dq, dk, dv = pair_backward(
            self_q_ref[:, lanes], self_k_ref[:, lanes], self_v_ref[:, lanes], self_weights_ref, 2 * pair,
            self_inverse_ref[:, lanes], self_heads_ref[:, lanes], grad_heads[:, lanes],
        )
        self_dq_ref[:, lanes] = dq
        self_dk_ref[lanes, :] = dk
        self_dv_ref[lanes, :] = dv
    projection_grads(
        core_ref[0], normed_ref, normed_ref, low_ref, self_dq_ref, self_dk_ref, self_dv_ref, self_heads_ref,
        theirs_ref, mine_ref,
    )
    incoming = dot(self_dq_ref[...], proj_ref[0], 1, 1) + (
        dot(self_dk_ref[...], proj_ref[1], 0, 1) + dot(self_dv_ref[...], proj_ref[2], 0, 1)
    )
    term_ref[...] = incoming
    term_ref.send()
    unit, _ = norm_unit(hidden_ref[...].astype(f32))
    self_gain_grad_ref[...] = column_sum(incoming * unit)
    self_shift_grad_ref[...] = column_sum(incoming)
    dq_sum_ref[...] = column_sum(self_dq_ref[...].astype(f32))
    dv_sum_ref[...] = row_sums(self_dv_ref[...])


def other_back(
    core, low, wo, wq, q, k, v, weights, inverse, heads, own_term, first, grad_second, gain,
    out_proj, proj, self_q, self_k, self_v, self_weights, self_inverse, self_heads, hidden, normed,
):
    rows, width = first.shape
    columns, half = k.shape
    vector = shaped((1, width), f32)
    grads = shaped((4, width // 2, half), f32)
    return call(
        other_back_kernel,
        "other_back",
        [
            shaped((half, columns), bf16),
            shaped((half, columns), bf16),
            shaped((rows, width), f32),
            vector,
            vector,
            vector,
            shaped((rows, width), f32),
            grads,
            grads,
            vector,
            vector,
            shaped((1, half), f32),
            shaped((8, half), f32),
            shaped((rows, width), bf16),
            shaped((rows, half), bf16),
            shaped((half, rows), bf16),
            shaped((half, rows), bf16),
        ],
        20 * rows * width * half + 24 * rows * (columns + rows) * half,
        8,
        (core,),
        low, wo, q, k, v, inverse, heads, (weights, half // PAIR), wq, own_term, first, grad_second, gain,
        (out_proj, 2), self_q, self_k, self_v, self_inverse, self_heads, (self_weights, half // PAIR),
        (proj, 3), hidden, normed,
    )


def encoder_grad_kernel(dk0_ref, dv0_ref, dk1_ref, dv1_ref, proj_ref, wk1_ref, wv1_ref, out_ref):
    own = dot(dk0_ref[...], proj_ref[1], 0, 1) + dot(dv0_ref[...], proj_ref[2], 0, 1)
    other = dot(dk1_ref[...], wk1_ref[...], 0, 1) + dot(dv1_ref[...], wv1_ref[...], 0, 1)
    out_ref[:, 0, :] = own + other


def encoder_grad(dk0, dv0, dk1, dv1, proj, wk1, wv1, frames):
    half, padded = dk0.shape
    width = wk1.shape[0]
    grad_block = pl.BlockSpec((half, FRAME_BLOCK), lambda i: (0, i))
    weight = pl.BlockSpec(wk1.shape, lambda i: (0, 0))
    return pl.pallas_call(
        encoder_grad_kernel,
        grid=(padded // FRAME_BLOCK,),
        in_specs=[grad_block] * 4 + [pl.BlockSpec(proj.shape, lambda i: (0, 0, 0)), weight, weight],
        out_specs=pl.BlockSpec((FRAME_BLOCK, 1, width), lambda i: (i, 0, 0)),
        out_shape=shaped((frames, 1, width), f32),
        compiler_params=pltpu.CompilerParams(vmem_limit_bytes=VMEM_LIMIT),
        cost_estimate=pl.CostEstimate(
            flops=8 * half * padded * width, bytes_accessed=6 * frames * width, transcendentals=0
        ),
        name="encoder_grad",
    )(dk0, dv0, dk1, dv1, proj, wk1, wv1)


def swap(value):
    return lax.ppermute(value, "tensor", [(0, 1), (1, 0)])


def tie(*values):
    return lax.optimization_barrier(values)


class Scatter:
    def __init__(self, theirs, mine):
        self.members = lax.axis_size("dp")
        self.bits = self.members.bit_length() - 1
        self.bit = 0
        self.theirs, self.mine = theirs, mine

    def launch(self):
        if self.bit == self.bits:
            return
        other = 1 << self.bit
        self.received = lax.ppermute(self.theirs, "dp", [(i, i ^ other) for i in range(self.members)])

    def land(self):
        if self.bit == self.bits:
            return
        total = self.mine + self.received
        if self.bit == 0:
            lead = total.shape[:-2]
            self.lead = len(lead)
            cuts = self.bits - 1
            total = total.reshape(lead + (2,) * cuts + (total.shape[-2] >> cuts, total.shape[-1]))
        self.bit += 1
        if self.bit < self.bits:
            axis = self.lead + self.bits - 1 - self.bit
            side = (lax.axis_index("dp") >> self.bit) & 1
            self.mine = lax.dynamic_index_in_dim(total, side, axis, keepdims=True)
            self.theirs = lax.dynamic_index_in_dim(total, 1 - side, axis, keepdims=True)
        else:
            self.part = total.reshape(total.shape[: self.lead] + total.shape[-2:])

    def finish(self):
        self.land()
        while self.bit < self.bits:
            self.launch()
            self.land()
        return self.part


def place_kernel(moves, gathered_ref, *refs):
    outs, (held, in_sems, out_sems) = refs[:-3], refs[-3:]
    reads = [
        pltpu.make_async_copy(gathered_ref.at[i], held.at[i], in_sems.at[i]) for i in range(held.shape[0])
    ]
    for read in reads:
        read.start()
    writes = []
    for i, read in enumerate(reads):
        read.wait()
        for start, count, out, target in moves[i]:
            writes.append(
                pltpu.make_async_copy(
                    held.at[i, pl.ds(start, count)], outs[out].at[target], out_sems.at[len(writes)]
                )
            )
            writes[-1].start()
    for write in writes:
        write.wait()


def place(gathered, width, units):
    members, total, half = gathered.shape
    parts = members // 2
    rows = 2 * units // members
    count = width // members
    proj = shaped((3, width, half), f32)
    outs = [shaped((units, width), f32), shaped((width, units), f32), proj, proj, shaped((2, half, width), f32)]
    if count % 8 == 0 and width % rows == 0:
        moves = []
        for i in range(members):
            q, c = i // 2, i % 2
            moves.append([])
            for j in range(2):
                row = i * rows
                if row < units:
                    target = (0, (pl.ds(row, rows), pl.ds(j * half, half)))
                else:
                    block, row = divmod(row - units, width)
                    target = (1, (pl.ds(row, rows), pl.ds(block * width + j * half, half)))
                moves[i].append((j * rows, rows) + target)
            here = pl.ds(c * (width // 2) + q * count, count)
            for branch in range(2):
                start = 2 * rows + branch * 4 * count
                for a in range(3):
                    moves[i].append((start + a * count, count, 2 + branch, (a, here)))
                target = (1 - branch, pl.ds(q * count, count), pl.ds(c * half, half))
                moves[i].append((start + 3 * count, count, 4, target))
        anywhere = pl.BlockSpec(memory_space=pl.ANY)
        return pl.pallas_call(
            partial(place_kernel, moves),
            in_specs=[anywhere],
            out_specs=[anywhere] * len(outs),
            out_shape=outs,
            scratch_shapes=[
                pltpu.VMEM(gathered.shape, f32),
                pltpu.SemaphoreType.DMA((members,)),
                pltpu.SemaphoreType.DMA((sum(len(m) for m in moves),)),
            ],
            compiler_params=pltpu.CompilerParams(vmem_limit_bytes=VMEM_LIMIT),
            cost_estimate=pl.CostEstimate(flops=0, bytes_accessed=8 * gathered.size, transcendentals=0),
            name="place",
        )(gathered)
    stacked = gathered[:, : 2 * rows].reshape(members, 2, rows, half).swapaxes(1, 2).reshape(-1, width)
    fc1 = from_column_blocks(stacked[units:], units // width)
    split = gathered[:, 2 * rows :].reshape(parts, 2, 2, 4, count, half)
    projections = split[:, :, :, :3].transpose(2, 3, 1, 0, 4, 5).reshape(2, 3, width, half)
    outputs = split[:, :, ::-1, 3].transpose(2, 0, 3, 1, 4).reshape(2, half, width)
    return stacked[:units], fc1, projections[0], projections[1], outputs


def from_column_blocks(value, blocks):
    rows = value.shape[0] // blocks
    return jnp.concatenate([value[i * rows : (i + 1) * rows] for i in range(blocks)], axis=1)


def per_device(
    hidden,
    encoder,
    text_len,
    audio_len,
    corpus_weight,
    cotangent,
    norm_gain,
    norm_bias,
    self_proj,
    self_bias,
    cross_proj,
    cross_bias,
    out_proj,
    out_bias,
    fc1_weight,
    fc1_bias,
    fc2_weight,
    fc2_bias,
):
    sequences, frames, width = encoder.shape
    members = lax.axis_size("dp")
    me = lax.axis_index("dp")
    half = self_proj.shape[2]
    padded = -(-frames // FRAME_BLOCK) * FRAME_BLOCK
    core = (me & 1).astype(jnp.int32).reshape(1)

    cross_rows = jnp.concatenate(
        [cross_proj.reshape(-1, half), out_proj[1][:, :half], out_proj[1][:, half:]], axis=0
    )
    count = cross_rows.shape[0] // members
    part = lax.dynamic_slice_in_dim(cross_rows, me * count, count, 0).astype(f32)
    part = swap(jnp.concatenate([part, cross_bias], axis=0))

    normed_self, q_self, k_self, v_self, weights_self, inverse_self, heads_self, partial_self = self_forward(
        text_len, hidden, norm_gain, norm_bias, self_proj, self_bias, out_proj
    )
    part, partial_self = tie(part, partial_self)
    other_bias = part[count:]
    gathered = lax.all_gather(part[:count], "dp", axis=0, tiled=True)
    received = swap(partial_self)

    frames_in = jnp.pad(encoder.reshape(frames, width), ((0, padded - frames), (0, 0)))
    k_own = dot(frames_in, cross_proj[1], 1, 0).astype(bf16)
    v_own = (dot(frames_in, cross_proj[2], 1, 0) + cross_bias[1]).astype(bf16)
    received, k_own, v_own = tie(received, k_own, v_own)
    first, normed_cross, q_own, weights_own, inverse_own, heads_own, term_own = cross_own(
        audio_len, hidden, partial_self, received, out_bias, norm_gain, norm_bias,
        cross_proj, cross_bias, k_own, v_own, out_proj,
    )
    gathered, normed_cross = tie(gathered, normed_cross)
    (
        q_other, k_other, v_other, weights_other, inverse_other, heads_other, term_other,
        wq_other, wk_other, wv_other, wo_other,
    ) = cross_other(audio_len, normed_cross, frames_in, gathered, other_bias)

    second, partial_normed, mlp_grads, partial_mlp, fc1_bias_grad, fc2_bias_grad = feed_forward(
        text_len, corpus_weight, first, term_own, term_other, out_bias, norm_gain, norm_bias, cotangent,
        fc1_weight, fc1_bias.reshape(1, -1), fc2_weight,
    )
    received = swap(partial_normed)
    mlp_part = lax.psum_scatter(mlp_grads, "dp", scatter_dimension=0, tiled=True)

    (
        grad_second, second_low, gain_mlp, shift_mlp, bias_cross, dq_own, dk_own, dv_own, back_own,
        dq_cross_sum, dv_cross_sum, cross_theirs, cross_mine,
    ) = cross_own_back(
        text_len, corpus_weight, core, cotangent, second, partial_normed, received, norm_gain,
        out_proj, cross_proj, q_own, k_own, v_own, weights_own, inverse_own, heads_own, normed_cross, frames_in,
    )
    cross_share = Scatter(cross_theirs, cross_mine)
    cross_share.launch()
    cross_share.land()
    second_low, cross_share.theirs = tie(second_low, cross_share.theirs)
    cross_share.launch()

    (
        dk_other, dv_other, grad_first, gain_cross, shift_cross, bias_self, partial_normed,
        self_theirs, self_mine, gain_self, shift_self, dq_self_sum, dv_self_sum, *_,
    ) = other_back(
        core, second_low, wo_other, wq_other, q_other, k_other, v_other, weights_other, inverse_other, heads_other,
        back_own, first, grad_second, norm_gain, out_proj, self_proj, q_self, k_self, v_self, weights_self,
        inverse_self, heads_self, hidden, normed_self,
    )
    self_share = Scatter(self_theirs, self_mine)
    self_share.launch()
    norm_self = jnp.concatenate([gain_self, shift_self], axis=0)
    norm_received = swap(norm_self)
    norm_self, partial_normed = tie(norm_self, partial_normed)
    received = swap(partial_normed)
    self_share.land()
    cross_share.received, self_share.theirs = tie(cross_share.received, self_share.theirs)
    self_share.launch()
    cross_share.land()
    cross_share.launch()
    dk_own, cross_share.theirs = tie(dk_own, cross_share.theirs)
    grad_encoder = encoder_grad(
        dk_own, dv_own, dk_other, dv_other, cross_proj, wk_other, wv_other, frames
    ).reshape(encoder.shape)
    cross_share.received, grad_encoder = tie(cross_share.received, grad_encoder)
    cross_share.land()
    cross_share.launch()
    partial_mlp, cross_share.theirs, received = tie(partial_mlp, cross_share.theirs, received)
    received_mlp = swap(partial_mlp)

    small = (
        norm_self + norm_received,
        gain_cross,
        gain_mlp,
        shift_cross,
        shift_mlp,
        dq_self_sum,
        dv_self_sum[0:1],
        dq_cross_sum,
        dv_cross_sum[0:1],
        bias_self,
        bias_cross,
        fc1_bias_grad,
        fc2_bias_grad,
    )
    flat = jnp.concatenate([item.reshape(-1, half) for item in small], axis=0)

    unit_self, root_self = norm_unit(hidden.astype(f32))
    grad_hidden = (
        grad_first + norm_backward(partial_normed + received, unit_self, root_self, norm_gain[0])
    ).astype(bf16)
    grad_hidden, flat, self_share.received = tie(grad_hidden, flat, self_share.received)
    self_share.land()
    self_share.launch()
    cross_part = cross_share.finish()
    self_part = self_share.finish()
    rows = mlp_part.shape[0]
    every = jnp.concatenate(
        [mlp_part[:, :half], mlp_part[:, half:], cross_part.reshape(-1, half), self_part.reshape(-1, half)], axis=0
    )
    flat, every = tie(flat, every)
    every = lax.all_gather(every, "dp", axis=0, tiled=False)
    for bit in range(members.bit_length() - 1):
        flat = flat + lax.ppermute(flat, "dp", [(i, i ^ (1 << bit)) for i in range(members)])
    result = (second + (partial_mlp + received_mlp) + fc2_bias).astype(bf16)
    fc2_weight_grad, fc1_weight_grad, cross_proj_grad, self_proj_grad, out_proj_grad = place(
        every, width, fc2_weight.shape[0]
    )
    small_out = []
    offset = 0
    for item in small:
        count = item.size // half
        small_out.append(flat[offset : offset + count].reshape(item.shape))
        offset += count
    (
        norm_self, gain_cross, gain_mlp, shift_cross, shift_mlp, dq_self_sum, dv_self_sum, dq_cross_sum,
        dv_cross_sum, bias_self, bias_cross, fc1_bias_grad, fc2_bias_grad,
    ) = small_out
    return (
        result,
        grad_hidden,
        grad_encoder,
        jnp.concatenate([norm_self[0:1], gain_cross, gain_mlp], axis=0),
        jnp.concatenate([norm_self[1:2], shift_cross, shift_mlp], axis=0),
        self_proj_grad,
        jnp.concatenate([dq_self_sum, dv_self_sum], axis=0),
        cross_proj_grad,
        jnp.concatenate([dq_cross_sum, dv_cross_sum], axis=0),
        out_proj_grad,
        jnp.concatenate([bias_self, bias_cross], axis=0),
        fc1_weight_grad,
        fc1_bias_grad.reshape(-1),
        fc2_weight_grad,
        fc2_bias_grad.reshape(-1),
    )


def solution(mesh):
    placed = (
        P("dp", None),
        P("dp", None, None),
        P("dp"),
        P("dp"),
        P("dp"),
        P("dp", None),
        P(),
        P(),
        P(None, None, "tensor"),
        P(None, "tensor"),
        P(None, None, "tensor"),
        P(None, "tensor"),
        P(None, "tensor", None),
        P(),
        P(None, "tensor"),
        P("tensor"),
        P("tensor", None),
        P(),
    )
    return jax.shard_map(
        per_device,
        mesh=mesh,
        in_specs=placed,
        out_specs=(
            P("dp", None),
            P("dp", None),
            P("dp", None, None),
            P(),
            P(),
            P(None, None, "tensor"),
            P(None, "tensor"),
            P(None, None, "tensor"),
            P(None, "tensor"),
            P(None, "tensor", None),
            P(),
            P(None, "tensor"),
            P("tensor"),
            P("tensor", None),
            P(),
        ),
        check_vma=False,
    )
```

```python
from functools import partial

import jax
import jax.numpy as jnp
from jax import lax
from jax.experimental import pallas as pl
from jax.experimental.pallas import tpu as pltpu
from jax.sharding import PartitionSpec as P

HEAD_DIM = 64
SCALE = HEAD_DIM ** (-0.5)
PAIR = 2 * HEAD_DIM
FF_BLOCK = 256
FRAME_BLOCK = 256
VMEM_LIMIT = 58 * 1024 * 1024
COST_SHARE = 64
epsilon = 1e-05
masked_value = -1e30
f32 = jnp.float32
bf16 = jnp.bfloat16


def dot(a, b, ca, cb):
    return lax.dot_general(a, b, (((ca,), (cb,)), ((), ())), preferred_element_type=f32)


def shaped(shape, dtype):
    return jax.ShapeDtypeStruct(shape, dtype)


class Source:
    def __init__(self, ref, held, sems, first_sem, pieces):
        self.held, self.shape, self.dtype = held, held.shape, held.dtype
        self.size = held.shape[0] // pieces
        self.ref, self.sems, self.first_sem = ref, sems, first_sem
        self.copies = [None] * pieces
        self.pending = [True] * pieces

    def fetch(self, *pieces):
        for piece in pieces or range(len(self.copies)):
            if self.copies[piece] is None:
                here = pl.ds(piece * self.size, self.size)
                self.copies[piece] = pltpu.make_async_copy(
                    self.ref.at[here], self.held.at[here], self.sems.at[self.first_sem + piece]
                )
                self.copies[piece].start()

    def wait(self, piece):
        if self.pending[piece]:
            self.fetch(piece)
            self.pending[piece] = False
            self.copies[piece].wait()

    def __getitem__(self, index):
        if len(self.copies) > 1 and isinstance(index, int):
            self.wait(index // self.size)
        else:
            for piece in range(len(self.copies)):
                self.wait(piece)
        return self.held[index]


class Sink:
    def __init__(self, ref, held, sems, first_sem, pieces):
        self.held, self.shape, self.dtype = held, held.shape, held.dtype
        self.size = held.shape[0] // pieces
        self.copies = []
        self.sent = []
        for i in range(pieces):
            here = pl.ds(i * self.size, self.size)
            self.copies.append(pltpu.make_async_copy(held.at[here], ref.at[here], sems.at[first_sem + i]))
            self.sent.append(False)

    def __getitem__(self, index):
        return self.held[index]

    def __setitem__(self, index, value):
        self.held[index] = value

    def send(self, piece=0):
        self.sent[piece] = True
        self.copies[piece].start()


class Resident:
    def __init__(self, value):
        self.value = value

    def __getitem__(self, index):
        return self.value[index]

    def __setitem__(self, index, value):
        self.value[index] = value


def call(kernel, name, out_shape, flops, scalars, *arrays):
    arrays = [a if isinstance(a, tuple) else (a, 1) for a in arrays]
    used = [a[2:] for a in arrays]
    arrays = [a[:2] for a in arrays]
    outs = [o if isinstance(o, tuple) else (o, 1) for o in out_shape]
    in_stays = [isinstance(a, Resident) for a, _ in arrays]
    out_stays = [isinstance(o, Resident) for o, _ in outs]
    in_pieces = [0 if stays else pieces for (_, pieces), stays in zip(arrays, in_stays)]
    out_pieces = [0 if stays else pieces for (_, pieces), stays in zip(outs, out_stays)]
    arrays = [a.value if stays else a for (a, _), stays in zip(arrays, in_stays)]
    outs = [o.value if stays else o for (o, _), stays in zip(outs, out_stays)]
    moved = sum(a.size * a.dtype.itemsize for a in (*arrays, *outs))

    def body(*refs):
        refs = list(refs)
        scalar_refs = [refs.pop(0) for _ in scalars]
        in_refs = [refs.pop(0) for _ in arrays]
        out_refs = [refs.pop(0) for _ in outs]
        in_held = [None if stays else refs.pop(0) for stays in in_stays]
        out_held = [None if stays else refs.pop(0) for stays in out_stays]
        in_sems, out_sems = refs
        sources = []
        for i, (ref, held) in enumerate(zip(in_refs, in_held)):
            if in_stays[i]:
                sources.append(Resident(ref))
            else:
                sources.append(Source(ref, held, in_sems, sum(in_pieces[:i]), in_pieces[i]))
        sinks = []
        for i, (ref, held) in enumerate(zip(out_refs, out_held)):
            if out_stays[i]:
                sinks.append(Resident(ref))
            else:
                sinks.append(Sink(ref, held, out_sems, sum(out_pieces[:i]), out_pieces[i]))
        moving = [source for source in sources if isinstance(source, Source)]
        leaving = [sink for sink in sinks if isinstance(sink, Sink)]
        for source, only in zip(sources, used):
            if isinstance(source, Source):
                source.fetch(*only)
        kernel(*scalar_refs, *sources, *sinks)
        for source in moving:
            for piece in range(len(source.copies)):
                if source.copies[piece] is not None:
                    source.wait(piece)
        for sink in leaving:
            for piece, sent in enumerate(sink.sent):
                if not sent:
                    sink.send(piece)
        for sink in leaving:
            for copy in sink.copies:
                copy.wait()

    anywhere = pl.BlockSpec(memory_space=pl.ANY)
    here = pl.BlockSpec(memory_space=pltpu.VMEM)
    scratch = [pltpu.VMEM(a.shape, a.dtype) for a, stays in zip(arrays, in_stays) if not stays]
    scratch += [pltpu.VMEM(o.shape, o.dtype) for o, stays in zip(outs, out_stays) if not stays]
    return pl.pallas_call(
        body,
        in_specs=[pl.BlockSpec(memory_space=pltpu.SMEM)] * len(scalars)
        + [here if stays else anywhere for stays in in_stays],
        out_specs=[here if stays else anywhere for stays in out_stays],
        out_shape=outs,
        scratch_shapes=scratch
        + [pltpu.SemaphoreType.DMA((sum(in_pieces),)), pltpu.SemaphoreType.DMA((sum(out_pieces),))],
        compiler_params=pltpu.CompilerParams(vmem_limit_bytes=VMEM_LIMIT),
        cost_estimate=pl.CostEstimate(
            flops=flops // COST_SHARE, bytes_accessed=moved // COST_SHARE, transcendentals=0
        ),
        name=name,
    )(*scalars, *arrays)


def lanes_of(pair):
    return slice(pair * PAIR, (pair + 1) * PAIR)


def add_up(terms):
    total = terms[0]
    for term in terms[1:]:
        total = total + term
    return total


def norm_unit(values):
    centered = values - jnp.mean(values, axis=-1, keepdims=True)
    inverse = lax.rsqrt(jnp.mean(centered * centered, axis=-1, keepdims=True) + epsilon)
    return centered * inverse, inverse


def norm_backward(incoming, unit, inverse, gain):
    scaled = incoming * gain
    scaled_mean = jnp.mean(scaled, axis=-1, keepdims=True)
    along_unit = jnp.mean(scaled * unit, axis=-1, keepdims=True)
    return inverse * (scaled - scaled_mean - unit * along_unit)


def column_sum(values):
    return jnp.sum(values, axis=0, keepdims=True)


def live_gradient(cotangent, text_len, corpus_weight):
    places = lax.broadcasted_iota(jnp.int32, (cotangent.shape[0], 1), 0)
    live = jnp.where(places < text_len, corpus_weight, 0.0)
    return cotangent.astype(f32) * live


def lane_masks(rows):
    return lax.broadcasted_iota(jnp.int32, (rows, PAIR), 1) < HEAD_DIM


def pair_forward(length, causal, q, k, v, weights_ref, start):
    rows, columns = q.shape[0], k.shape[0]
    first_lanes = lane_masks(rows)
    if causal:
        places = lax.broadcasted_iota(jnp.int32, (rows, columns), 1)
        allowed = (places < length) & (places <= lax.broadcasted_iota(jnp.int32, (rows, columns), 0))
    else:
        places = lax.broadcasted_iota(jnp.int32, (1, columns), 1)
        shift = jnp.where(places < length, 0.0, masked_value)
    scores = []
    for head in range(2):
        mine = first_lanes if head == 0 else jnp.logical_not(first_lanes)
        raw = dot(jnp.where(mine, q, jnp.zeros_like(q)), k, 1, 1)
        scores.append(jnp.where(allowed, raw, masked_value) if causal else raw + shift)
    inverses = []
    for head in range(2):
        largest = jnp.max(scores[head], axis=-1, keepdims=True)
        weights = jnp.exp(scores[head] - largest)
        inverses.append(1.0 / jnp.sum(weights, axis=-1, keepdims=True))
        weights_ref[start + head] = weights.astype(bf16)
    mixed = [dot(weights_ref[start + head], v, 1, 0) for head in range(2)]
    inverse = jnp.where(first_lanes, inverses[0], inverses[1])
    return (jnp.where(first_lanes, mixed[0], mixed[1]) * inverse).astype(bf16), inverse


def pair_backward(q, k, v, weights_ref, start, inverse, heads, grad_heads):
    first_lanes = lane_masks(q.shape[0])
    grad = (grad_heads.astype(f32) * inverse).astype(bf16)
    along = grad.astype(f32) * heads.astype(f32)
    dq = []
    dk = None
    dv = None
    for head in range(2):
        mine = first_lanes if head == 0 else jnp.logical_not(first_lanes)
        grad_one = jnp.where(mine, grad, jnp.zeros_like(grad))
        q_one = jnp.where(mine, q, jnp.zeros_like(q))
        row_terms = jnp.sum(jnp.where(mine, along, 0.0), axis=-1, keepdims=True)
        weights = weights_ref[start + head]
        grad_probs = dot(grad_one, v, 1, 1)
        grad_scores = (weights.astype(f32) * (grad_probs - row_terms)).astype(bf16)
        dv_one = dot(grad_one, weights, 0, 0)
        dk_one = dot(q_one, grad_scores, 0, 0)
        dq.append(dot(grad_scores, k, 1, 0))
        dk = dk_one if dk is None else dk + dk_one
        dv = dv_one if dv is None else dv + dv_one
    dq = (jnp.where(first_lanes, dq[0], dq[1]) * SCALE).astype(bf16)
    return dq, dk.astype(bf16), dv.astype(bf16)


def row_sums(values):
    return dot(jnp.ones((8, values.shape[1]), bf16), values, 1, 1)


def self_forward_kernel(
    length_ref, hidden_ref, gain_ref, shift_ref, proj_ref, bias_ref, out_ref,
    normed_ref, q_ref, k_ref, v_ref, weights_ref, inverse_ref, heads_ref, partial_ref,
):
    unit, _ = norm_unit(hidden_ref[...].astype(f32))
    normed = (unit * gain_ref[0:1, :] + shift_ref[0:1, :]).astype(bf16)
    normed_ref[...] = normed
    normed_ref.send()
    q_ref[...] = ((dot(normed, proj_ref[0], 1, 0) + bias_ref[0:1]) * SCALE).astype(bf16)
    k_ref[...] = dot(normed, proj_ref[1], 1, 0).astype(bf16)
    v_ref[...] = (dot(normed, proj_ref[2], 1, 0) + bias_ref[1:2]).astype(bf16)
    q_ref.send()
    k_ref.send()
    v_ref.send()
    for pair in range(q_ref.shape[1] // PAIR):
        lanes = lanes_of(pair)
        heads, inverse = pair_forward(
            length_ref[0], True, q_ref[:, lanes], k_ref[:, lanes], v_ref[:, lanes], weights_ref, 2 * pair
        )
        weights_ref.send(pair)
        heads_ref[:, lanes] = heads
        inverse_ref[:, lanes] = inverse
    heads_ref.send()
    inverse_ref.send()
    partial_ref[...] = dot(heads_ref[...], out_ref[0], 1, 0)


def self_forward(text_len, hidden, gain, shift, proj, bias, out_proj):
    rows, width = hidden.shape
    half = proj.shape[2]
    return call(
        self_forward_kernel,
        "self_forward",
        [
            shaped((rows, width), bf16),
            shaped((rows, half), bf16),
            shaped((rows, half), bf16),
            shaped((rows, half), bf16),
            (shaped((half // HEAD_DIM, rows, rows), bf16), half // PAIR),
            shaped((rows, half), f32),
            shaped((rows, half), bf16),
            Resident(shaped((rows, width), f32)),
        ],
        8 * rows * width * half + 12 * rows * rows * half,
        (text_len,),
        hidden, gain, shift, (proj, 3), bias, (out_proj, 2, 0),
    )


def cross_own_kernel(
    length_ref, received_ref, partial_ref, hidden_ref, out_bias_ref, gain_ref, shift_ref,
    proj_ref, bias_ref, k_ref, v_ref, out_ref,
    first_ref, normed_ref, q_ref, weights_ref, inverse_ref, heads_ref, term_ref,
):
    first = hidden_ref[...].astype(f32) + (partial_ref[...] + received_ref[...]) + out_bias_ref[0:1, :]
    first_ref[...] = first
    first_ref.send()
    unit, _ = norm_unit(first)
    normed = (unit * gain_ref[1:2, :] + shift_ref[1:2, :]).astype(bf16)
    normed_ref[...] = normed
    normed_ref.send()
    q_ref[...] = ((dot(normed, proj_ref[0], 1, 0) + bias_ref[0:1]) * SCALE).astype(bf16)
    q_ref.send()
    for pair in range(q_ref.shape[1] // PAIR):
        lanes = lanes_of(pair)
        heads, inverse = pair_forward(
            length_ref[0], False, q_ref[:, lanes], k_ref[:, lanes], v_ref[:, lanes], weights_ref, 2 * pair
        )
        weights_ref.send(pair)
        heads_ref[:, lanes] = heads
        inverse_ref[:, lanes] = inverse
    heads_ref.send()
    inverse_ref.send()
    term_ref[...] = dot(heads_ref[...], out_ref[1], 1, 0)


def cross_own(audio_len, hidden, partial_self, received, out_bias, gain, shift, proj, bias, k, v, out_proj):
    rows, width = hidden.shape
    columns, half = k.shape
    return call(
        cross_own_kernel,
        "cross_own",
        [
            shaped((rows, width), f32),
            shaped((rows, width), bf16),
            shaped((rows, half), bf16),
            (shaped((half // HEAD_DIM, rows, columns), bf16), half // PAIR),
            shaped((rows, half), f32),
            shaped((rows, half), bf16),
            shaped((rows, width), f32),
        ],
        4 * rows * width * half + 12 * rows * columns * half,
        (audio_len,),
        Resident(received), Resident(partial_self), hidden, out_bias, gain, shift, (proj, 3, 0), bias, k, v,
        (out_proj, 2, 1),
    )


def error_function(x):
    x = jnp.clip(x, -4.0, 4.0)
    square = x * x
    top = jnp.full_like(x, -2.72614225801306e-10)
    for c in (
        2.77068142495902e-08,
        -2.10102402082508e-06,
        -5.69250639462346e-05,
        -7.34990630326855e-04,
        -2.95459980854025e-03,
        -1.60960333262415e-02,
    ):
        top = top * square + c
    bottom = jnp.full_like(x, -1.45660718464996e-05)
    for c in (-2.13374055278905e-04, -1.68282697438203e-03, -7.37332916720468e-03, -1.42647390514189e-02):
        bottom = bottom * square + c
    return x * top / bottom


def late_forward_kernel(
    audio_ref, text_ref, weight_ref, core_ref, gathered_ref, normed_ref, frames_ref, bias_ref, own_ref, first_ref,
    out_bias_ref, gain_ref, shift_ref, fc1_ref, fc1_bias_ref, cotangent_ref, fc2_ref,
    q_ref, k_ref, v_ref, weights_ref, inverse_ref, heads_ref, wq_ref, wk_ref, wv_ref, wo_ref,
    second_ref, normed_grad_ref, fc2_theirs_ref, fc1_theirs_ref, fc2_mine_ref, fc1_mine_ref, mlp_ref,
    fc1_bias_grad_ref, fc2_bias_grad_ref,
):
    width, half = wq_ref.shape
    for i, ref in enumerate((wq_ref, wk_ref, wv_ref)):
        ref[...] = gathered_ref[i * width : (i + 1) * width, :].astype(bf16)
        ref.send()
    for i in range(width // half):
        start = 3 * width + i * half
        wo_ref[:, i * half : (i + 1) * half] = gathered_ref[start : start + half, :].astype(bf16)
    wo_ref.send()
    q_ref[...] = ((dot(normed_ref[...], wq_ref[...], 1, 0) + bias_ref[0:1]) * SCALE).astype(bf16)
    k_ref[...] = dot(frames_ref[...], wk_ref[...], 1, 0).astype(bf16)
    v_ref[...] = (dot(frames_ref[...], wv_ref[...], 1, 0) + bias_ref[1:2]).astype(bf16)
    q_ref.send()
    k_ref.send()
    v_ref.send()
    for pair in range(half // PAIR):
        lanes = lanes_of(pair)
        heads, inverse = pair_forward(
            audio_ref[0], False, q_ref[:, lanes], k_ref[:, lanes], v_ref[:, lanes], weights_ref, 2 * pair
        )
        weights_ref.send(pair)
        heads_ref[:, lanes] = heads
        inverse_ref[:, lanes] = inverse
    heads_ref.send()
    inverse_ref.send()
    other = dot(heads_ref[...], wo_ref[...], 1, 0)

    second = first_ref[...] + (own_ref[...] + other) + out_bias_ref[1:2, :]
    second_ref[...] = second
    second_ref.send()
    unit, _ = norm_unit(second)
    normed = (unit * gain_ref[2:3, :] + shift_ref[2:3, :]).astype(bf16)
    grad_y = live_gradient(cotangent_ref[...], text_ref[0], weight_ref[0])
    fc2_bias_grad_ref[...] = column_sum(grad_y)
    grad = grad_y.astype(bf16)
    part = fc2_theirs_ref.shape[0]
    for turn, (fc2_out, fc1_out) in enumerate(((fc2_theirs_ref, fc1_theirs_ref), (fc2_mine_ref, fc1_mine_ref))):
        side = 1 - core_ref[0] if turn == 0 else core_ref[0]
        for start in range(0, part, FF_BLOCK):
            here = pl.ds(pl.multiple_of(side * part + start, FF_BLOCK), FF_BLOCK)
            there = slice(start, start + FF_BLOCK)
            fc1 = fc1_ref[:, here]
            pre = dot(normed, fc1, 1, 0) + fc1_bias_ref[:, here]
            cdf = 0.5 * (1.0 + error_function(pre * 0.7071067811865476))
            inner = (pre * cdf).astype(bf16)
            slope = cdf + pre * (0.3989422804014327 * jnp.exp(-0.5 * pre * pre))
            fc2 = fc2_ref[here, :]
            grad_pre = (dot(grad, fc2, 1, 1) * slope).astype(bf16)
            fc1_bias_grad_ref[:, here] = column_sum(grad_pre.astype(f32))
            fc2_out[there, :] = dot(inner, grad, 0, 0)
            fc1_out[:, there] = dot(normed, grad_pre, 0, 0)
            mlp_term = dot(inner, fc2, 1, 0)
            normed_term = dot(grad_pre, fc1, 1, 1)
            if turn == 0 and start == 0:
                mlp_ref[...] = mlp_term
                normed_grad_ref[...] = normed_term
            else:
                mlp_ref[...] += mlp_term
                normed_grad_ref[...] += normed_term
        fc2_out.send()
        fc1_out.send()


def late_forward(
    audio_len, text_len, corpus_weight, core, gathered, normed, frames_in, bias, own, first, out_bias, gain, shift,
    fc1, fc1_bias, cotangent, fc2,
):
    rows, width = first.shape
    units = fc2.shape[0]
    columns = frames_in.shape[0]
    half = gathered.shape[1]
    full = shaped((rows, width), f32)
    proj = shaped((width, half), bf16)
    return call(
        late_forward_kernel,
        "late_forward",
        [
            shaped((rows, half), bf16),
            shaped((columns, half), bf16),
            shaped((columns, half), bf16),
            (shaped((half // HEAD_DIM, rows, columns), bf16), half // PAIR),
            shaped((rows, half), f32),
            shaped((rows, half), bf16),
            proj,
            proj,
            proj,
            shaped((half, width), bf16),
            full,
            Resident(full),
            shaped((units // 2, width), f32),
            shaped((width, units // 2), f32),
            shaped((units // 2, width), f32),
            shaped((width, units // 2), f32),
            full,
            shaped((1, units), f32),
            shaped((1, width), f32),
        ],
        4 * rows * width * half + 4 * columns * width * half + 12 * rows * (columns * half + width * units),
        (audio_len, text_len, corpus_weight, core),
        gathered, normed, frames_in, bias, own, first, out_bias, gain, shift, fc1, fc1_bias, cotangent, fc2,
    )


def projection_grads(core, normed, source, low, dq, dk, dv, heads, theirs_ref, mine_ref):
    part = theirs_ref.shape[1]
    for out_ref, side in ((theirs_ref, 1 - core), (mine_ref, core)):
        here = pl.ds(pl.multiple_of(side * part, PAIR), part)
        piece = source[:, here]
        out_ref[0] = dot(normed[:, here], dq[...], 0, 0)
        out_ref[1] = dot(piece, dk[...], 0, 1)
        out_ref[2] = dot(piece, dv[...], 0, 1)
        out_ref[3] = dot(heads[...], low[:, here], 0, 0)
        out_ref.send()


def cross_own_back_kernel(
    length_ref, weight_ref, core_ref, received_ref, partial_ref, second_ref, cotangent_ref, gain_ref,
    out_ref, q_ref, k_ref, v_ref, inverse_ref, heads_ref, weights_ref, proj_ref, normed_ref, frames_ref,
    grad_second_ref, low_ref, gain_grad_ref, shift_grad_ref, bias_grad_ref,
    dq_ref, dk_ref, dv_ref, term_ref, dq_sum_ref, dv_sum_ref, theirs_ref, mine_ref,
):
    incoming = partial_ref[...] + received_ref[...]
    unit, inverse = norm_unit(second_ref[...])
    gain_grad_ref[...] = column_sum(incoming * unit)
    shift_grad_ref[...] = column_sum(incoming)
    grad_second = live_gradient(cotangent_ref[...], length_ref[0], weight_ref[0]) + norm_backward(
        incoming, unit, inverse, gain_ref[2:3, :]
    )
    grad_second_ref[...] = grad_second
    grad_second_ref.send()
    low = grad_second.astype(bf16)
    low_ref[...] = low
    low_ref.send()
    bias_grad_ref[...] = column_sum(grad_second)
    grad_heads = dot(low, out_ref[1], 1, 1).astype(bf16)
    for pair in range(q_ref.shape[1] // PAIR):
        lanes = lanes_of(pair)
        dq, dk, dv = pair_backward(
            q_ref[:, lanes], k_ref[:, lanes], v_ref[:, lanes], weights_ref, 2 * pair,
            inverse_ref[:, lanes], heads_ref[:, lanes], grad_heads[:, lanes],
        )
        dq_ref[:, lanes] = dq
        dk_ref[lanes, :] = dk
        dv_ref[lanes, :] = dv
    dk_ref.send()
    dv_ref.send()
    projection_grads(
        core_ref[0], normed_ref, frames_ref, low_ref, dq_ref, dk_ref, dv_ref, heads_ref, theirs_ref, mine_ref
    )
    term_ref[...] = dot(dq_ref[...], proj_ref[0], 1, 1)
    dq_sum_ref[...] = column_sum(dq_ref[...].astype(f32))
    dv_sum_ref[...] = row_sums(dv_ref[...])


def cross_own_back(
    text_len, corpus_weight, core, cotangent, second, partial_normed, received, gain, out_proj, proj,
    q, k, v, weights, inverse, heads, normed, frames_in,
):
    rows, width = second.shape
    columns, half = k.shape
    vector = shaped((1, width), f32)
    grads = shaped((4, width // 2, half), f32)
    return call(
        cross_own_back_kernel,
        "cross_own_back",
        [
            shaped((rows, width), f32),
            shaped((rows, width), bf16),
            vector,
            vector,
            vector,
            shaped((rows, half), bf16),
            shaped((half, columns), bf16),
            shaped((half, columns), bf16),
            shaped((rows, width), f32),
            shaped((1, half), f32),
            shaped((8, half), f32),
            grads,
            grads,
        ],
        8 * rows * width * half + 4 * columns * width * half + 24 * rows * columns * half,
        (text_len, corpus_weight, core),
        Resident(received), Resident(partial_normed), second, cotangent, gain, (out_proj, 2, 1), q, k, v, inverse, heads,
        (weights, half // PAIR), (proj, 3, 0), normed, frames_in,
    )


def other_back_kernel(
    core_ref, low_in_ref, wo_ref, q_ref, k_ref, v_ref, inverse_ref, heads_ref, weights_ref, wq_ref,
    own_term_ref, first_ref, grad_second_ref, gain_ref,
    out_ref, self_q_ref, self_k_ref, self_v_ref, self_inverse_ref, self_heads_ref, self_weights_ref,
    proj_ref, hidden_ref, normed_ref,
    dk_ref, dv_ref, grad_first_ref, gain_grad_ref, shift_grad_ref, bias_grad_ref,
    term_ref, theirs_ref, mine_ref, self_gain_grad_ref, self_shift_grad_ref, dq_sum_ref, dv_sum_ref,
    low_ref, self_dq_ref, self_dk_ref, self_dv_ref,
):
    grad_heads = dot(low_in_ref[...], wo_ref[...], 1, 1).astype(bf16)
    pairs = q_ref.shape[1] // PAIR
    dqs = []
    for pair in range(pairs):
        lanes = lanes_of(pair)
        dq, dk, dv = pair_backward(
            q_ref[:, lanes], k_ref[:, lanes], v_ref[:, lanes], weights_ref, 2 * pair,
            inverse_ref[:, lanes], heads_ref[:, lanes], grad_heads[:, lanes],
        )
        dqs.append(dq)
        dk_ref[lanes, :] = dk
        dv_ref[lanes, :] = dv
    dk_ref.send()
    dv_ref.send()
    incoming = own_term_ref[...] + dot(jnp.concatenate(dqs, axis=1), wq_ref[...], 1, 1)
    unit, inverse = norm_unit(first_ref[...])
    gain_grad_ref[...] = column_sum(incoming * unit)
    shift_grad_ref[...] = column_sum(incoming)
    grad_first = grad_second_ref[...] + norm_backward(incoming, unit, inverse, gain_ref[1:2, :])
    grad_first_ref[...] = grad_first
    grad_first_ref.send()
    low = grad_first.astype(bf16)
    low_ref[...] = low
    bias_grad_ref[...] = column_sum(grad_first)

    grad_heads = dot(low, out_ref[0], 1, 1).astype(bf16)
    for pair in range(pairs):
        lanes = lanes_of(pair)
        dq, dk, dv = pair_backward(
            self_q_ref[:, lanes], self_k_ref[:, lanes], self_v_ref[:, lanes], self_weights_ref, 2 * pair,
            self_inverse_ref[:, lanes], self_heads_ref[:, lanes], grad_heads[:, lanes],
        )
        self_dq_ref[:, lanes] = dq
        self_dk_ref[lanes, :] = dk
        self_dv_ref[lanes, :] = dv
    projection_grads(
        core_ref[0], normed_ref, normed_ref, low_ref, self_dq_ref, self_dk_ref, self_dv_ref, self_heads_ref,
        theirs_ref, mine_ref,
    )
    incoming = dot(self_dq_ref[...], proj_ref[0], 1, 1) + (
        dot(self_dk_ref[...], proj_ref[1], 0, 1) + dot(self_dv_ref[...], proj_ref[2], 0, 1)
    )
    term_ref[...] = incoming
    term_ref.send()
    unit, _ = norm_unit(hidden_ref[...].astype(f32))
    self_gain_grad_ref[...] = column_sum(incoming * unit)
    self_shift_grad_ref[...] = column_sum(incoming)
    dq_sum_ref[...] = column_sum(self_dq_ref[...].astype(f32))
    dv_sum_ref[...] = row_sums(self_dv_ref[...])


def other_back(
    core, low, wo, wq, q, k, v, weights, inverse, heads, own_term, first, grad_second, gain,
    out_proj, proj, self_q, self_k, self_v, self_weights, self_inverse, self_heads, hidden, normed,
):
    rows, width = first.shape
    columns, half = k.shape
    vector = shaped((1, width), f32)
    grads = shaped((4, width // 2, half), f32)
    return call(
        other_back_kernel,
        "other_back",
        [
            shaped((half, columns), bf16),
            shaped((half, columns), bf16),
            shaped((rows, width), f32),
            vector,
            vector,
            vector,
            shaped((rows, width), f32),
            grads,
            grads,
            vector,
            vector,
            shaped((1, half), f32),
            shaped((8, half), f32),
            shaped((rows, width), bf16),
            shaped((rows, half), bf16),
            shaped((half, rows), bf16),
            shaped((half, rows), bf16),
        ],
        20 * rows * width * half + 24 * rows * (columns + rows) * half,
        (core,),
        low, wo, q, k, v, inverse, heads, (weights, half // PAIR), wq, own_term, first, grad_second, gain,
        (out_proj, 2, 0), self_q, self_k, self_v, self_inverse, self_heads, (self_weights, half // PAIR),
        (proj, 3), hidden, normed,
    )


def encoder_grad_kernel(dk0_ref, dv0_ref, dk1_ref, dv1_ref, proj_ref, wk1_ref, wv1_ref, out_ref):
    own = dot(dk0_ref[...], proj_ref[1], 0, 1) + dot(dv0_ref[...], proj_ref[2], 0, 1)
    other = dot(dk1_ref[...], wk1_ref[...], 0, 1) + dot(dv1_ref[...], wv1_ref[...], 0, 1)
    out_ref[:, 0, :] = own + other


def encoder_grad(dk0, dv0, dk1, dv1, proj, wk1, wv1, frames):
    half, padded = dk0.shape
    width = wk1.shape[0]
    grad_block = pl.BlockSpec((half, FRAME_BLOCK), lambda i: (0, i))
    weight = pl.BlockSpec(wk1.shape, lambda i: (0, 0))
    return pl.pallas_call(
        encoder_grad_kernel,
        grid=(padded // FRAME_BLOCK,),
        in_specs=[grad_block] * 4 + [pl.BlockSpec(proj.shape, lambda i: (0, 0, 0)), weight, weight],
        out_specs=pl.BlockSpec((FRAME_BLOCK, 1, width), lambda i: (i, 0, 0)),
        out_shape=shaped((frames, 1, width), f32),
        compiler_params=pltpu.CompilerParams(vmem_limit_bytes=VMEM_LIMIT),
        cost_estimate=pl.CostEstimate(
            flops=8 * half * padded * width, bytes_accessed=6 * frames * width, transcendentals=0
        ),
        name="encoder_grad",
    )(dk0, dv0, dk1, dv1, proj, wk1, wv1)


def swap(value):
    return lax.ppermute(value, "tensor", [(0, 1), (1, 0)])


def tie(*values):
    return lax.optimization_barrier(values)


class Scatter:
    def __init__(self, theirs, mine, turned=False):
        self.members = lax.axis_size("dp")
        self.bits = self.members.bit_length() - 1
        self.order = list(range(self.bits))
        if turned and self.bits > 2:
            self.order = [0] + self.order[2:] + [1]
        self.stage = 0
        self.theirs, self.mine = theirs, mine

    def launch(self):
        if self.stage == self.bits:
            return
        other = 1 << self.order[self.stage]
        self.received = lax.ppermute(self.theirs, "dp", [(i, i ^ other) for i in range(self.members)])

    def land(self):
        if self.stage == self.bits:
            return
        total = self.mine + self.received
        if self.stage == 0:
            lead = total.shape[:-2]
            self.lead = len(lead)
            cuts = self.bits - 1
            total = total.reshape(lead + (2,) * cuts + (total.shape[-2] >> cuts, total.shape[-1]))
        self.stage += 1
        if self.stage < self.bits:
            bit = self.order[self.stage]
            axis = self.lead + self.bits - 1 - bit
            side = (lax.axis_index("dp") >> bit) & 1
            self.mine = lax.dynamic_index_in_dim(total, side, axis, keepdims=True)
            self.theirs = lax.dynamic_index_in_dim(total, 1 - side, axis, keepdims=True)
        else:
            self.part = total.reshape(total.shape[: self.lead] + total.shape[-2:])

    def finish(self):
        while self.stage < self.bits:
            self.land()
            self.launch()
        return self.part


def place_kernel(moves, gathered_ref, *refs):
    outs, (held, in_sems, out_sems) = refs[:-3], refs[-3:]
    reads = [
        pltpu.make_async_copy(gathered_ref.at[i], held.at[i], in_sems.at[i]) for i in range(held.shape[0])
    ]
    for read in reads:
        read.start()
    writes = []
    for i, read in enumerate(reads):
        read.wait()
        for start, count, out, target in moves[i]:
            writes.append(
                pltpu.make_async_copy(
                    held.at[i, pl.ds(start, count)], outs[out].at[target], out_sems.at[len(writes)]
                )
            )
            writes[-1].start()
    for write in writes:
        write.wait()


def place(gathered, width, units):
    members, total, half = gathered.shape
    parts = members // 2
    rows = units // members
    count = width // members
    proj = shaped((3, width, half), f32)
    outs = [shaped((units, width), f32), shaped((width, units), f32), proj, proj, shaped((2, half, width), f32)]
    if count % 8 == 0:
        moves = []
        for i in range(members):
            q, c = i // 2, i % 2
            moves.append([])
            for j in range(2):
                columns = pl.ds(j * half, half)
                moves[i].append((j * rows, rows, 0, (pl.ds(c * width + q * rows, rows), columns)))
                columns = pl.ds(c * width + j * half, half)
                moves[i].append(((2 + j) * rows, rows, 1, (pl.ds(q * rows, rows), columns)))
            here = pl.ds(c * (width // 2) + q * count, count)
            for branch in range(2):
                start = 4 * rows + branch * 4 * count
                for a in range(3):
                    moves[i].append((start + a * count, count, 2 + branch, (a, here)))
                target = (1 - branch, pl.ds(q * count, count), pl.ds(c * half, half))
                moves[i].append((start + 3 * count, count, 4, target))
        anywhere = pl.BlockSpec(memory_space=pl.ANY)
        return pl.pallas_call(
            partial(place_kernel, moves),
            in_specs=[anywhere],
            out_specs=[anywhere] * len(outs),
            out_shape=outs,
            scratch_shapes=[
                pltpu.VMEM(gathered.shape, f32),
                pltpu.SemaphoreType.DMA((members,)),
                pltpu.SemaphoreType.DMA((sum(len(m) for m in moves),)),
            ],
            compiler_params=pltpu.CompilerParams(vmem_limit_bytes=VMEM_LIMIT),
            cost_estimate=pl.CostEstimate(flops=0, bytes_accessed=8 * gathered.size, transcendentals=0),
            name="place",
        )(gathered)
    split = gathered[:, : 4 * rows].reshape(parts, 2, 2, 2, rows, half)
    fc2 = split[:, :, 0].transpose(1, 0, 3, 2, 4).reshape(units, width)
    fc1 = split[:, :, 1].transpose(0, 3, 1, 2, 4).reshape(width, units)
    split = gathered[:, 4 * rows :].reshape(parts, 2, 2, 4, count, half)
    projections = split[:, :, :, :3].transpose(2, 3, 1, 0, 4, 5).reshape(2, 3, width, half)
    outputs = split[:, :, ::-1, 3].transpose(2, 0, 3, 1, 4).reshape(2, half, width)
    return fc2, fc1, projections[0], projections[1], outputs


def per_device(
    hidden,
    encoder,
    text_len,
    audio_len,
    corpus_weight,
    cotangent,
    norm_gain,
    norm_bias,
    self_proj,
    self_bias,
    cross_proj,
    cross_bias,
    out_proj,
    out_bias,
    fc1_weight,
    fc1_bias,
    fc2_weight,
    fc2_bias,
):
    sequences, frames, width = encoder.shape
    members = lax.axis_size("dp")
    me = lax.axis_index("dp")
    half = self_proj.shape[2]
    padded = -(-frames // FRAME_BLOCK) * FRAME_BLOCK
    core = (me & 1).astype(jnp.int32).reshape(1)

    cross_rows = jnp.concatenate(
        [cross_proj.reshape(-1, half), out_proj[1][:, :half], out_proj[1][:, half:]], axis=0
    )
    count = cross_rows.shape[0] // members
    part = swap(lax.dynamic_slice_in_dim(cross_rows, me * count, count, 0).astype(f32))
    hidden_in, part = tie(hidden, part)
    gathered = lax.all_gather(part, "dp", axis=0, tiled=True)

    normed_self, q_self, k_self, v_self, weights_self, inverse_self, heads_self, partial_self = self_forward(
        text_len, hidden_in, norm_gain, norm_bias, self_proj, self_bias, out_proj
    )
    received = swap(partial_self)
    other_bias = swap(cross_bias)

    frames_in = jnp.pad(encoder.reshape(frames, width), ((0, padded - frames), (0, 0)))
    k_own = dot(frames_in, cross_proj[1], 1, 0).astype(bf16)
    v_own = (dot(frames_in, cross_proj[2], 1, 0) + cross_bias[1]).astype(bf16)
    received, k_own, v_own = tie(received, k_own, v_own)
    first, normed_cross, q_own, weights_own, inverse_own, heads_own, term_own = cross_own(
        audio_len, hidden, partial_self, received, out_bias, norm_gain, norm_bias,
        cross_proj, cross_bias, k_own, v_own, out_proj,
    )
    gathered, normed_cross = tie(gathered, normed_cross)
    (
        q_other, k_other, v_other, weights_other, inverse_other, heads_other,
        wq_other, wk_other, wv_other, wo_other,
        second, partial_normed, fc2_theirs, fc1_theirs, fc2_mine, fc1_mine, partial_mlp,
        fc1_bias_grad, fc2_bias_grad,
    ) = late_forward(
        audio_len, text_len, corpus_weight, core, gathered, normed_cross, frames_in, other_bias, term_own, first,
        out_bias, norm_gain, norm_bias, fc1_weight, fc1_bias.reshape(1, -1), cotangent, fc2_weight,
    )
    received = swap(partial_normed)
    fc2_share = Scatter(fc2_theirs, fc2_mine)
    fc1_share = Scatter(fc1_theirs, fc1_mine, turned=True)
    fc2_share.launch()
    fc1_share.launch()
    fc2_share.land()
    fc2_share.launch()
    fc1_share.land()
    fc1_share.launch()

    (
        grad_second, second_low, gain_mlp, shift_mlp, bias_cross, dq_own, dk_own, dv_own, back_own,
        dq_cross_sum, dv_cross_sum, cross_theirs, cross_mine,
    ) = cross_own_back(
        text_len, corpus_weight, core, cotangent, second, partial_normed, received, norm_gain,
        out_proj, cross_proj, q_own, k_own, v_own, weights_own, inverse_own, heads_own, normed_cross, frames_in,
    )
    cross_theirs, fc2_share.received, fc1_share.received = tie(
        cross_theirs, fc2_share.received, fc1_share.received
    )
    cross_share = Scatter(cross_theirs, cross_mine)
    cross_share.launch()
    fc2_share.land()
    fc1_share.land()
    fc2_share.launch()
    fc1_share.launch()
    cross_share.received, fc2_share.theirs, fc1_share.theirs = tie(
        cross_share.received, fc2_share.theirs, fc1_share.theirs
    )
    cross_share.land()
    second_low, cross_share.theirs = tie(second_low, cross_share.theirs)
    cross_share.launch()

    (
        dk_other, dv_other, grad_first, gain_cross, shift_cross, bias_self, partial_normed,
        self_theirs, self_mine, gain_self, shift_self, dq_self_sum, dv_self_sum, *_,
    ) = other_back(
        core, second_low, wo_other, wq_other, q_other, k_other, v_other, weights_other, inverse_other, heads_other,
        back_own, first, grad_second, norm_gain, out_proj, self_proj, q_self, k_self, v_self, weights_self,
        inverse_self, heads_self, hidden, normed_self,
    )
    self_theirs, cross_share.received, fc1_share.received, fc2_share.received = tie(
        self_theirs, cross_share.received, fc1_share.received, fc2_share.received
    )
    self_share = Scatter(self_theirs, self_mine)
    self_share.launch()
    fc1_share.land()
    cross_share.land()
    fc1_share.launch()
    cross_share.launch()
    fc2_share.land()
    fc2_share.launch()
    self_share.received, fc1_share.theirs, cross_share.theirs, fc2_share.theirs = tie(
        self_share.received, fc1_share.theirs, cross_share.theirs, fc2_share.theirs
    )
    self_share.land()
    self_share.launch()
    partial_normed, dk_own, self_share.theirs = tie(partial_normed, dk_own, self_share.theirs)
    received = swap(partial_normed)
    norm_self = jnp.concatenate([gain_self, shift_self], axis=0)
    norm_received = swap(norm_self)
    cross_share.received, fc2_share.received, fc1_share.received, partial_normed = tie(
        cross_share.received, fc2_share.received, fc1_share.received, partial_normed
    )
    cross_share.land()
    cross_share.launch()
    fc2_part = fc2_share.finish()
    fc1_part = fc1_share.finish()
    dk_own, cross_share.theirs = tie(dk_own, cross_share.theirs)
    grad_encoder = encoder_grad(
        dk_own, dv_own, dk_other, dv_other, cross_proj, wk_other, wv_other, frames
    ).reshape(encoder.shape)
    cross_share.received, self_share.received, grad_encoder, fc2_part, fc1_part = tie(
        cross_share.received, self_share.received, grad_encoder, fc2_part, fc1_part
    )
    self_share.land()
    self_share.launch()
    cross_part = cross_share.finish()
    cross_part, self_share.theirs = tie(cross_part, self_share.theirs)

    small = (
        norm_self + norm_received,
        gain_cross,
        gain_mlp,
        shift_cross,
        shift_mlp,
        dq_self_sum,
        dv_self_sum[0:1],
        dq_cross_sum,
        dv_cross_sum[0:1],
        bias_self,
        bias_cross,
        fc1_bias_grad,
        fc2_bias_grad,
    )
    flat = jnp.concatenate([item.reshape(-1, half) for item in small], axis=0)

    most = [fc2_part[:, :half], fc2_part[:, half:], fc1_part[:, :half], fc1_part[:, half:]]
    most = jnp.concatenate([item.reshape(-1, half) for item in (*most, cross_part)], axis=0)
    unit_self, root_self = norm_unit(hidden.astype(f32))
    grad_hidden = (
        grad_first + norm_backward(partial_normed + received, unit_self, root_self, norm_gain[0])
    ).astype(bf16)
    grad_hidden, flat, most, self_share.received = tie(grad_hidden, flat, most, self_share.received)
    self_part = self_share.finish()
    every = jnp.concatenate([most, self_part.reshape(-1, half)], axis=0)
    flat, partial_mlp, every = tie(flat, partial_mlp, every)
    every = lax.all_gather(every, "dp", axis=0, tiled=False)
    for bit in range(members.bit_length() - 1):
        flat = flat + lax.ppermute(flat, "dp", [(i, i ^ (1 << bit)) for i in range(members)])
    received_mlp = swap(partial_mlp)
    result = (second + (partial_mlp + received_mlp) + fc2_bias).astype(bf16)
    fc2_weight_grad, fc1_weight_grad, cross_proj_grad, self_proj_grad, out_proj_grad = place(
        every, width, fc2_weight.shape[0]
    )
    small_out = []
    offset = 0
    for item in small:
        count = item.size // half
        small_out.append(flat[offset : offset + count].reshape(item.shape))
        offset += count
    (
        norm_self, gain_cross, gain_mlp, shift_cross, shift_mlp, dq_self_sum, dv_self_sum, dq_cross_sum,
        dv_cross_sum, bias_self, bias_cross, fc1_bias_grad, fc2_bias_grad,
    ) = small_out
    return (
        result,
        grad_hidden,
        grad_encoder,
        jnp.concatenate([norm_self[0:1], gain_cross, gain_mlp], axis=0),
        jnp.concatenate([norm_self[1:2], shift_cross, shift_mlp], axis=0),
        self_proj_grad,
        jnp.concatenate([dq_self_sum, dv_self_sum], axis=0),
        cross_proj_grad,
        jnp.concatenate([dq_cross_sum, dv_cross_sum], axis=0),
        out_proj_grad,
        jnp.concatenate([bias_self, bias_cross], axis=0),
        fc1_weight_grad,
        fc1_bias_grad.reshape(-1),
        fc2_weight_grad,
        fc2_bias_grad.reshape(-1),
    )


def solution(mesh):
    placed = (
        P("dp", None),
        P("dp", None, None),
        P("dp"),
        P("dp"),
        P("dp"),
        P("dp", None),
        P(),
        P(),
        P(None, None, "tensor"),
        P(None, "tensor"),
        P(None, None, "tensor"),
        P(None, "tensor"),
        P(None, "tensor", None),
        P(),
        P(None, "tensor"),
        P("tensor"),
        P("tensor", None),
        P(),
    )
    return jax.shard_map(
        per_device,
        mesh=mesh,
        in_specs=placed,
        out_specs=(
            P("dp", None),
            P("dp", None),
            P("dp", None, None),
            P(),
            P(),
            P(None, None, "tensor"),
            P(None, "tensor"),
            P(None, None, "tensor"),
            P(None, "tensor"),
            P(None, "tensor", None),
            P(),
            P(None, "tensor"),
            P("tensor"),
            P("tensor", None),
            P(),
        ),
        check_vma=False,
    )
```

```python
from functools import partial

import jax
import jax.numpy as jnp
from jax import lax
from jax.experimental import pallas as pl
from jax.experimental.pallas import tpu as pltpu
from jax.sharding import PartitionSpec as P

HEAD_DIM = 64
SCALE = HEAD_DIM ** (-0.5)
PAIR = 2 * HEAD_DIM
FF_BLOCK = 256
FRAME_BLOCK = 256
VMEM_LIMIT = 63 * 1024 * 1024 + 512 * 1024
COST_SHARE = 64
epsilon = 1e-05
masked_value = -1e30
f32 = jnp.float32
bf16 = jnp.bfloat16


def dot(a, b, ca, cb):
    return lax.dot_general(a, b, (((ca,), (cb,)), ((), ())), preferred_element_type=f32)


def shaped(shape, dtype):
    return jax.ShapeDtypeStruct(shape, dtype)


class Source:
    def __init__(self, ref, held, sems, first_sem, pieces):
        self.held, self.shape, self.dtype = held, held.shape, held.dtype
        self.size = held.shape[0] // pieces
        self.ref, self.sems, self.first_sem = ref, sems, first_sem
        self.copies = [None] * pieces
        self.pending = [True] * pieces

    def fetch(self, *pieces):
        for piece in pieces or range(len(self.copies)):
            if self.copies[piece] is None:
                here = pl.ds(piece * self.size, self.size)
                self.copies[piece] = pltpu.make_async_copy(
                    self.ref.at[here], self.held.at[here], self.sems.at[self.first_sem + piece]
                )
                self.copies[piece].start()

    def wait(self, piece):
        if self.pending[piece]:
            self.fetch(piece)
            self.pending[piece] = False
            self.copies[piece].wait()

    def __getitem__(self, index):
        if len(self.copies) > 1 and isinstance(index, int):
            self.wait(index // self.size)
        else:
            for piece in range(len(self.copies)):
                self.wait(piece)
        return self.held[index]


class Sink:
    def __init__(self, ref, held, sems, first_sem, pieces):
        self.held, self.shape, self.dtype = held, held.shape, held.dtype
        self.size = held.shape[0] // pieces
        self.copies = []
        self.sent = []
        for i in range(pieces):
            here = pl.ds(i * self.size, self.size)
            self.copies.append(pltpu.make_async_copy(held.at[here], ref.at[here], sems.at[first_sem + i]))
            self.sent.append(False)

    def __getitem__(self, index):
        return self.held[index]

    def __setitem__(self, index, value):
        self.held[index] = value

    def send(self, piece=0):
        self.sent[piece] = True
        self.copies[piece].start()


class Resident:
    def __init__(self, value):
        self.value = value

    def __getitem__(self, index):
        return self.value[index]

    def __setitem__(self, index, value):
        self.value[index] = value


def call(kernel, name, out_shape, flops, scalars, *arrays):
    arrays = [a if isinstance(a, tuple) else (a, 1) for a in arrays]
    used = [a[2:] for a in arrays]
    arrays = [a[:2] for a in arrays]
    outs = [o if isinstance(o, tuple) else (o, 1) for o in out_shape]
    in_stays = [isinstance(a, Resident) for a, _ in arrays]
    out_stays = [isinstance(o, Resident) for o, _ in outs]
    in_pieces = [0 if stays else pieces for (_, pieces), stays in zip(arrays, in_stays)]
    out_pieces = [0 if stays else pieces for (_, pieces), stays in zip(outs, out_stays)]
    arrays = [a.value if stays else a for (a, _), stays in zip(arrays, in_stays)]
    outs = [o.value if stays else o for (o, _), stays in zip(outs, out_stays)]
    moved = sum(a.size * a.dtype.itemsize for a in (*arrays, *outs))

    def body(*refs):
        refs = list(refs)
        scalar_refs = [refs.pop(0) for _ in scalars]
        in_refs = [refs.pop(0) for _ in arrays]
        out_refs = [refs.pop(0) for _ in outs]
        in_held = [None if stays else refs.pop(0) for stays in in_stays]
        out_held = [None if stays else refs.pop(0) for stays in out_stays]
        in_sems, out_sems = refs
        sources = []
        for i, (ref, held) in enumerate(zip(in_refs, in_held)):
            if in_stays[i]:
                sources.append(Resident(ref))
            else:
                sources.append(Source(ref, held, in_sems, sum(in_pieces[:i]), in_pieces[i]))
        sinks = []
        for i, (ref, held) in enumerate(zip(out_refs, out_held)):
            if out_stays[i]:
                sinks.append(Resident(ref))
            else:
                sinks.append(Sink(ref, held, out_sems, sum(out_pieces[:i]), out_pieces[i]))
        moving = [source for source in sources if isinstance(source, Source)]
        leaving = [sink for sink in sinks if isinstance(sink, Sink)]
        for source, only in zip(sources, used):
            if isinstance(source, Source):
                source.fetch(*only)
        kernel(*scalar_refs, *sources, *sinks)
        for source in moving:
            for piece in range(len(source.copies)):
                if source.copies[piece] is not None:
                    source.wait(piece)
        for sink in leaving:
            for piece, sent in enumerate(sink.sent):
                if not sent:
                    sink.send(piece)
        for sink in leaving:
            for copy in sink.copies:
                copy.wait()

    anywhere = pl.BlockSpec(memory_space=pl.ANY)
    here = pl.BlockSpec(memory_space=pltpu.VMEM)
    scratch = [pltpu.VMEM(a.shape, a.dtype) for a, stays in zip(arrays, in_stays) if not stays]
    scratch += [pltpu.VMEM(o.shape, o.dtype) for o, stays in zip(outs, out_stays) if not stays]
    return pl.pallas_call(
        body,
        in_specs=[pl.BlockSpec(memory_space=pltpu.SMEM)] * len(scalars)
        + [here if stays else anywhere for stays in in_stays],
        out_specs=[here if stays else anywhere for stays in out_stays],
        out_shape=outs,
        scratch_shapes=scratch
        + [pltpu.SemaphoreType.DMA((sum(in_pieces),)), pltpu.SemaphoreType.DMA((sum(out_pieces),))],
        compiler_params=pltpu.CompilerParams(vmem_limit_bytes=VMEM_LIMIT),
        cost_estimate=pl.CostEstimate(
            flops=flops // COST_SHARE, bytes_accessed=moved // COST_SHARE, transcendentals=0
        ),
        name=name,
    )(*scalars, *arrays)


def lanes_of(pair):
    return slice(pair * PAIR, (pair + 1) * PAIR)


def add_up(terms):
    total = terms[0]
    for term in terms[1:]:
        total = total + term
    return total


def norm_unit(values):
    centered = values - jnp.mean(values, axis=-1, keepdims=True)
    inverse = lax.rsqrt(jnp.mean(centered * centered, axis=-1, keepdims=True) + epsilon)
    return centered * inverse, inverse


def norm_backward(incoming, unit, inverse, gain):
    scaled = incoming * gain
    scaled_mean = jnp.mean(scaled, axis=-1, keepdims=True)
    along_unit = jnp.mean(scaled * unit, axis=-1, keepdims=True)
    return inverse * (scaled - scaled_mean - unit * along_unit)


def column_sum(values):
    return jnp.sum(values, axis=0, keepdims=True)


def live_gradient(cotangent, text_len, corpus_weight):
    places = lax.broadcasted_iota(jnp.int32, (cotangent.shape[0], 1), 0)
    live = jnp.where(places < text_len, corpus_weight, 0.0)
    return cotangent.astype(f32) * live


def lane_masks(rows):
    return lax.broadcasted_iota(jnp.int32, (rows, PAIR), 1) < HEAD_DIM


def pair_forward(length, causal, q, k, v, weights_ref, start):
    rows, columns = q.shape[0], k.shape[0]
    first_lanes = lane_masks(rows)
    if causal:
        places = lax.broadcasted_iota(jnp.int32, (rows, columns), 1)
        allowed = (places < length) & (places <= lax.broadcasted_iota(jnp.int32, (rows, columns), 0))
    else:
        places = lax.broadcasted_iota(jnp.int32, (1, columns), 1)
        shift = jnp.where(places < length, 0.0, masked_value)
    scores = []
    for head in range(2):
        mine = first_lanes if head == 0 else jnp.logical_not(first_lanes)
        raw = dot(jnp.where(mine, q, jnp.zeros_like(q)), k, 1, 1)
        scores.append(jnp.where(allowed, raw, masked_value) if causal else raw + shift)
    inverses = []
    for head in range(2):
        largest = jnp.max(scores[head], axis=-1, keepdims=True)
        weights = jnp.exp(scores[head] - largest)
        inverses.append(1.0 / jnp.sum(weights, axis=-1, keepdims=True))
        weights_ref[start + head] = weights.astype(bf16)
    mixed = [dot(weights_ref[start + head], v, 1, 0) for head in range(2)]
    inverse = jnp.where(first_lanes, inverses[0], inverses[1])
    return (jnp.where(first_lanes, mixed[0], mixed[1]) * inverse).astype(bf16), inverse


def pair_backward(q, k, v, weights_ref, start, inverse, heads, grad_heads):
    first_lanes = lane_masks(q.shape[0])
    grad = (grad_heads.astype(f32) * inverse).astype(bf16)
    along = grad.astype(f32) * heads.astype(f32)
    dq = []
    dk = None
    dv = None
    for head in range(2):
        mine = first_lanes if head == 0 else jnp.logical_not(first_lanes)
        grad_one = jnp.where(mine, grad, jnp.zeros_like(grad))
        q_one = jnp.where(mine, q, jnp.zeros_like(q))
        row_terms = jnp.sum(jnp.where(mine, along, 0.0), axis=-1, keepdims=True)
        weights = weights_ref[start + head]
        grad_probs = dot(grad_one, v, 1, 1)
        grad_scores = (weights.astype(f32) * (grad_probs - row_terms)).astype(bf16)
        dv_one = dot(grad_one, weights, 0, 0)
        dk_one = dot(q_one, grad_scores, 0, 0)
        dq.append(dot(grad_scores, k, 1, 0))
        dk = dk_one if dk is None else dk + dk_one
        dv = dv_one if dv is None else dv + dv_one
    dq = (jnp.where(first_lanes, dq[0], dq[1]) * SCALE).astype(bf16)
    return dq, dk.astype(bf16), dv.astype(bf16)


def row_sums(values):
    return dot(jnp.ones((8, values.shape[1]), bf16), values, 1, 1)


def self_forward_kernel(
    length_ref, hidden_ref, gain_ref, shift_ref, proj_ref, bias_ref, out_ref,
    normed_ref, q_ref, k_ref, v_ref, weights_ref, inverse_ref, heads_ref, partial_ref,
):
    unit, _ = norm_unit(hidden_ref[...].astype(f32))
    normed = (unit * gain_ref[0:1, :] + shift_ref[0:1, :]).astype(bf16)
    normed_ref[...] = normed
    normed_ref.send()
    q_ref[...] = ((dot(normed, proj_ref[0], 1, 0) + bias_ref[0:1]) * SCALE).astype(bf16)
    k_ref[...] = dot(normed, proj_ref[1], 1, 0).astype(bf16)
    v_ref[...] = (dot(normed, proj_ref[2], 1, 0) + bias_ref[1:2]).astype(bf16)
    q_ref.send()
    k_ref.send()
    v_ref.send()
    for pair in range(q_ref.shape[1] // PAIR):
        lanes = lanes_of(pair)
        heads, inverse = pair_forward(
            length_ref[0], True, q_ref[:, lanes], k_ref[:, lanes], v_ref[:, lanes], weights_ref, 2 * pair
        )
        weights_ref.send(pair)
        heads_ref[:, lanes] = heads
        inverse_ref[:, lanes] = inverse
    heads_ref.send()
    inverse_ref.send()
    partial_ref[...] = dot(heads_ref[...], out_ref[0], 1, 0)


def self_forward(text_len, hidden, gain, shift, proj, bias, out_proj):
    rows, width = hidden.shape
    half = proj.shape[2]
    return call(
        self_forward_kernel,
        "self_forward",
        [
            shaped((rows, width), bf16),
            shaped((rows, half), bf16),
            shaped((rows, half), bf16),
            shaped((rows, half), bf16),
            (shaped((half // HEAD_DIM, rows, rows), bf16), half // PAIR),
            shaped((rows, half), f32),
            shaped((rows, half), bf16),
            shaped((rows, width), f32),
        ],
        8 * rows * width * half + 12 * rows * rows * half,
        (text_len,),
        hidden, gain, shift, (proj, 3), bias, (out_proj, 2, 0),
    )


def cross_own_kernel(
    length_ref, received_ref, partial_ref, hidden_ref, out_bias_ref, gain_ref, shift_ref,
    proj_ref, bias_ref, k_ref, v_ref, out_ref,
    first_ref, normed_ref, q_ref, weights_ref, inverse_ref, heads_ref, term_ref,
):
    first = hidden_ref[...].astype(f32) + (partial_ref[...] + received_ref[...]) + out_bias_ref[0:1, :]
    first_ref[...] = first
    first_ref.send()
    unit, _ = norm_unit(first)
    normed = (unit * gain_ref[1:2, :] + shift_ref[1:2, :]).astype(bf16)
    normed_ref[...] = normed
    normed_ref.send()
    q_ref[...] = ((dot(normed, proj_ref[0], 1, 0) + bias_ref[0:1]) * SCALE).astype(bf16)
    q_ref.send()
    for pair in range(q_ref.shape[1] // PAIR):
        lanes = lanes_of(pair)
        heads, inverse = pair_forward(
            length_ref[0], False, q_ref[:, lanes], k_ref[:, lanes], v_ref[:, lanes], weights_ref, 2 * pair
        )
        weights_ref.send(pair)
        heads_ref[:, lanes] = heads
        inverse_ref[:, lanes] = inverse
    heads_ref.send()
    inverse_ref.send()
    term_ref[...] = dot(heads_ref[...], out_ref[1], 1, 0)


def cross_own(audio_len, hidden, partial_self, received, out_bias, gain, shift, proj, bias, k, v, out_proj):
    rows, width = hidden.shape
    columns, half = k.shape
    return call(
        cross_own_kernel,
        "cross_own",
        [
            shaped((rows, width), f32),
            shaped((rows, width), bf16),
            shaped((rows, half), bf16),
            (shaped((half // HEAD_DIM, rows, columns), bf16), half // PAIR),
            shaped((rows, half), f32),
            shaped((rows, half), bf16),
            shaped((rows, width), f32),
        ],
        4 * rows * width * half + 12 * rows * columns * half,
        (audio_len,),
        received, partial_self, hidden, out_bias, gain, shift, (proj, 3, 0), bias, k, v,
        (out_proj, 2, 1),
    )


def error_function(x):
    x = jnp.clip(x, -4.0, 4.0)
    square = x * x
    top = jnp.full_like(x, -2.72614225801306e-10)
    for c in (
        2.77068142495902e-08,
        -2.10102402082508e-06,
        -5.69250639462346e-05,
        -7.34990630326855e-04,
        -2.95459980854025e-03,
        -1.60960333262415e-02,
    ):
        top = top * square + c
    bottom = jnp.full_like(x, -1.45660718464996e-05)
    for c in (-2.13374055278905e-04, -1.68282697438203e-03, -7.37332916720468e-03, -1.42647390514189e-02):
        bottom = bottom * square + c
    return x * top / bottom


def late_forward_kernel(
    audio_ref, text_ref, weight_ref, core_ref, gathered_ref, normed_ref, frames_ref, bias_ref, own_ref, first_ref,
    out_bias_ref, gain_ref, shift_ref, fc1_ref, fc1_bias_ref, cotangent_ref, fc2_ref,
    q_ref, k_ref, v_ref, weights_ref, inverse_ref, heads_ref, wq_ref, wk_ref, wv_ref, wo_ref,
    second_ref, normed_grad_ref, fc2_theirs_ref, fc1_theirs_ref, fc2_mine_ref, fc1_mine_ref, mlp_ref,
    fc1_bias_grad_ref, fc2_bias_grad_ref,
):
    width, half = wq_ref.shape
    for i, ref in enumerate((wq_ref, wk_ref, wv_ref)):
        ref[...] = gathered_ref[i * width : (i + 1) * width, :].astype(bf16)
        ref.send()
    for i in range(width // half):
        start = 3 * width + i * half
        wo_ref[:, i * half : (i + 1) * half] = gathered_ref[start : start + half, :].astype(bf16)
    wo_ref.send()
    q_ref[...] = ((dot(normed_ref[...], wq_ref[...], 1, 0) + bias_ref[0:1]) * SCALE).astype(bf16)
    k_ref[...] = dot(frames_ref[...], wk_ref[...], 1, 0).astype(bf16)
    v_ref[...] = (dot(frames_ref[...], wv_ref[...], 1, 0) + bias_ref[1:2]).astype(bf16)
    q_ref.send()
    k_ref.send()
    v_ref.send()
    for pair in range(half // PAIR):
        lanes = lanes_of(pair)
        heads, inverse = pair_forward(
            audio_ref[0], False, q_ref[:, lanes], k_ref[:, lanes], v_ref[:, lanes], weights_ref, 2 * pair
        )
        weights_ref.send(pair)
        heads_ref[:, lanes] = heads
        inverse_ref[:, lanes] = inverse
    heads_ref.send()
    inverse_ref.send()
    other = dot(heads_ref[...], wo_ref[...], 1, 0)

    second = first_ref[...] + (own_ref[...] + other) + out_bias_ref[1:2, :]
    second_ref[...] = second
    second_ref.send()
    unit, _ = norm_unit(second)
    normed = (unit * gain_ref[2:3, :] + shift_ref[2:3, :]).astype(bf16)
    grad_y = live_gradient(cotangent_ref[...], text_ref[0], weight_ref[0])
    fc2_bias_grad_ref[...] = column_sum(grad_y)
    grad = grad_y.astype(bf16)
    part = fc2_theirs_ref.shape[0]
    for turn, (fc2_out, fc1_out) in enumerate(((fc2_theirs_ref, fc1_theirs_ref), (fc2_mine_ref, fc1_mine_ref))):
        side = 1 - core_ref[0] if turn == 0 else core_ref[0]
        for start in range(0, part, FF_BLOCK):
            here = pl.ds(pl.multiple_of(side * part + start, FF_BLOCK), FF_BLOCK)
            there = slice(start, start + FF_BLOCK)
            fc1 = fc1_ref[:, here]
            pre = dot(normed, fc1, 1, 0) + fc1_bias_ref[:, here]
            cdf = 0.5 * (1.0 + error_function(pre * 0.7071067811865476))
            inner = (pre * cdf).astype(bf16)
            slope = cdf + pre * (0.3989422804014327 * jnp.exp(-0.5 * pre * pre))
            fc2 = fc2_ref[here, :]
            grad_pre = (dot(grad, fc2, 1, 1) * slope).astype(bf16)
            fc1_bias_grad_ref[:, here] = column_sum(grad_pre.astype(f32))
            fc2_out[there, :] = dot(inner, grad, 0, 0)
            fc1_out[:, there] = dot(normed, grad_pre, 0, 0)
            mlp_term = dot(inner, fc2, 1, 0)
            normed_term = dot(grad_pre, fc1, 1, 1)
            if turn == 0 and start == 0:
                mlp_ref[...] = mlp_term
                normed_grad_ref[...] = normed_term
            else:
                mlp_ref[...] += mlp_term
                normed_grad_ref[...] += normed_term
        fc2_out.send()
        fc1_out.send()


def late_forward(
    audio_len, text_len, corpus_weight, core, gathered, normed, frames_in, bias, own, first, out_bias, gain, shift,
    fc1, fc1_bias, cotangent, fc2,
):
    rows, width = first.shape
    units = fc2.shape[0]
    columns = frames_in.shape[0]
    half = gathered.shape[1]
    full = shaped((rows, width), f32)
    proj = shaped((width, half), bf16)
    return call(
        late_forward_kernel,
        "late_forward",
        [
            shaped((rows, half), bf16),
            shaped((columns, half), bf16),
            shaped((columns, half), bf16),
            (shaped((half // HEAD_DIM, rows, columns), bf16), half // PAIR),
            shaped((rows, half), f32),
            shaped((rows, half), bf16),
            proj,
            proj,
            proj,
            shaped((half, width), bf16),
            full,
            full,
            shaped((units // 2, width), f32),
            shaped((width, units // 2), f32),
            shaped((units // 2, width), f32),
            shaped((width, units // 2), f32),
            full,
            shaped((1, units), f32),
            shaped((1, width), f32),
        ],
        4 * rows * width * half + 4 * columns * width * half + 12 * rows * (columns * half + width * units),
        (audio_len, text_len, corpus_weight, core),
        gathered, normed, frames_in, bias, own, first, out_bias, gain, shift, fc1, fc1_bias, cotangent, fc2,
    )


def projection_grads(core, normed, source, low, dq, dk, dv, heads, theirs_ref, mine_ref):
    part = theirs_ref.shape[1]
    for out_ref, side in ((theirs_ref, 1 - core), (mine_ref, core)):
        here = pl.ds(pl.multiple_of(side * part, PAIR), part)
        piece = source[:, here]
        out_ref[0] = dot(normed[:, here], dq[...], 0, 0)
        out_ref[1] = dot(piece, dk[...], 0, 1)
        out_ref[2] = dot(piece, dv[...], 0, 1)
        out_ref[3] = dot(heads[...], low[:, here], 0, 0)
        out_ref.send()


def cross_own_back_kernel(
    length_ref, weight_ref, core_ref, received_ref, partial_ref, second_ref, cotangent_ref, gain_ref,
    out_ref, q_ref, k_ref, v_ref, inverse_ref, heads_ref, weights_ref, proj_ref, normed_ref, frames_ref,
    grad_second_ref, low_ref, gain_grad_ref, shift_grad_ref, bias_grad_ref,
    dq_ref, dk_ref, dv_ref, term_ref, dq_sum_ref, dv_sum_ref, theirs_ref, mine_ref,
):
    incoming = partial_ref[...] + received_ref[...]
    unit, inverse = norm_unit(second_ref[...])
    gain_grad_ref[...] = column_sum(incoming * unit)
    shift_grad_ref[...] = column_sum(incoming)
    grad_second = live_gradient(cotangent_ref[...], length_ref[0], weight_ref[0]) + norm_backward(
        incoming, unit, inverse, gain_ref[2:3, :]
    )
    grad_second_ref[...] = grad_second
    grad_second_ref.send()
    low = grad_second.astype(bf16)
    low_ref[...] = low
    low_ref.send()
    bias_grad_ref[...] = column_sum(grad_second)
    grad_heads = dot(low, out_ref[1], 1, 1).astype(bf16)
    for pair in range(q_ref.shape[1] // PAIR):
        lanes = lanes_of(pair)
        dq, dk, dv = pair_backward(
            q_ref[:, lanes], k_ref[:, lanes], v_ref[:, lanes], weights_ref, 2 * pair,
            inverse_ref[:, lanes], heads_ref[:, lanes], grad_heads[:, lanes],
        )
        dq_ref[:, lanes] = dq
        dk_ref[lanes, :] = dk
        dv_ref[lanes, :] = dv
    dk_ref.send()
    dv_ref.send()
    projection_grads(
        core_ref[0], normed_ref, frames_ref, low_ref, dq_ref, dk_ref, dv_ref, heads_ref, theirs_ref, mine_ref
    )
    term_ref[...] = dot(dq_ref[...], proj_ref[0], 1, 1)
    dq_sum_ref[...] = column_sum(dq_ref[...].astype(f32))
    dv_sum_ref[...] = row_sums(dv_ref[...])


def cross_own_back(
    text_len, corpus_weight, core, cotangent, second, partial_normed, received, gain, out_proj, proj,
    q, k, v, weights, inverse, heads, normed, frames_in,
):
    rows, width = second.shape
    columns, half = k.shape
    vector = shaped((1, width), f32)
    grads = shaped((4, width // 2, half), f32)
    return call(
        cross_own_back_kernel,
        "cross_own_back",
        [
            shaped((rows, width), f32),
            shaped((rows, width), bf16),
            vector,
            vector,
            vector,
            shaped((rows, half), bf16),
            shaped((half, columns), bf16),
            shaped((half, columns), bf16),
            shaped((rows, width), f32),
            shaped((1, half), f32),
            shaped((8, half), f32),
            grads,
            grads,
        ],
        8 * rows * width * half + 4 * columns * width * half + 24 * rows * columns * half,
        (text_len, corpus_weight, core),
        received, partial_normed, second, cotangent, gain, (out_proj, 2, 1), q, k, v, inverse, heads,
        (weights, half // PAIR), (proj, 3, 0), normed, frames_in,
    )


def other_back_kernel(
    core_ref, low_in_ref, wo_ref, q_ref, k_ref, v_ref, inverse_ref, heads_ref, weights_ref, wq_ref,
    own_term_ref, first_ref, grad_second_ref, gain_ref,
    out_ref, self_q_ref, self_k_ref, self_v_ref, self_inverse_ref, self_heads_ref, self_weights_ref,
    proj_ref, hidden_ref, normed_ref,
    dk_ref, dv_ref, grad_first_ref, gain_grad_ref, shift_grad_ref, bias_grad_ref,
    term_ref, theirs_ref, mine_ref, self_gain_grad_ref, self_shift_grad_ref, dq_sum_ref, dv_sum_ref,
    low_ref, self_dq_ref, self_dk_ref, self_dv_ref,
):
    grad_heads = dot(low_in_ref[...], wo_ref[...], 1, 1).astype(bf16)
    pairs = q_ref.shape[1] // PAIR
    dqs = []
    for pair in range(pairs):
        lanes = lanes_of(pair)
        dq, dk, dv = pair_backward(
            q_ref[:, lanes], k_ref[:, lanes], v_ref[:, lanes], weights_ref, 2 * pair,
            inverse_ref[:, lanes], heads_ref[:, lanes], grad_heads[:, lanes],
        )
        dqs.append(dq)
        dk_ref[lanes, :] = dk
        dv_ref[lanes, :] = dv
    dk_ref.send()
    dv_ref.send()
    incoming = own_term_ref[...] + dot(jnp.concatenate(dqs, axis=1), wq_ref[...], 1, 1)
    unit, inverse = norm_unit(first_ref[...])
    gain_grad_ref[...] = column_sum(incoming * unit)
    shift_grad_ref[...] = column_sum(incoming)
    grad_first = grad_second_ref[...] + norm_backward(incoming, unit, inverse, gain_ref[1:2, :])
    grad_first_ref[...] = grad_first
    grad_first_ref.send()
    low = grad_first.astype(bf16)
    low_ref[...] = low
    bias_grad_ref[...] = column_sum(grad_first)

    grad_heads = dot(low, out_ref[0], 1, 1).astype(bf16)
    for pair in range(pairs):
        lanes = lanes_of(pair)
        dq, dk, dv = pair_backward(
            self_q_ref[:, lanes], self_k_ref[:, lanes], self_v_ref[:, lanes], self_weights_ref, 2 * pair,
            self_inverse_ref[:, lanes], self_heads_ref[:, lanes], grad_heads[:, lanes],
        )
        self_dq_ref[:, lanes] = dq
        self_dk_ref[lanes, :] = dk
        self_dv_ref[lanes, :] = dv
    projection_grads(
        core_ref[0], normed_ref, normed_ref, low_ref, self_dq_ref, self_dk_ref, self_dv_ref, self_heads_ref,
        theirs_ref, mine_ref,
    )
    incoming = dot(self_dq_ref[...], proj_ref[0], 1, 1) + (
        dot(self_dk_ref[...], proj_ref[1], 0, 1) + dot(self_dv_ref[...], proj_ref[2], 0, 1)
    )
    term_ref[...] = incoming
    term_ref.send()
    unit, _ = norm_unit(hidden_ref[...].astype(f32))
    self_gain_grad_ref[...] = column_sum(incoming * unit)
    self_shift_grad_ref[...] = column_sum(incoming)
    dq_sum_ref[...] = column_sum(self_dq_ref[...].astype(f32))
    dv_sum_ref[...] = row_sums(self_dv_ref[...])


def other_back(
    core, low, wo, wq, q, k, v, weights, inverse, heads, own_term, first, grad_second, gain,
    out_proj, proj, self_q, self_k, self_v, self_weights, self_inverse, self_heads, hidden, normed,
):
    rows, width = first.shape
    columns, half = k.shape
    vector = shaped((1, width), f32)
    grads = shaped((4, width // 2, half), f32)
    return call(
        other_back_kernel,
        "other_back",
        [
            shaped((half, columns), bf16),
            shaped((half, columns), bf16),
            shaped((rows, width), f32),
            vector,
            vector,
            vector,
            shaped((rows, width), f32),
            grads,
            grads,
            vector,
            vector,
            shaped((1, half), f32),
            shaped((8, half), f32),
            shaped((rows, width), bf16),
            shaped((rows, half), bf16),
            shaped((half, rows), bf16),
            shaped((half, rows), bf16),
        ],
        20 * rows * width * half + 24 * rows * (columns + rows) * half,
        (core,),
        low, wo, q, k, v, inverse, heads, (weights, half // PAIR), wq, own_term, first, grad_second, gain,
        (out_proj, 2, 0), self_q, self_k, self_v, self_inverse, self_heads, (self_weights, half // PAIR),
        (proj, 3), hidden, normed,
    )


def encoder_grad_kernel(dk0_ref, dv0_ref, dk1_ref, dv1_ref, proj_ref, wk1_ref, wv1_ref, out_ref):
    own = dot(dk0_ref[...], proj_ref[1], 0, 1) + dot(dv0_ref[...], proj_ref[2], 0, 1)
    other = dot(dk1_ref[...], wk1_ref[...], 0, 1) + dot(dv1_ref[...], wv1_ref[...], 0, 1)
    out_ref[:, 0, :] = own + other


def encoder_grad(dk0, dv0, dk1, dv1, proj, wk1, wv1, frames):
    half, padded = dk0.shape
    width = wk1.shape[0]
    grad_block = pl.BlockSpec((half, FRAME_BLOCK), lambda i: (0, i))
    weight = pl.BlockSpec(wk1.shape, lambda i: (0, 0))
    return pl.pallas_call(
        encoder_grad_kernel,
        grid=(padded // FRAME_BLOCK,),
        in_specs=[grad_block] * 4 + [pl.BlockSpec(proj.shape, lambda i: (0, 0, 0)), weight, weight],
        out_specs=pl.BlockSpec((FRAME_BLOCK, 1, width), lambda i: (i, 0, 0)),
        out_shape=shaped((frames, 1, width), f32),
        compiler_params=pltpu.CompilerParams(vmem_limit_bytes=VMEM_LIMIT),
        cost_estimate=pl.CostEstimate(
            flops=8 * half * padded * width, bytes_accessed=6 * frames * width, transcendentals=0
        ),
        name="encoder_grad",
    )(dk0, dv0, dk1, dv1, proj, wk1, wv1)


def swap(value):
    return lax.ppermute(value, "tensor", [(0, 1), (1, 0)])


def tie(*values):
    return lax.optimization_barrier(values)


class Scatter:
    def __init__(self, theirs, mine, turned=False):
        self.members = lax.axis_size("dp")
        self.bits = self.members.bit_length() - 1
        self.order = list(range(self.bits))
        if turned and self.bits > 2:
            self.order = [0] + self.order[2:] + [1]
        self.stage = 0
        self.theirs, self.mine = theirs, mine

    def launch(self):
        if self.stage == self.bits:
            return
        other = 1 << self.order[self.stage]
        self.received = lax.ppermute(self.theirs, "dp", [(i, i ^ other) for i in range(self.members)])

    def land(self):
        if self.stage == self.bits:
            return
        total = self.mine + self.received
        if self.stage == 0:
            lead = total.shape[:-2]
            self.lead = len(lead)
            cuts = self.bits - 1
            total = total.reshape(lead + (2,) * cuts + (total.shape[-2] >> cuts, total.shape[-1]))
        self.stage += 1
        if self.stage < self.bits:
            bit = self.order[self.stage]
            axis = self.lead + self.bits - 1 - bit
            side = (lax.axis_index("dp") >> bit) & 1
            self.mine = lax.dynamic_index_in_dim(total, side, axis, keepdims=True)
            self.theirs = lax.dynamic_index_in_dim(total, 1 - side, axis, keepdims=True)
        else:
            self.part = total.reshape(total.shape[: self.lead] + total.shape[-2:])

    def finish(self):
        while self.stage < self.bits:
            self.land()
            self.launch()
        return self.part


def place_kernel(moves, gathered_ref, *refs):
    outs, (held, in_sems, out_sems) = refs[:-3], refs[-3:]
    reads = [
        pltpu.make_async_copy(gathered_ref.at[i], held.at[i], in_sems.at[i]) for i in range(held.shape[0])
    ]
    for read in reads:
        read.start()
    writes = []
    for i, read in enumerate(reads):
        read.wait()
        for start, count, out, target in moves[i]:
            writes.append(
                pltpu.make_async_copy(
                    held.at[i, pl.ds(start, count)], outs[out].at[target], out_sems.at[len(writes)]
                )
            )
            writes[-1].start()
    for write in writes:
        write.wait()


def place(gathered, width, units):
    members, total, half = gathered.shape
    parts = members // 2
    rows = units // members
    count = width // members
    proj = shaped((3, width, half), f32)
    outs = [shaped((units, width), f32), shaped((width, units), f32), proj, proj, shaped((2, half, width), f32)]
    if count % 8 == 0:
        moves = []
        for i in range(members):
            q, c = i // 2, i % 2
            moves.append([])
            for j in range(2):
                columns = pl.ds(j * half, half)
                moves[i].append((j * rows, rows, 0, (pl.ds(c * width + q * rows, rows), columns)))
                columns = pl.ds(c * width + j * half, half)
                moves[i].append(((2 + j) * rows, rows, 1, (pl.ds(q * rows, rows), columns)))
            here = pl.ds(c * (width // 2) + q * count, count)
            for branch in range(2):
                start = 4 * rows + branch * 4 * count
                for a in range(3):
                    moves[i].append((start + a * count, count, 2 + branch, (a, here)))
                target = (1 - branch, pl.ds(q * count, count), pl.ds(c * half, half))
                moves[i].append((start + 3 * count, count, 4, target))
        anywhere = pl.BlockSpec(memory_space=pl.ANY)
        return pl.pallas_call(
            partial(place_kernel, moves),
            in_specs=[anywhere],
            out_specs=[anywhere] * len(outs),
            out_shape=outs,
            scratch_shapes=[
                pltpu.VMEM(gathered.shape, f32),
                pltpu.SemaphoreType.DMA((members,)),
                pltpu.SemaphoreType.DMA((sum(len(m) for m in moves),)),
            ],
            compiler_params=pltpu.CompilerParams(vmem_limit_bytes=VMEM_LIMIT),
            cost_estimate=pl.CostEstimate(flops=0, bytes_accessed=8 * gathered.size, transcendentals=0),
            name="place",
        )(gathered)
    split = gathered[:, : 4 * rows].reshape(parts, 2, 2, 2, rows, half)
    fc2 = split[:, :, 0].transpose(1, 0, 3, 2, 4).reshape(units, width)
    fc1 = split[:, :, 1].transpose(0, 3, 1, 2, 4).reshape(width, units)
    split = gathered[:, 4 * rows :].reshape(parts, 2, 2, 4, count, half)
    projections = split[:, :, :, :3].transpose(2, 3, 1, 0, 4, 5).reshape(2, 3, width, half)
    outputs = split[:, :, ::-1, 3].transpose(2, 0, 3, 1, 4).reshape(2, half, width)
    return fc2, fc1, projections[0], projections[1], outputs


def per_device(
    hidden,
    encoder,
    text_len,
    audio_len,
    corpus_weight,
    cotangent,
    norm_gain,
    norm_bias,
    self_proj,
    self_bias,
    cross_proj,
    cross_bias,
    out_proj,
    out_bias,
    fc1_weight,
    fc1_bias,
    fc2_weight,
    fc2_bias,
):
    sequences, frames, width = encoder.shape
    members = lax.axis_size("dp")
    me = lax.axis_index("dp")
    half = self_proj.shape[2]
    padded = -(-frames // FRAME_BLOCK) * FRAME_BLOCK
    core = (me & 1).astype(jnp.int32).reshape(1)

    cross_rows = jnp.concatenate(
        [cross_proj.reshape(-1, half), out_proj[1][:, :half], out_proj[1][:, half:]], axis=0
    )
    count = cross_rows.shape[0] // members
    part = swap(lax.dynamic_slice_in_dim(cross_rows, me * count, count, 0).astype(f32))
    hidden_in, part = tie(hidden, part)
    gathered = lax.all_gather(part, "dp", axis=0, tiled=True)

    normed_self, q_self, k_self, v_self, weights_self, inverse_self, heads_self, partial_self = self_forward(
        text_len, hidden_in, norm_gain, norm_bias, self_proj, self_bias, out_proj
    )
    received = swap(partial_self)
    other_bias = swap(cross_bias)

    frames_in = jnp.pad(encoder.reshape(frames, width), ((0, padded - frames), (0, 0)))
    k_own = dot(frames_in, cross_proj[1], 1, 0).astype(bf16)
    v_own = (dot(frames_in, cross_proj[2], 1, 0) + cross_bias[1]).astype(bf16)
    received, k_own, v_own = tie(received, k_own, v_own)
    first, normed_cross, q_own, weights_own, inverse_own, heads_own, term_own = cross_own(
        audio_len, hidden, partial_self, received, out_bias, norm_gain, norm_bias,
        cross_proj, cross_bias, k_own, v_own, out_proj,
    )
    gathered, normed_cross = tie(gathered, normed_cross)
    (
        q_other, k_other, v_other, weights_other, inverse_other, heads_other,
        wq_other, wk_other, wv_other, wo_other,
        second, partial_normed, fc2_theirs, fc1_theirs, fc2_mine, fc1_mine, partial_mlp,
        fc1_bias_grad, fc2_bias_grad,
    ) = late_forward(
        audio_len, text_len, corpus_weight, core, gathered, normed_cross, frames_in, other_bias, term_own, first,
        out_bias, norm_gain, norm_bias, fc1_weight, fc1_bias.reshape(1, -1), cotangent, fc2_weight,
    )
    received = swap(partial_normed)
    fc2_share = Scatter(fc2_theirs, fc2_mine)
    fc1_share = Scatter(fc1_theirs, fc1_mine, turned=True)
    fc2_share.launch()
    fc1_share.launch()
    fc2_share.land()
    fc2_share.launch()
    fc1_share.land()
    fc1_share.launch()

    (
        grad_second, second_low, gain_mlp, shift_mlp, bias_cross, dq_own, dk_own, dv_own, back_own,
        dq_cross_sum, dv_cross_sum, cross_theirs, cross_mine,
    ) = cross_own_back(
        text_len, corpus_weight, core, cotangent, second, partial_normed, received, norm_gain,
        out_proj, cross_proj, q_own, k_own, v_own, weights_own, inverse_own, heads_own, normed_cross, frames_in,
    )
    cross_theirs, fc2_share.received, fc1_share.received = tie(
        cross_theirs, fc2_share.received, fc1_share.received
    )
    cross_share = Scatter(cross_theirs, cross_mine)
    cross_share.launch()
    fc2_share.land()
    fc1_share.land()
    fc2_share.launch()
    fc1_share.launch()
    cross_share.received, fc2_share.theirs, fc1_share.theirs = tie(
        cross_share.received, fc2_share.theirs, fc1_share.theirs
    )
    cross_share.land()
    second_low, cross_share.theirs = tie(second_low, cross_share.theirs)
    cross_share.launch()

    (
        dk_other, dv_other, grad_first, gain_cross, shift_cross, bias_self, partial_normed,
        self_theirs, self_mine, gain_self, shift_self, dq_self_sum, dv_self_sum, *_,
    ) = other_back(
        core, second_low, wo_other, wq_other, q_other, k_other, v_other, weights_other, inverse_other, heads_other,
        back_own, first, grad_second, norm_gain, out_proj, self_proj, q_self, k_self, v_self, weights_self,
        inverse_self, heads_self, hidden, normed_self,
    )
    self_theirs, cross_share.received, fc1_share.received, fc2_share.received = tie(
        self_theirs, cross_share.received, fc1_share.received, fc2_share.received
    )
    self_share = Scatter(self_theirs, self_mine)
    self_share.launch()
    fc2_share.land()
    fc2_share.launch()
    cross_share.received, fc2_share.theirs = tie(cross_share.received, fc2_share.theirs)
    cross_share.land()
    self_share.land()
    self_share.theirs, cross_share.theirs, partial_normed, dk_own = tie(
        self_share.theirs, cross_share.theirs, partial_normed, dk_own
    )
    self_share.launch()
    cross_share.launch()
    received = swap(partial_normed)
    grad_encoder = encoder_grad(
        dk_own, dv_own, dk_other, dv_other, cross_proj, wk_other, wv_other, frames
    ).reshape(encoder.shape)
    cross_share.received, fc1_share.received, partial_normed, grad_encoder = tie(
        cross_share.received, fc1_share.received, partial_normed, grad_encoder
    )
    cross_share.land()
    fc1_share.land()
    cross_share.launch()
    self_share.received, cross_share.theirs = tie(self_share.received, cross_share.theirs)
    self_share.land()
    self_share.launch()
    fc1_share.theirs, self_share.theirs, hidden = tie(fc1_share.theirs, self_share.theirs, hidden)
    fc1_share.launch()
    cross_share.received, fc2_share.received, fc1_share.received, grad_encoder, _ = tie(
        cross_share.received, fc2_share.received, fc1_share.received, grad_encoder, self_share.theirs
    )
    cross_part = cross_share.finish()
    fc2_part = fc2_share.finish()
    fc1_part = fc1_share.finish()

    most = [fc2_part[:, :half], fc2_part[:, half:], fc1_part[:, :half], fc1_part[:, half:]]
    most = jnp.concatenate([item.reshape(-1, half) for item in (*most, cross_part)], axis=0)
    unit_self, root_self = norm_unit(hidden.astype(f32))
    grad_hidden = (
        grad_first + norm_backward(partial_normed + received, unit_self, root_self, norm_gain[0])
    ).astype(bf16)
    grad_hidden, most, self_share.received = tie(grad_hidden, most, self_share.received)
    self_part = self_share.finish()
    every = jnp.concatenate([most, self_part.reshape(-1, half)], axis=0)

    small = (
        gain_self,
        shift_self,
        gain_cross,
        gain_mlp,
        shift_cross,
        shift_mlp,
        dq_self_sum,
        dv_self_sum,
        dq_cross_sum,
        dv_cross_sum,
        bias_self,
        bias_cross,
        fc1_bias_grad,
        fc2_bias_grad,
    )
    *small, partial_mlp, every = tie(*small, partial_mlp, every)
    every = lax.all_gather(every, "dp", axis=0, tiled=False)
    small[7] = small[7][0:1]
    small[9] = small[9][0:1]
    norm_self = jnp.concatenate(small[0:2], axis=0)
    small = [norm_self + swap(norm_self)] + small[2:]
    flat = jnp.concatenate([item.reshape(-1, half) for item in small], axis=0)
    for bit in range(members.bit_length() - 1):
        flat = flat + lax.ppermute(flat, "dp", [(i, i ^ (1 << bit)) for i in range(members)])
    received_mlp = swap(partial_mlp)
    result = (second + (partial_mlp + received_mlp) + fc2_bias).astype(bf16)
    fc2_weight_grad, fc1_weight_grad, cross_proj_grad, self_proj_grad, out_proj_grad = place(
        every, width, fc2_weight.shape[0]
    )
    small_out = []
    offset = 0
    for item in small:
        count = item.size // half
        small_out.append(flat[offset : offset + count].reshape(item.shape))
        offset += count
    (
        norm_self, gain_cross, gain_mlp, shift_cross, shift_mlp, dq_self_sum, dv_self_sum, dq_cross_sum,
        dv_cross_sum, bias_self, bias_cross, fc1_bias_grad, fc2_bias_grad,
    ) = small_out
    return (
        result,
        grad_hidden,
        grad_encoder,
        jnp.concatenate([norm_self[0:1], gain_cross, gain_mlp], axis=0),
        jnp.concatenate([norm_self[1:2], shift_cross, shift_mlp], axis=0),
        self_proj_grad,
        jnp.concatenate([dq_self_sum, dv_self_sum], axis=0),
        cross_proj_grad,
        jnp.concatenate([dq_cross_sum, dv_cross_sum], axis=0),
        out_proj_grad,
        jnp.concatenate([bias_self, bias_cross], axis=0),
        fc1_weight_grad,
        fc1_bias_grad.reshape(-1),
        fc2_weight_grad,
        fc2_bias_grad.reshape(-1),
    )


def solution(mesh):
    placed = (
        P("dp", None),
        P("dp", None, None),
        P("dp"),
        P("dp"),
        P("dp"),
        P("dp", None),
        P(),
        P(),
        P(None, None, "tensor"),
        P(None, "tensor"),
        P(None, None, "tensor"),
        P(None, "tensor"),
        P(None, "tensor", None),
        P(),
        P(None, "tensor"),
        P("tensor"),
        P("tensor", None),
        P(),
    )
    return jax.shard_map(
        per_device,
        mesh=mesh,
        in_specs=placed,
        out_specs=(
            P("dp", None),
            P("dp", None),
            P("dp", None, None),
            P(),
            P(),
            P(None, None, "tensor"),
            P(None, "tensor"),
            P(None, None, "tensor"),
            P(None, "tensor"),
            P(None, "tensor", None),
            P(),
            P(None, "tensor"),
            P("tensor"),
            P("tensor", None),
            P(),
        ),
        check_vma=False,
    )
```

```python
from functools import partial

import jax
import jax.numpy as jnp
from jax import lax
from jax.experimental import pallas as pl
from jax.experimental.pallas import tpu as pltpu
from jax.sharding import PartitionSpec as P

HEAD_DIM = 64
SCALE = HEAD_DIM ** (-0.5)
PAIR = 2 * HEAD_DIM
FF_BLOCK = 768
FRAME_BLOCK = 256
VMEM_LIMIT = 63 * 1024 * 1024 + 512 * 1024
COST_SHARE = 64
epsilon = 1e-05
masked_value = -1e30
f32 = jnp.float32
bf16 = jnp.bfloat16


def dot(a, b, ca, cb):
    return lax.dot_general(a, b, (((ca,), (cb,)), ((), ())), preferred_element_type=f32)


def shaped(shape, dtype):
    return jax.ShapeDtypeStruct(shape, dtype)


class Source:
    def __init__(self, ref, held, sems, first_sem, pieces):
        self.held, self.shape, self.dtype = held, held.shape, held.dtype
        self.size = held.shape[0] // pieces
        self.ref, self.sems, self.first_sem = ref, sems, first_sem
        self.copies = [None] * pieces
        self.pending = [True] * pieces

    def fetch(self, *pieces):
        for piece in pieces or range(len(self.copies)):
            if self.copies[piece] is None:
                here = pl.ds(piece * self.size, self.size)
                self.copies[piece] = pltpu.make_async_copy(
                    self.ref.at[here], self.held.at[here], self.sems.at[self.first_sem + piece]
                )
                self.copies[piece].start()

    def wait(self, piece):
        if self.pending[piece]:
            self.fetch(piece)
            self.pending[piece] = False
            self.copies[piece].wait()

    def __getitem__(self, index):
        if len(self.copies) > 1 and isinstance(index, int):
            self.wait(index // self.size)
        else:
            for piece in range(len(self.copies)):
                self.wait(piece)
        return self.held[index]


class Sink:
    def __init__(self, ref, held, sems, first_sem, pieces):
        self.held, self.shape, self.dtype = held, held.shape, held.dtype
        self.size = held.shape[0] // pieces
        self.copies = []
        self.sent = []
        for i in range(pieces):
            here = pl.ds(i * self.size, self.size)
            self.copies.append(pltpu.make_async_copy(held.at[here], ref.at[here], sems.at[first_sem + i]))
            self.sent.append(False)

    def __getitem__(self, index):
        return self.held[index]

    def __setitem__(self, index, value):
        self.held[index] = value

    def send(self, piece=0):
        self.sent[piece] = True
        self.copies[piece].start()


class Resident:
    def __init__(self, value):
        self.value = value

    def __getitem__(self, index):
        return self.value[index]

    def __setitem__(self, index, value):
        self.value[index] = value


def call(kernel, name, out_shape, flops, scalars, *arrays):
    arrays = [a if isinstance(a, tuple) else (a, 1) for a in arrays]
    used = [a[2:] for a in arrays]
    arrays = [a[:2] for a in arrays]
    outs = [o if isinstance(o, tuple) else (o, 1) for o in out_shape]
    in_stays = [isinstance(a, Resident) for a, _ in arrays]
    out_stays = [isinstance(o, Resident) for o, _ in outs]
    in_pieces = [0 if stays else pieces for (_, pieces), stays in zip(arrays, in_stays)]
    out_pieces = [0 if stays else pieces for (_, pieces), stays in zip(outs, out_stays)]
    arrays = [a.value if stays else a for (a, _), stays in zip(arrays, in_stays)]
    outs = [o.value if stays else o for (o, _), stays in zip(outs, out_stays)]
    moved = sum(a.size * a.dtype.itemsize for a in (*arrays, *outs))

    def body(*refs):
        refs = list(refs)
        scalar_refs = [refs.pop(0) for _ in scalars]
        in_refs = [refs.pop(0) for _ in arrays]
        out_refs = [refs.pop(0) for _ in outs]
        in_held = [None if stays else refs.pop(0) for stays in in_stays]
        out_held = [None if stays else refs.pop(0) for stays in out_stays]
        in_sems, out_sems = refs
        sources = []
        for i, (ref, held) in enumerate(zip(in_refs, in_held)):
            if in_stays[i]:
                sources.append(Resident(ref))
            else:
                sources.append(Source(ref, held, in_sems, sum(in_pieces[:i]), in_pieces[i]))
        sinks = []
        for i, (ref, held) in enumerate(zip(out_refs, out_held)):
            if out_stays[i]:
                sinks.append(Resident(ref))
            else:
                sinks.append(Sink(ref, held, out_sems, sum(out_pieces[:i]), out_pieces[i]))
        moving = [source for source in sources if isinstance(source, Source)]
        leaving = [sink for sink in sinks if isinstance(sink, Sink)]
        for source, only in zip(sources, used):
            if isinstance(source, Source):
                source.fetch(*only)
        kernel(*scalar_refs, *sources, *sinks)
        for source in moving:
            for piece in range(len(source.copies)):
                if source.copies[piece] is not None:
                    source.wait(piece)
        for sink in leaving:
            for piece, sent in enumerate(sink.sent):
                if not sent:
                    sink.send(piece)
        for sink in leaving:
            for copy in sink.copies:
                copy.wait()

    anywhere = pl.BlockSpec(memory_space=pl.ANY)
    here = pl.BlockSpec(memory_space=pltpu.VMEM)
    scratch = [pltpu.VMEM(a.shape, a.dtype) for a, stays in zip(arrays, in_stays) if not stays]
    scratch += [pltpu.VMEM(o.shape, o.dtype) for o, stays in zip(outs, out_stays) if not stays]
    return pl.pallas_call(
        body,
        in_specs=[pl.BlockSpec(memory_space=pltpu.SMEM)] * len(scalars)
        + [here if stays else anywhere for stays in in_stays],
        out_specs=[here if stays else anywhere for stays in out_stays],
        out_shape=outs,
        scratch_shapes=scratch
        + [pltpu.SemaphoreType.DMA((sum(in_pieces),)), pltpu.SemaphoreType.DMA((sum(out_pieces),))],
        compiler_params=pltpu.CompilerParams(vmem_limit_bytes=VMEM_LIMIT),
        cost_estimate=pl.CostEstimate(
            flops=flops // COST_SHARE, bytes_accessed=moved // COST_SHARE, transcendentals=0
        ),
        name=name,
    )(*scalars, *arrays)


def lanes_of(pair):
    return slice(pair * PAIR, (pair + 1) * PAIR)


def add_up(terms):
    total = terms[0]
    for term in terms[1:]:
        total = total + term
    return total


def norm_unit(values):
    centered = values - jnp.mean(values, axis=-1, keepdims=True)
    inverse = lax.rsqrt(jnp.mean(centered * centered, axis=-1, keepdims=True) + epsilon)
    return centered * inverse, inverse


def norm_backward(incoming, unit, inverse, gain):
    scaled = incoming * gain
    scaled_mean = jnp.mean(scaled, axis=-1, keepdims=True)
    along_unit = jnp.mean(scaled * unit, axis=-1, keepdims=True)
    return inverse * (scaled - scaled_mean - unit * along_unit)


def column_sum(values):
    return jnp.sum(values, axis=0, keepdims=True)


def live_gradient(cotangent, text_len, corpus_weight):
    places = lax.broadcasted_iota(jnp.int32, (cotangent.shape[0], 1), 0)
    live = jnp.where(places < text_len, corpus_weight, 0.0)
    return cotangent.astype(f32) * live


def lane_masks(rows):
    return lax.broadcasted_iota(jnp.int32, (rows, PAIR), 1) < HEAD_DIM


def pair_forward(length, causal, q, k, v, weights_ref, start):
    rows, columns = q.shape[0], k.shape[0]
    first_lanes = lane_masks(rows)
    if causal:
        places = lax.broadcasted_iota(jnp.int32, (rows, columns), 1)
        allowed = (places < length) & (places <= lax.broadcasted_iota(jnp.int32, (rows, columns), 0))
    else:
        places = lax.broadcasted_iota(jnp.int32, (1, columns), 1)
        shift = jnp.where(places < length, 0.0, masked_value)
    scores = []
    for head in range(2):
        mine = first_lanes if head == 0 else jnp.logical_not(first_lanes)
        raw = dot(jnp.where(mine, q, jnp.zeros_like(q)), k, 1, 1)
        scores.append(jnp.where(allowed, raw, masked_value) if causal else raw + shift)
    inverses = []
    for head in range(2):
        largest = jnp.max(scores[head], axis=-1, keepdims=True)
        weights = jnp.exp(scores[head] - largest)
        inverses.append(1.0 / jnp.sum(weights, axis=-1, keepdims=True))
        weights_ref[start + head] = weights.astype(bf16)
    mixed = [dot(weights_ref[start + head], v, 1, 0) for head in range(2)]
    inverse = jnp.where(first_lanes, inverses[0], inverses[1])
    return (jnp.where(first_lanes, mixed[0], mixed[1]) * inverse).astype(bf16), inverse


def pair_backward(q, k, v, weights_ref, start, inverse, heads, grad_heads):
    first_lanes = lane_masks(q.shape[0])
    grad = (grad_heads.astype(f32) * inverse).astype(bf16)
    along = grad.astype(f32) * heads.astype(f32)
    dq = []
    dk = None
    dv = None
    for head in range(2):
        mine = first_lanes if head == 0 else jnp.logical_not(first_lanes)
        grad_one = jnp.where(mine, grad, jnp.zeros_like(grad))
        q_one = jnp.where(mine, q, jnp.zeros_like(q))
        row_terms = jnp.sum(jnp.where(mine, along, 0.0), axis=-1, keepdims=True)
        weights = weights_ref[start + head]
        grad_probs = dot(grad_one, v, 1, 1)
        grad_scores = (weights.astype(f32) * (grad_probs - row_terms)).astype(bf16)
        dv_one = dot(grad_one, weights, 0, 0)
        dk_one = dot(q_one, grad_scores, 0, 0)
        dq.append(dot(grad_scores, k, 1, 0))
        dk = dk_one if dk is None else dk + dk_one
        dv = dv_one if dv is None else dv + dv_one
    dq = (jnp.where(first_lanes, dq[0], dq[1]) * SCALE).astype(bf16)
    return dq, dk.astype(bf16), dv.astype(bf16)


def row_sums(values):
    return dot(jnp.ones((8, values.shape[1]), bf16), values, 1, 1)


def self_forward_kernel(
    length_ref, hidden_ref, gain_ref, shift_ref, proj_ref, bias_ref, out_ref,
    normed_ref, q_ref, k_ref, v_ref, weights_ref, inverse_ref, heads_ref, partial_ref,
):
    unit, _ = norm_unit(hidden_ref[...].astype(f32))
    normed = (unit * gain_ref[0:1, :] + shift_ref[0:1, :]).astype(bf16)
    normed_ref[...] = normed
    normed_ref.send()
    q_ref[...] = ((dot(normed, proj_ref[0], 1, 0) + bias_ref[0:1]) * SCALE).astype(bf16)
    k_ref[...] = dot(normed, proj_ref[1], 1, 0).astype(bf16)
    v_ref[...] = (dot(normed, proj_ref[2], 1, 0) + bias_ref[1:2]).astype(bf16)
    q_ref.send()
    k_ref.send()
    v_ref.send()
    for pair in range(q_ref.shape[1] // PAIR):
        lanes = lanes_of(pair)
        heads, inverse = pair_forward(
            length_ref[0], True, q_ref[:, lanes], k_ref[:, lanes], v_ref[:, lanes], weights_ref, 2 * pair
        )
        weights_ref.send(pair)
        heads_ref[:, lanes] = heads
        inverse_ref[:, lanes] = inverse
    heads_ref.send()
    inverse_ref.send()
    partial_ref[...] = dot(heads_ref[...], out_ref[0], 1, 0)


def self_forward(text_len, hidden, gain, shift, proj, bias, out_proj):
    rows, width = hidden.shape
    half = proj.shape[2]
    return call(
        self_forward_kernel,
        "self_forward",
        [
            shaped((rows, width), bf16),
            shaped((rows, half), bf16),
            shaped((rows, half), bf16),
            shaped((rows, half), bf16),
            (shaped((half // HEAD_DIM, rows, rows), bf16), half // PAIR),
            shaped((rows, half), f32),
            shaped((rows, half), bf16),
            shaped((rows, width), f32),
        ],
        8 * rows * width * half + 12 * rows * rows * half,
        (text_len,),
        hidden, gain, shift, (proj, 3), bias, (out_proj, 2, 0),
    )


def cross_own_kernel(
    length_ref, received_ref, partial_ref, hidden_ref, out_bias_ref, gain_ref, shift_ref,
    proj_ref, bias_ref, k_ref, v_ref, out_ref,
    first_ref, normed_ref, q_ref, weights_ref, inverse_ref, heads_ref, term_ref,
):
    first = hidden_ref[...].astype(f32) + (partial_ref[...] + received_ref[...]) + out_bias_ref[0:1, :]
    first_ref[...] = first
    first_ref.send()
    unit, _ = norm_unit(first)
    normed = (unit * gain_ref[1:2, :] + shift_ref[1:2, :]).astype(bf16)
    normed_ref[...] = normed
    normed_ref.send()
    q_ref[...] = ((dot(normed, proj_ref[0], 1, 0) + bias_ref[0:1]) * SCALE).astype(bf16)
    q_ref.send()
    for pair in range(q_ref.shape[1] // PAIR):
        lanes = lanes_of(pair)
        heads, inverse = pair_forward(
            length_ref[0], False, q_ref[:, lanes], k_ref[:, lanes], v_ref[:, lanes], weights_ref, 2 * pair
        )
        weights_ref.send(pair)
        heads_ref[:, lanes] = heads
        inverse_ref[:, lanes] = inverse
    heads_ref.send()
    inverse_ref.send()
    term_ref[...] = dot(heads_ref[...], out_ref[1], 1, 0)


def cross_own(audio_len, hidden, partial_self, received, out_bias, gain, shift, proj, bias, k, v, out_proj):
    rows, width = hidden.shape
    columns, half = k.shape
    return call(
        cross_own_kernel,
        "cross_own",
        [
            shaped((rows, width), f32),
            shaped((rows, width), bf16),
            shaped((rows, half), bf16),
            (shaped((half // HEAD_DIM, rows, columns), bf16), half // PAIR),
            shaped((rows, half), f32),
            shaped((rows, half), bf16),
            shaped((rows, width), f32),
        ],
        4 * rows * width * half + 12 * rows * columns * half,
        (audio_len,),
        received, partial_self, hidden, out_bias, gain, shift, (proj, 3, 0), bias, k, v,
        (out_proj, 2, 1),
    )


def error_function(x):
    x = jnp.clip(x, -4.0, 4.0)
    square = x * x
    top = jnp.full_like(x, -2.72614225801306e-10)
    for c in (
        2.77068142495902e-08,
        -2.10102402082508e-06,
        -5.69250639462346e-05,
        -7.34990630326855e-04,
        -2.95459980854025e-03,
        -1.60960333262415e-02,
    ):
        top = top * square + c
    bottom = jnp.full_like(x, -1.45660718464996e-05)
    for c in (-2.13374055278905e-04, -1.68282697438203e-03, -7.37332916720468e-03, -1.42647390514189e-02):
        bottom = bottom * square + c
    return x * top / bottom


def late_forward_kernel(
    audio_ref, text_ref, weight_ref, core_ref, gathered_ref, normed_ref, frames_ref, bias_ref, own_ref, first_ref,
    out_bias_ref, gain_ref, shift_ref, fc1_ref, fc1_bias_ref, cotangent_ref, fc2_ref,
    q_ref, k_ref, v_ref, weights_ref, inverse_ref, heads_ref, wq_ref, wk_ref, wv_ref, wo_ref,
    second_ref, normed_grad_ref, fc2_theirs_ref, fc1_theirs_ref, fc2_mine_ref, fc1_mine_ref, mlp_ref,
    fc1_bias_grad_ref, fc2_bias_grad_ref,
):
    width, half = wq_ref.shape
    for i, ref in enumerate((wq_ref, wk_ref, wv_ref)):
        ref[...] = gathered_ref[i * width : (i + 1) * width, :].astype(bf16)
        ref.send()
    for i in range(width // half):
        start = 3 * width + i * half
        wo_ref[:, i * half : (i + 1) * half] = gathered_ref[start : start + half, :].astype(bf16)
    wo_ref.send()
    q_ref[...] = ((dot(normed_ref[...], wq_ref[...], 1, 0) + bias_ref[0:1]) * SCALE).astype(bf16)
    k_ref[...] = dot(frames_ref[...], wk_ref[...], 1, 0).astype(bf16)
    v_ref[...] = (dot(frames_ref[...], wv_ref[...], 1, 0) + bias_ref[1:2]).astype(bf16)
    q_ref.send()
    k_ref.send()
    v_ref.send()
    for pair in range(half // PAIR):
        lanes = lanes_of(pair)
        heads, inverse = pair_forward(
            audio_ref[0], False, q_ref[:, lanes], k_ref[:, lanes], v_ref[:, lanes], weights_ref, 2 * pair
        )
        weights_ref.send(pair)
        heads_ref[:, lanes] = heads
        inverse_ref[:, lanes] = inverse
    heads_ref.send()
    inverse_ref.send()
    other = dot(heads_ref[...], wo_ref[...], 1, 0)

    second = first_ref[...] + (own_ref[...] + other) + out_bias_ref[1:2, :]
    second_ref[...] = second
    second_ref.send()
    unit, _ = norm_unit(second)
    normed = (unit * gain_ref[2:3, :] + shift_ref[2:3, :]).astype(bf16)
    grad_y = live_gradient(cotangent_ref[...], text_ref[0], weight_ref[0])
    fc2_bias_grad_ref[...] = column_sum(grad_y)
    grad = grad_y.astype(bf16)
    part = fc2_theirs_ref.shape[0]
    for turn, (fc2_out, fc1_out) in enumerate(((fc2_theirs_ref, fc1_theirs_ref), (fc2_mine_ref, fc1_mine_ref))):
        side = 1 - core_ref[0] if turn == 0 else core_ref[0]
        for start in range(0, part, FF_BLOCK):
            here = pl.ds(pl.multiple_of(side * part + start, FF_BLOCK), FF_BLOCK)
            there = slice(start, start + FF_BLOCK)
            fc1 = fc1_ref[:, here]
            pre = dot(normed, fc1, 1, 0) + fc1_bias_ref[:, here]
            cdf = 0.5 * (1.0 + error_function(pre * 0.7071067811865476))
            inner = (pre * cdf).astype(bf16)
            slope = cdf + pre * (0.3989422804014327 * jnp.exp(-0.5 * pre * pre))
            fc2 = fc2_ref[here, :]
            grad_pre = (dot(grad, fc2, 1, 1) * slope).astype(bf16)
            fc1_bias_grad_ref[:, here] = column_sum(grad_pre.astype(f32))
            fc2_out[there, :] = dot(inner, grad, 0, 0)
            fc1_out[:, there] = dot(normed, grad_pre, 0, 0)
            mlp_term = dot(inner, fc2, 1, 0)
            normed_term = dot(grad_pre, fc1, 1, 1)
            if turn == 0 and start == 0:
                mlp_ref[...] = mlp_term
                normed_grad_ref[...] = normed_term
            else:
                mlp_ref[...] += mlp_term
                normed_grad_ref[...] += normed_term
        fc2_out.send()
        fc1_out.send()


def late_forward(
    audio_len, text_len, corpus_weight, core, gathered, normed, frames_in, bias, own, first, out_bias, gain, shift,
    fc1, fc1_bias, cotangent, fc2,
):
    rows, width = first.shape
    units = fc2.shape[0]
    columns = frames_in.shape[0]
    half = gathered.shape[1]
    full = shaped((rows, width), f32)
    proj = shaped((width, half), bf16)
    return call(
        late_forward_kernel,
        "late_forward",
        [
            shaped((rows, half), bf16),
            shaped((columns, half), bf16),
            shaped((columns, half), bf16),
            (shaped((half // HEAD_DIM, rows, columns), bf16), half // PAIR),
            shaped((rows, half), f32),
            shaped((rows, half), bf16),
            proj,
            proj,
            proj,
            shaped((half, width), bf16),
            full,
            full,
            shaped((units // 2, width), f32),
            shaped((width, units // 2), f32),
            shaped((units // 2, width), f32),
            shaped((width, units // 2), f32),
            full,
            shaped((1, units), f32),
            shaped((1, width), f32),
        ],
        4 * rows * width * half + 4 * columns * width * half + 12 * rows * (columns * half + width * units),
        (audio_len, text_len, corpus_weight, core),
        gathered, normed, frames_in, bias, own, first, out_bias, gain, shift, fc1, fc1_bias, cotangent, fc2,
    )


def projection_grads(core, normed, source, low, dq, dk, dv, heads, theirs_ref, mine_ref):
    part = theirs_ref.shape[1]
    for out_ref, side in ((theirs_ref, 1 - core), (mine_ref, core)):
        here = pl.ds(pl.multiple_of(side * part, PAIR), part)
        piece = source[:, here]
        out_ref[0] = dot(normed[:, here], dq[...], 0, 0)
        out_ref[1] = dot(piece, dk[...], 0, 1)
        out_ref[2] = dot(piece, dv[...], 0, 1)
        out_ref[3] = dot(heads[...], low[:, here], 0, 0)
        out_ref.send()


def cross_own_back_kernel(
    length_ref, weight_ref, core_ref, received_ref, partial_ref, second_ref, cotangent_ref, gain_ref,
    out_ref, q_ref, k_ref, v_ref, inverse_ref, heads_ref, weights_ref, proj_ref, normed_ref, frames_ref,
    grad_second_ref, low_ref, gain_grad_ref, shift_grad_ref, bias_grad_ref,
    dq_ref, dk_ref, dv_ref, term_ref, dq_sum_ref, dv_sum_ref, theirs_ref, mine_ref,
):
    incoming = partial_ref[...] + received_ref[...]
    unit, inverse = norm_unit(second_ref[...])
    gain_grad_ref[...] = column_sum(incoming * unit)
    shift_grad_ref[...] = column_sum(incoming)
    grad_second = live_gradient(cotangent_ref[...], length_ref[0], weight_ref[0]) + norm_backward(
        incoming, unit, inverse, gain_ref[2:3, :]
    )
    grad_second_ref[...] = grad_second
    grad_second_ref.send()
    low = grad_second.astype(bf16)
    low_ref[...] = low
    low_ref.send()
    bias_grad_ref[...] = column_sum(grad_second)
    grad_heads = dot(low, out_ref[1], 1, 1).astype(bf16)
    for pair in range(q_ref.shape[1] // PAIR):
        lanes = lanes_of(pair)
        dq, dk, dv = pair_backward(
            q_ref[:, lanes], k_ref[:, lanes], v_ref[:, lanes], weights_ref, 2 * pair,
            inverse_ref[:, lanes], heads_ref[:, lanes], grad_heads[:, lanes],
        )
        dq_ref[:, lanes] = dq
        dk_ref[lanes, :] = dk
        dv_ref[lanes, :] = dv
    dk_ref.send()
    dv_ref.send()
    projection_grads(
        core_ref[0], normed_ref, frames_ref, low_ref, dq_ref, dk_ref, dv_ref, heads_ref, theirs_ref, mine_ref
    )
    term_ref[...] = dot(dq_ref[...], proj_ref[0], 1, 1)
    dq_sum_ref[...] = column_sum(dq_ref[...].astype(f32))
    dv_sum_ref[...] = row_sums(dv_ref[...])


def cross_own_back(
    text_len, corpus_weight, core, cotangent, second, partial_normed, received, gain, out_proj, proj,
    q, k, v, weights, inverse, heads, normed, frames_in,
):
    rows, width = second.shape
    columns, half = k.shape
    vector = shaped((1, width), f32)
    grads = shaped((4, width // 2, half), f32)
    return call(
        cross_own_back_kernel,
        "cross_own_back",
        [
            shaped((rows, width), f32),
            shaped((rows, width), bf16),
            vector,
            vector,
            vector,
            shaped((rows, half), bf16),
            shaped((half, columns), bf16),
            shaped((half, columns), bf16),
            shaped((rows, width), f32),
            shaped((1, half), f32),
            shaped((8, half), f32),
            grads,
            grads,
        ],
        8 * rows * width * half + 4 * columns * width * half + 24 * rows * columns * half,
        (text_len, corpus_weight, core),
        received, partial_normed, second, cotangent, gain, (out_proj, 2, 1), q, k, v, inverse, heads,
        (weights, half // PAIR), (proj, 3, 0), normed, frames_in,
    )


def other_back_kernel(
    core_ref, low_in_ref, wo_ref, q_ref, k_ref, v_ref, inverse_ref, heads_ref, weights_ref, wq_ref,
    own_term_ref, first_ref, grad_second_ref, gain_ref,
    out_ref, self_q_ref, self_k_ref, self_v_ref, self_inverse_ref, self_heads_ref, self_weights_ref,
    proj_ref, hidden_ref, normed_ref,
    dk_ref, dv_ref, grad_first_ref, gain_grad_ref, shift_grad_ref, bias_grad_ref,
    term_ref, theirs_ref, mine_ref, self_gain_grad_ref, self_shift_grad_ref, dq_sum_ref, dv_sum_ref,
    low_ref, self_dq_ref, self_dk_ref, self_dv_ref,
):
    grad_heads = dot(low_in_ref[...], wo_ref[...], 1, 1).astype(bf16)
    pairs = q_ref.shape[1] // PAIR
    dqs = []
    for pair in range(pairs):
        lanes = lanes_of(pair)
        dq, dk, dv = pair_backward(
            q_ref[:, lanes], k_ref[:, lanes], v_ref[:, lanes], weights_ref, 2 * pair,
            inverse_ref[:, lanes], heads_ref[:, lanes], grad_heads[:, lanes],
        )
        dqs.append(dq)
        dk_ref[lanes, :] = dk
        dv_ref[lanes, :] = dv
    dk_ref.send()
    dv_ref.send()
    incoming = own_term_ref[...] + dot(jnp.concatenate(dqs, axis=1), wq_ref[...], 1, 1)
    unit, inverse = norm_unit(first_ref[...])
    gain_grad_ref[...] = column_sum(incoming * unit)
    shift_grad_ref[...] = column_sum(incoming)
    grad_first = grad_second_ref[...] + norm_backward(incoming, unit, inverse, gain_ref[1:2, :])
    grad_first_ref[...] = grad_first
    grad_first_ref.send()
    low = grad_first.astype(bf16)
    low_ref[...] = low
    bias_grad_ref[...] = column_sum(grad_first)

    grad_heads = dot(low, out_ref[0], 1, 1).astype(bf16)
    for pair in range(pairs):
        lanes = lanes_of(pair)
        dq, dk, dv = pair_backward(
            self_q_ref[:, lanes], self_k_ref[:, lanes], self_v_ref[:, lanes], self_weights_ref, 2 * pair,
            self_inverse_ref[:, lanes], self_heads_ref[:, lanes], grad_heads[:, lanes],
        )
        self_dq_ref[:, lanes] = dq
        self_dk_ref[lanes, :] = dk
        self_dv_ref[lanes, :] = dv
    projection_grads(
        core_ref[0], normed_ref, normed_ref, low_ref, self_dq_ref, self_dk_ref, self_dv_ref, self_heads_ref,
        theirs_ref, mine_ref,
    )
    incoming = dot(self_dq_ref[...], proj_ref[0], 1, 1) + (
        dot(self_dk_ref[...], proj_ref[1], 0, 1) + dot(self_dv_ref[...], proj_ref[2], 0, 1)
    )
    term_ref[...] = incoming
    term_ref.send()
    unit, _ = norm_unit(hidden_ref[...].astype(f32))
    self_gain_grad_ref[...] = column_sum(incoming * unit)
    self_shift_grad_ref[...] = column_sum(incoming)
    dq_sum_ref[...] = column_sum(self_dq_ref[...].astype(f32))
    dv_sum_ref[...] = row_sums(self_dv_ref[...])


def other_back(
    core, low, wo, wq, q, k, v, weights, inverse, heads, own_term, first, grad_second, gain,
    out_proj, proj, self_q, self_k, self_v, self_weights, self_inverse, self_heads, hidden, normed,
):
    rows, width = first.shape
    columns, half = k.shape
    vector = shaped((1, width), f32)
    grads = shaped((4, width // 2, half), f32)
    return call(
        other_back_kernel,
        "other_back",
        [
            shaped((half, columns), bf16),
            shaped((half, columns), bf16),
            shaped((rows, width), f32),
            vector,
            vector,
            vector,
            shaped((rows, width), f32),
            grads,
            grads,
            vector,
            vector,
            shaped((1, half), f32),
            shaped((8, half), f32),
            shaped((rows, width), bf16),
            shaped((rows, half), bf16),
            shaped((half, rows), bf16),
            shaped((half, rows), bf16),
        ],
        20 * rows * width * half + 24 * rows * (columns + rows) * half,
        (core,),
        low, wo, q, k, v, inverse, heads, (weights, half // PAIR), wq, own_term, first, grad_second, gain,
        (out_proj, 2, 0), self_q, self_k, self_v, self_inverse, self_heads, (self_weights, half // PAIR),
        (proj, 3), hidden, normed,
    )


def encoder_grad_kernel(dk0_ref, dv0_ref, dk1_ref, dv1_ref, proj_ref, wk1_ref, wv1_ref, out_ref):
    own = dot(dk0_ref[...], proj_ref[1], 0, 1) + dot(dv0_ref[...], proj_ref[2], 0, 1)
    other = dot(dk1_ref[...], wk1_ref[...], 0, 1) + dot(dv1_ref[...], wv1_ref[...], 0, 1)
    out_ref[:, 0, :] = own + other


def encoder_grad(dk0, dv0, dk1, dv1, proj, wk1, wv1, frames):
    half, padded = dk0.shape
    width = wk1.shape[0]
    grad_block = pl.BlockSpec((half, FRAME_BLOCK), lambda i: (0, i))
    weight = pl.BlockSpec(wk1.shape, lambda i: (0, 0))
    return pl.pallas_call(
        encoder_grad_kernel,
        grid=(padded // FRAME_BLOCK,),
        in_specs=[grad_block] * 4 + [pl.BlockSpec(proj.shape, lambda i: (0, 0, 0)), weight, weight],
        out_specs=pl.BlockSpec((FRAME_BLOCK, 1, width), lambda i: (i, 0, 0)),
        out_shape=shaped((frames, 1, width), f32),
        compiler_params=pltpu.CompilerParams(vmem_limit_bytes=VMEM_LIMIT),
        cost_estimate=pl.CostEstimate(
            flops=8 * half * padded * width, bytes_accessed=6 * frames * width, transcendentals=0
        ),
        name="encoder_grad",
    )(dk0, dv0, dk1, dv1, proj, wk1, wv1)


def swap(value):
    return lax.ppermute(value, "tensor", [(0, 1), (1, 0)])


def tie(*values):
    return lax.optimization_barrier(values)


class Scatter:
    def __init__(self, theirs, mine, turned=False):
        self.members = lax.axis_size("dp")
        self.bits = self.members.bit_length() - 1
        self.order = list(range(self.bits))
        if turned and self.bits > 2:
            self.order = [0] + self.order[2:] + [1]
        self.stage = 0
        self.theirs, self.mine = theirs, mine

    def launch(self):
        if self.stage == self.bits:
            return
        other = 1 << self.order[self.stage]
        self.received = lax.ppermute(self.theirs, "dp", [(i, i ^ other) for i in range(self.members)])

    def land(self):
        if self.stage == self.bits:
            return
        mine, received = self.mine, self.received
        if self.stage == 0:
            lead = mine.shape[:-2]
            self.lead = len(lead)
            cuts = self.bits - 1
            shape = lead + (2,) * cuts + (mine.shape[-2] >> cuts, mine.shape[-1])
            mine, received = mine.reshape(shape), received.reshape(shape)
        self.stage += 1
        if self.stage < self.bits:
            bit = self.order[self.stage]
            axis = self.lead + self.bits - 1 - bit
            side = (lax.axis_index("dp") >> bit) & 1

            def half(which):
                return lax.dynamic_index_in_dim(mine, which, axis, keepdims=True) + lax.dynamic_index_in_dim(
                    received, which, axis, keepdims=True
                )

            self.theirs = half(1 - side)
            self.mine = half(side)
        else:
            total = mine + received
            self.part = total.reshape(total.shape[: self.lead] + total.shape[-2:])

    def finish(self):
        while self.stage < self.bits:
            self.land()
            self.launch()
        return self.part


def place_kernel(moves, gathered_ref, *refs):
    outs, (held, in_sems, out_sems) = refs[:-3], refs[-3:]
    reads = [
        pltpu.make_async_copy(gathered_ref.at[i], held.at[i], in_sems.at[i]) for i in range(held.shape[0])
    ]
    for read in reads:
        read.start()
    writes = []
    for i, read in enumerate(reads):
        read.wait()
        for start, count, out, target in moves[i]:
            writes.append(
                pltpu.make_async_copy(
                    held.at[i, pl.ds(start, count)], outs[out].at[target], out_sems.at[len(writes)]
                )
            )
            writes[-1].start()
    for write in writes:
        write.wait()


def place(gathered, width, units):
    members, total, half = gathered.shape
    parts = members // 2
    rows = units // members
    count = width // members
    proj = shaped((3, width, half), f32)
    outs = [shaped((units, width), f32), shaped((width, units), f32), proj, proj, shaped((2, half, width), f32)]
    if count % 8 == 0:
        moves = []
        for i in range(members):
            q, c = i // 2, i % 2
            moves.append([])
            for j in range(2):
                columns = pl.ds(j * half, half)
                moves[i].append((j * rows, rows, 0, (pl.ds(c * width + q * rows, rows), columns)))
                columns = pl.ds(c * width + j * half, half)
                moves[i].append(((2 + j) * rows, rows, 1, (pl.ds(q * rows, rows), columns)))
            here = pl.ds(c * (width // 2) + q * count, count)
            for branch in range(2):
                start = 4 * rows + branch * 4 * count
                for a in range(3):
                    moves[i].append((start + a * count, count, 2 + branch, (a, here)))
                target = (1 - branch, pl.ds(q * count, count), pl.ds(c * half, half))
                moves[i].append((start + 3 * count, count, 4, target))
        anywhere = pl.BlockSpec(memory_space=pl.ANY)
        return pl.pallas_call(
            partial(place_kernel, moves),
            in_specs=[anywhere],
            out_specs=[anywhere] * len(outs),
            out_shape=outs,
            scratch_shapes=[
                pltpu.VMEM(gathered.shape, f32),
                pltpu.SemaphoreType.DMA((members,)),
                pltpu.SemaphoreType.DMA((sum(len(m) for m in moves),)),
            ],
            compiler_params=pltpu.CompilerParams(vmem_limit_bytes=VMEM_LIMIT),
            cost_estimate=pl.CostEstimate(flops=0, bytes_accessed=8 * gathered.size, transcendentals=0),
            name="place",
        )(gathered)
    split = gathered[:, : 4 * rows].reshape(parts, 2, 2, 2, rows, half)
    fc2 = split[:, :, 0].transpose(1, 0, 3, 2, 4).reshape(units, width)
    fc1 = split[:, :, 1].transpose(0, 3, 1, 2, 4).reshape(width, units)
    split = gathered[:, 4 * rows :].reshape(parts, 2, 2, 4, count, half)
    projections = split[:, :, :, :3].transpose(2, 3, 1, 0, 4, 5).reshape(2, 3, width, half)
    outputs = split[:, :, ::-1, 3].transpose(2, 0, 3, 1, 4).reshape(2, half, width)
    return fc2, fc1, projections[0], projections[1], outputs


def per_device(
    hidden,
    encoder,
    text_len,
    audio_len,
    corpus_weight,
    cotangent,
    norm_gain,
    norm_bias,
    self_proj,
    self_bias,
    cross_proj,
    cross_bias,
    out_proj,
    out_bias,
    fc1_weight,
    fc1_bias,
    fc2_weight,
    fc2_bias,
):
    sequences, frames, width = encoder.shape
    members = lax.axis_size("dp")
    me = lax.axis_index("dp")
    half = self_proj.shape[2]
    padded = -(-frames // FRAME_BLOCK) * FRAME_BLOCK
    core = (me & 1).astype(jnp.int32).reshape(1)

    cross_rows = jnp.concatenate(
        [cross_proj.reshape(-1, half), out_proj[1][:, :half], out_proj[1][:, half:]], axis=0
    )
    count = cross_rows.shape[0] // members
    part = swap(lax.dynamic_slice_in_dim(cross_rows, me * count, count, 0).astype(f32))
    hidden_in, part = tie(hidden, part)
    gathered = lax.all_gather(part, "dp", axis=0, tiled=True)

    normed_self, q_self, k_self, v_self, weights_self, inverse_self, heads_self, partial_self = self_forward(
        text_len, hidden_in, norm_gain, norm_bias, self_proj, self_bias, out_proj
    )
    received = swap(partial_self)
    other_bias = swap(cross_bias)

    frames_in = jnp.pad(encoder.reshape(frames, width), ((0, padded - frames), (0, 0)))
    k_own = dot(frames_in, cross_proj[1], 1, 0).astype(bf16)
    v_own = (dot(frames_in, cross_proj[2], 1, 0) + cross_bias[1]).astype(bf16)
    received, k_own, v_own = tie(received, k_own, v_own)
    first, normed_cross, q_own, weights_own, inverse_own, heads_own, term_own = cross_own(
        audio_len, hidden, partial_self, received, out_bias, norm_gain, norm_bias,
        cross_proj, cross_bias, k_own, v_own, out_proj,
    )
    gathered, normed_cross = tie(gathered, normed_cross)
    (
        q_other, k_other, v_other, weights_other, inverse_other, heads_other,
        wq_other, wk_other, wv_other, wo_other,
        second, partial_normed, fc2_theirs, fc1_theirs, fc2_mine, fc1_mine, partial_mlp,
        fc1_bias_grad, fc2_bias_grad,
    ) = late_forward(
        audio_len, text_len, corpus_weight, core, gathered, normed_cross, frames_in, other_bias, term_own, first,
        out_bias, norm_gain, norm_bias, fc1_weight, fc1_bias.reshape(1, -1), cotangent, fc2_weight,
    )
    received = swap(partial_normed)
    fc2_share = Scatter(fc2_theirs, fc2_mine)
    fc1_share = Scatter(fc1_theirs, fc1_mine, turned=True)
    fc2_share.launch()
    fc1_share.launch()
    fc2_share.land()
    fc2_share.launch()
    fc1_share.land()
    fc1_share.launch()

    (
        grad_second, second_low, gain_mlp, shift_mlp, bias_cross, dq_own, dk_own, dv_own, back_own,
        dq_cross_sum, dv_cross_sum, cross_theirs, cross_mine,
    ) = cross_own_back(
        text_len, corpus_weight, core, cotangent, second, partial_normed, received, norm_gain,
        out_proj, cross_proj, q_own, k_own, v_own, weights_own, inverse_own, heads_own, normed_cross, frames_in,
    )
    cross_theirs, fc2_share.received, fc1_share.received = tie(
        cross_theirs, fc2_share.received, fc1_share.received
    )
    cross_share = Scatter(cross_theirs, cross_mine)
    cross_share.launch()
    fc2_share.land()
    fc1_share.land()
    fc2_share.launch()
    fc1_share.launch()
    cross_share.received, fc2_share.theirs, fc1_share.theirs = tie(
        cross_share.received, fc2_share.theirs, fc1_share.theirs
    )
    cross_share.land()
    second_low, cross_share.theirs = tie(second_low, cross_share.theirs)
    cross_share.launch()

    (
        dk_other, dv_other, grad_first, gain_cross, shift_cross, bias_self, partial_normed,
        self_theirs, self_mine, gain_self, shift_self, dq_self_sum, dv_self_sum, *_,
    ) = other_back(
        core, second_low, wo_other, wq_other, q_other, k_other, v_other, weights_other, inverse_other, heads_other,
        back_own, first, grad_second, norm_gain, out_proj, self_proj, q_self, k_self, v_self, weights_self,
        inverse_self, heads_self, hidden, normed_self,
    )
    self_theirs, cross_share.received, fc1_share.received, fc2_share.received = tie(
        self_theirs, cross_share.received, fc1_share.received, fc2_share.received
    )
    self_share = Scatter(self_theirs, self_mine)
    self_share.launch()
    fc2_share.land()
    fc2_share.launch()
    cross_share.received, fc2_share.theirs = tie(cross_share.received, fc2_share.theirs)
    cross_share.land()
    self_share.land()
    self_share.theirs, cross_share.theirs, partial_normed, dk_own = tie(
        self_share.theirs, cross_share.theirs, partial_normed, dk_own
    )
    self_share.launch()
    cross_share.launch()
    received = swap(partial_normed)
    grad_encoder = encoder_grad(
        dk_own, dv_own, dk_other, dv_other, cross_proj, wk_other, wv_other, frames
    ).reshape(encoder.shape)
    cross_share.received, fc1_share.received, partial_normed, grad_encoder = tie(
        cross_share.received, fc1_share.received, partial_normed, grad_encoder
    )
    cross_share.land()
    fc1_share.land()
    cross_share.launch()
    self_share.received, cross_share.theirs = tie(self_share.received, cross_share.theirs)
    self_share.land()
    self_share.launch()
    fc1_share.theirs, self_share.theirs, hidden = tie(fc1_share.theirs, self_share.theirs, hidden)
    fc1_share.launch()
    cross_share.received, fc2_share.received, fc1_share.received, grad_encoder, _ = tie(
        cross_share.received, fc2_share.received, fc1_share.received, grad_encoder, self_share.theirs
    )
    cross_part = cross_share.finish()
    fc2_part = fc2_share.finish()
    fc1_part = fc1_share.finish()

    most = [fc2_part[:, :half], fc2_part[:, half:], fc1_part[:, :half], fc1_part[:, half:]]
    most = jnp.concatenate([item.reshape(-1, half) for item in (*most, cross_part)], axis=0)
    unit_self, root_self = norm_unit(hidden.astype(f32))
    grad_hidden = (
        grad_first + norm_backward(partial_normed + received, unit_self, root_self, norm_gain[0])
    ).astype(bf16)
    grad_hidden, most, self_share.received = tie(grad_hidden, most, self_share.received)
    self_part = self_share.finish()
    every = jnp.concatenate([most, self_part.reshape(-1, half)], axis=0)

    small = (
        gain_self,
        shift_self,
        gain_cross,
        gain_mlp,
        shift_cross,
        shift_mlp,
        dq_self_sum,
        dv_self_sum,
        dq_cross_sum,
        dv_cross_sum,
        bias_self,
        bias_cross,
        fc1_bias_grad,
        fc2_bias_grad,
    )
    *small, partial_mlp, every = tie(*small, partial_mlp, every)
    every = lax.all_gather(every, "dp", axis=0, tiled=False)
    small[7] = small[7][0:1]
    small[9] = small[9][0:1]
    norm_self = jnp.concatenate(small[0:2], axis=0)
    small = [norm_self + swap(norm_self)] + small[2:]
    flat = jnp.concatenate([item.reshape(-1, half) for item in small], axis=0)
    for bit in range(members.bit_length() - 1):
        flat = flat + lax.ppermute(flat, "dp", [(i, i ^ (1 << bit)) for i in range(members)])
    received_mlp = swap(partial_mlp)
    result = (second + (partial_mlp + received_mlp) + fc2_bias).astype(bf16)
    fc2_weight_grad, fc1_weight_grad, cross_proj_grad, self_proj_grad, out_proj_grad = place(
        every, width, fc2_weight.shape[0]
    )
    small_out = []
    offset = 0
    for item in small:
        count = item.size // half
        small_out.append(flat[offset : offset + count].reshape(item.shape))
        offset += count
    (
        norm_self, gain_cross, gain_mlp, shift_cross, shift_mlp, dq_self_sum, dv_self_sum, dq_cross_sum,
        dv_cross_sum, bias_self, bias_cross, fc1_bias_grad, fc2_bias_grad,
    ) = small_out
    return (
        result,
        grad_hidden,
        grad_encoder,
        jnp.concatenate([norm_self[0:1], gain_cross, gain_mlp], axis=0),
        jnp.concatenate([norm_self[1:2], shift_cross, shift_mlp], axis=0),
        self_proj_grad,
        jnp.concatenate([dq_self_sum, dv_self_sum], axis=0),
        cross_proj_grad,
        jnp.concatenate([dq_cross_sum, dv_cross_sum], axis=0),
        out_proj_grad,
        jnp.concatenate([bias_self, bias_cross], axis=0),
        fc1_weight_grad,
        fc1_bias_grad.reshape(-1),
        fc2_weight_grad,
        fc2_bias_grad.reshape(-1),
    )


def solution(mesh):
    placed = (
        P("dp", None),
        P("dp", None, None),
        P("dp"),
        P("dp"),
        P("dp"),
        P("dp", None),
        P(),
        P(),
        P(None, None, "tensor"),
        P(None, "tensor"),
        P(None, None, "tensor"),
        P(None, "tensor"),
        P(None, "tensor", None),
        P(),
        P(None, "tensor"),
        P("tensor"),
        P("tensor", None),
        P(),
    )
    return jax.shard_map(
        per_device,
        mesh=mesh,
        in_specs=placed,
        out_specs=(
            P("dp", None),
            P("dp", None),
            P("dp", None, None),
            P(),
            P(),
            P(None, None, "tensor"),
            P(None, "tensor"),
            P(None, None, "tensor"),
            P(None, "tensor"),
            P(None, "tensor", None),
            P(),
            P(None, "tensor"),
            P("tensor"),
            P("tensor", None),
            P(),
        ),
        check_vma=False,
    )
```

```python
from functools import partial

import jax
import jax.numpy as jnp
from jax import lax
from jax.experimental import pallas as pl
from jax.experimental.pallas import tpu as pltpu
from jax.sharding import PartitionSpec as P

HEAD_DIM = 64
SCALE = HEAD_DIM ** (-0.5)
PAIR = 2 * HEAD_DIM
FF_BLOCK = 768
FRAME_BLOCK = 256
VMEM_LIMIT = 63 * 1024 * 1024 + 512 * 1024
COST_SHARE = 64
epsilon = 1e-05
masked_value = -1e30
f32 = jnp.float32
bf16 = jnp.bfloat16


def dot(a, b, ca, cb):
    return lax.dot_general(a, b, (((ca,), (cb,)), ((), ())), preferred_element_type=f32)


def shaped(shape, dtype):
    return jax.ShapeDtypeStruct(shape, dtype)


class Source:
    def __init__(self, ref, held, sems, first_sem, pieces):
        self.held, self.shape, self.dtype = held, held.shape, held.dtype
        self.size = held.shape[0] // pieces
        self.ref, self.sems, self.first_sem = ref, sems, first_sem
        self.copies = [None] * pieces
        self.pending = [True] * pieces

    def fetch(self, *pieces):
        for piece in pieces or range(len(self.copies)):
            if self.copies[piece] is None:
                here = pl.ds(piece * self.size, self.size)
                self.copies[piece] = pltpu.make_async_copy(
                    self.ref.at[here], self.held.at[here], self.sems.at[self.first_sem + piece]
                )
                self.copies[piece].start()

    def wait(self, piece):
        if self.pending[piece]:
            self.fetch(piece)
            self.pending[piece] = False
            self.copies[piece].wait()

    def __getitem__(self, index):
        if len(self.copies) > 1 and isinstance(index, int):
            self.wait(index // self.size)
        else:
            for piece in range(len(self.copies)):
                self.wait(piece)
        return self.held[index]


class Sink:
    def __init__(self, ref, held, sems, first_sem, pieces):
        self.held, self.shape, self.dtype = held, held.shape, held.dtype
        self.size = held.shape[0] // pieces
        self.copies = []
        self.sent = []
        for i in range(pieces):
            here = pl.ds(i * self.size, self.size)
            self.copies.append(pltpu.make_async_copy(held.at[here], ref.at[here], sems.at[first_sem + i]))
            self.sent.append(False)

    def __getitem__(self, index):
        return self.held[index]

    def __setitem__(self, index, value):
        self.held[index] = value

    def send(self, piece=0):
        self.sent[piece] = True
        self.copies[piece].start()


class Resident:
    def __init__(self, value):
        self.value = value

    def __getitem__(self, index):
        return self.value[index]

    def __setitem__(self, index, value):
        self.value[index] = value


def call(kernel, name, out_shape, flops, scalars, *arrays):
    arrays = [a if isinstance(a, tuple) else (a, 1) for a in arrays]
    used = [a[2:] for a in arrays]
    arrays = [a[:2] for a in arrays]
    outs = [o if isinstance(o, tuple) else (o, 1) for o in out_shape]
    in_stays = [isinstance(a, Resident) for a, _ in arrays]
    out_stays = [isinstance(o, Resident) for o, _ in outs]
    in_pieces = [0 if stays else pieces for (_, pieces), stays in zip(arrays, in_stays)]
    out_pieces = [0 if stays else pieces for (_, pieces), stays in zip(outs, out_stays)]
    arrays = [a.value if stays else a for (a, _), stays in zip(arrays, in_stays)]
    outs = [o.value if stays else o for (o, _), stays in zip(outs, out_stays)]
    moved = sum(a.size * a.dtype.itemsize for a in (*arrays, *outs))

    def body(*refs):
        refs = list(refs)
        scalar_refs = [refs.pop(0) for _ in scalars]
        in_refs = [refs.pop(0) for _ in arrays]
        out_refs = [refs.pop(0) for _ in outs]
        in_held = [None if stays else refs.pop(0) for stays in in_stays]
        out_held = [None if stays else refs.pop(0) for stays in out_stays]
        in_sems, out_sems = refs
        sources = []
        for i, (ref, held) in enumerate(zip(in_refs, in_held)):
            if in_stays[i]:
                sources.append(Resident(ref))
            else:
                sources.append(Source(ref, held, in_sems, sum(in_pieces[:i]), in_pieces[i]))
        sinks = []
        for i, (ref, held) in enumerate(zip(out_refs, out_held)):
            if out_stays[i]:
                sinks.append(Resident(ref))
            else:
                sinks.append(Sink(ref, held, out_sems, sum(out_pieces[:i]), out_pieces[i]))
        moving = [source for source in sources if isinstance(source, Source)]
        leaving = [sink for sink in sinks if isinstance(sink, Sink)]
        for source, only in zip(sources, used):
            if isinstance(source, Source):
                source.fetch(*only)
        kernel(*scalar_refs, *sources, *sinks)
        for source in moving:
            for piece in range(len(source.copies)):
                if source.copies[piece] is not None:
                    source.wait(piece)
        for sink in leaving:
            for piece, sent in enumerate(sink.sent):
                if not sent:
                    sink.send(piece)
        for sink in leaving:
            for copy in sink.copies:
                copy.wait()

    anywhere = pl.BlockSpec(memory_space=pl.ANY)
    here = pl.BlockSpec(memory_space=pltpu.VMEM)
    scratch = [pltpu.VMEM(a.shape, a.dtype) for a, stays in zip(arrays, in_stays) if not stays]
    scratch += [pltpu.VMEM(o.shape, o.dtype) for o, stays in zip(outs, out_stays) if not stays]
    return pl.pallas_call(
        body,
        in_specs=[pl.BlockSpec(memory_space=pltpu.SMEM)] * len(scalars)
        + [here if stays else anywhere for stays in in_stays],
        out_specs=[here if stays else anywhere for stays in out_stays],
        out_shape=outs,
        scratch_shapes=scratch
        + [pltpu.SemaphoreType.DMA((sum(in_pieces),)), pltpu.SemaphoreType.DMA((sum(out_pieces),))],
        compiler_params=pltpu.CompilerParams(vmem_limit_bytes=VMEM_LIMIT),
        cost_estimate=pl.CostEstimate(
            flops=flops // COST_SHARE, bytes_accessed=moved // COST_SHARE, transcendentals=0
        ),
        name=name,
    )(*scalars, *arrays)


def lanes_of(pair):
    return slice(pair * PAIR, (pair + 1) * PAIR)


def add_up(terms):
    total = terms[0]
    for term in terms[1:]:
        total = total + term
    return total


def norm_unit(values):
    centered = values - jnp.mean(values, axis=-1, keepdims=True)
    inverse = lax.rsqrt(jnp.mean(centered * centered, axis=-1, keepdims=True) + epsilon)
    return centered * inverse, inverse


def norm_backward(incoming, unit, inverse, gain):
    scaled = incoming * gain
    scaled_mean = jnp.mean(scaled, axis=-1, keepdims=True)
    along_unit = jnp.mean(scaled * unit, axis=-1, keepdims=True)
    return inverse * (scaled - scaled_mean - unit * along_unit)


def column_sum(values):
    return jnp.sum(values, axis=0, keepdims=True)


def live_gradient(cotangent, text_len, corpus_weight):
    places = lax.broadcasted_iota(jnp.int32, (cotangent.shape[0], 1), 0)
    live = jnp.where(places < text_len, corpus_weight, 0.0)
    return cotangent.astype(f32) * live


def lane_masks(rows):
    return lax.broadcasted_iota(jnp.int32, (rows, PAIR), 1) < HEAD_DIM


def pair_forward(length, causal, q, k, v, weights_ref, start):
    rows, columns = q.shape[0], k.shape[0]
    first_lanes = lane_masks(rows)
    if causal:
        places = lax.broadcasted_iota(jnp.int32, (rows, columns), 1)
        allowed = (places < length) & (places <= lax.broadcasted_iota(jnp.int32, (rows, columns), 0))
    else:
        places = lax.broadcasted_iota(jnp.int32, (1, columns), 1)
        shift = jnp.where(places < length, 0.0, masked_value)
    scores = []
    for head in range(2):
        mine = first_lanes if head == 0 else jnp.logical_not(first_lanes)
        raw = dot(jnp.where(mine, q, jnp.zeros_like(q)), k, 1, 1)
        scores.append(jnp.where(allowed, raw, masked_value) if causal else raw + shift)
    inverses = []
    for head in range(2):
        largest = jnp.max(scores[head], axis=-1, keepdims=True)
        weights = jnp.exp(scores[head] - largest)
        inverses.append(1.0 / jnp.sum(weights, axis=-1, keepdims=True))
        weights_ref[start + head] = weights.astype(bf16)
    mixed = [dot(weights_ref[start + head], v, 1, 0) for head in range(2)]
    inverse = jnp.where(first_lanes, inverses[0], inverses[1])
    return (jnp.where(first_lanes, mixed[0], mixed[1]) * inverse).astype(bf16), inverse


def pair_backward(q, k, v, weights_ref, start, inverse, heads, grad_heads):
    first_lanes = lane_masks(q.shape[0])
    grad = (grad_heads.astype(f32) * inverse).astype(bf16)
    along = grad.astype(f32) * heads.astype(f32)
    dq = []
    dk = None
    dv = None
    for head in range(2):
        mine = first_lanes if head == 0 else jnp.logical_not(first_lanes)
        grad_one = jnp.where(mine, grad, jnp.zeros_like(grad))
        q_one = jnp.where(mine, q, jnp.zeros_like(q))
        row_terms = jnp.sum(jnp.where(mine, along, 0.0), axis=-1, keepdims=True)
        weights = weights_ref[start + head]
        grad_probs = dot(grad_one, v, 1, 1)
        grad_scores = (weights.astype(f32) * (grad_probs - row_terms)).astype(bf16)
        dv_one = dot(grad_one, weights, 0, 0)
        dk_one = dot(q_one, grad_scores, 0, 0)
        dq.append(dot(grad_scores, k, 1, 0))
        dk = dk_one if dk is None else dk + dk_one
        dv = dv_one if dv is None else dv + dv_one
    dq = (jnp.where(first_lanes, dq[0], dq[1]) * SCALE).astype(bf16)
    return dq, dk.astype(bf16), dv.astype(bf16)


def row_sums(values):
    return dot(jnp.ones((8, values.shape[1]), bf16), values, 1, 1)


def self_forward_kernel(
    length_ref, hidden_ref, gain_ref, shift_ref, proj_ref, bias_ref, out_ref,
    normed_ref, q_ref, k_ref, v_ref, weights_ref, inverse_ref, heads_ref, partial_ref,
):
    unit, _ = norm_unit(hidden_ref[...].astype(f32))
    normed = (unit * gain_ref[0:1, :] + shift_ref[0:1, :]).astype(bf16)
    normed_ref[...] = normed
    normed_ref.send()
    q_ref[...] = ((dot(normed, proj_ref[0], 1, 0) + bias_ref[0:1]) * SCALE).astype(bf16)
    k_ref[...] = dot(normed, proj_ref[1], 1, 0).astype(bf16)
    v_ref[...] = (dot(normed, proj_ref[2], 1, 0) + bias_ref[1:2]).astype(bf16)
    q_ref.send()
    k_ref.send()
    v_ref.send()
    for pair in range(q_ref.shape[1] // PAIR):
        lanes = lanes_of(pair)
        heads, inverse = pair_forward(
            length_ref[0], True, q_ref[:, lanes], k_ref[:, lanes], v_ref[:, lanes], weights_ref, 2 * pair
        )
        weights_ref.send(pair)
        heads_ref[:, lanes] = heads
        inverse_ref[:, lanes] = inverse
    heads_ref.send()
    inverse_ref.send()
    partial_ref[...] = dot(heads_ref[...], out_ref[0], 1, 0)


def self_forward(text_len, hidden, gain, shift, proj, bias, out_proj):
    rows, width = hidden.shape
    half = proj.shape[2]
    return call(
        self_forward_kernel,
        "self_forward",
        [
            shaped((rows, width), bf16),
            shaped((rows, half), bf16),
            shaped((rows, half), bf16),
            shaped((rows, half), bf16),
            (shaped((half // HEAD_DIM, rows, rows), bf16), half // PAIR),
            shaped((rows, half), f32),
            shaped((rows, half), bf16),
            shaped((rows, width), f32),
        ],
        8 * rows * width * half + 12 * rows * rows * half,
        (text_len,),
        hidden, gain, shift, (proj, 3), bias, (out_proj, 2, 0),
    )


def cross_own_kernel(
    length_ref, received_ref, partial_ref, hidden_ref, out_bias_ref, gain_ref, shift_ref,
    proj_ref, bias_ref, k_ref, v_ref, out_ref,
    first_ref, normed_ref, q_ref, weights_ref, inverse_ref, heads_ref, term_ref,
):
    first = hidden_ref[...].astype(f32) + (partial_ref[...] + received_ref[...]) + out_bias_ref[0:1, :]
    first_ref[...] = first
    first_ref.send()
    unit, _ = norm_unit(first)
    normed = (unit * gain_ref[1:2, :] + shift_ref[1:2, :]).astype(bf16)
    normed_ref[...] = normed
    normed_ref.send()
    q_ref[...] = ((dot(normed, proj_ref[0], 1, 0) + bias_ref[0:1]) * SCALE).astype(bf16)
    q_ref.send()
    for pair in range(q_ref.shape[1] // PAIR):
        lanes = lanes_of(pair)
        heads, inverse = pair_forward(
            length_ref[0], False, q_ref[:, lanes], k_ref[:, lanes], v_ref[:, lanes], weights_ref, 2 * pair
        )
        weights_ref.send(pair)
        heads_ref[:, lanes] = heads
        inverse_ref[:, lanes] = inverse
    heads_ref.send()
    inverse_ref.send()
    term_ref[...] = dot(heads_ref[...], out_ref[1], 1, 0)


def cross_own(audio_len, hidden, partial_self, received, out_bias, gain, shift, proj, bias, k, v, out_proj):
    rows, width = hidden.shape
    columns, half = k.shape
    return call(
        cross_own_kernel,
        "cross_own",
        [
            shaped((rows, width), f32),
            shaped((rows, width), bf16),
            shaped((rows, half), bf16),
            (shaped((half // HEAD_DIM, rows, columns), bf16), half // PAIR),
            shaped((rows, half), f32),
            shaped((rows, half), bf16),
            shaped((rows, width), f32),
        ],
        4 * rows * width * half + 12 * rows * columns * half,
        (audio_len,),
        received, partial_self, hidden, out_bias, gain, shift, (proj, 3, 0), bias, k, v,
        (out_proj, 2, 1),
    )


def error_function(x):
    x = jnp.clip(x, -4.0, 4.0)
    square = x * x
    top = jnp.full_like(x, -2.72614225801306e-10)
    for c in (
        2.77068142495902e-08,
        -2.10102402082508e-06,
        -5.69250639462346e-05,
        -7.34990630326855e-04,
        -2.95459980854025e-03,
        -1.60960333262415e-02,
    ):
        top = top * square + c
    bottom = jnp.full_like(x, -1.45660718464996e-05)
    for c in (-2.13374055278905e-04, -1.68282697438203e-03, -7.37332916720468e-03, -1.42647390514189e-02):
        bottom = bottom * square + c
    return x * top / bottom


def late_forward_kernel(
    audio_ref, text_ref, weight_ref, core_ref, gathered_ref, normed_ref, frames_ref, bias_ref, own_ref, first_ref,
    out_bias_ref, gain_ref, shift_ref, fc1_ref, fc1_bias_ref, cotangent_ref, fc2_ref,
    q_ref, k_ref, v_ref, weights_ref, inverse_ref, heads_ref, wq_ref, wk_ref, wv_ref, wo_ref,
    second_ref, normed_grad_ref, fc2_theirs_ref, fc1_theirs_ref, fc2_mine_ref, fc1_mine_ref, mlp_ref,
    fc1_bias_grad_ref, fc2_bias_grad_ref,
):
    width, half = wq_ref.shape
    for i, ref in enumerate((wq_ref, wk_ref, wv_ref)):
        ref[...] = gathered_ref[i * width : (i + 1) * width, :].astype(bf16)
        ref.send()
    for i in range(width // half):
        start = 3 * width + i * half
        wo_ref[:, i * half : (i + 1) * half] = gathered_ref[start : start + half, :].astype(bf16)
    wo_ref.send()
    q_ref[...] = ((dot(normed_ref[...], wq_ref[...], 1, 0) + bias_ref[0:1]) * SCALE).astype(bf16)
    k_ref[...] = dot(frames_ref[...], wk_ref[...], 1, 0).astype(bf16)
    v_ref[...] = (dot(frames_ref[...], wv_ref[...], 1, 0) + bias_ref[1:2]).astype(bf16)
    q_ref.send()
    k_ref.send()
    v_ref.send()
    for pair in range(half // PAIR):
        lanes = lanes_of(pair)
        heads, inverse = pair_forward(
            audio_ref[0], False, q_ref[:, lanes], k_ref[:, lanes], v_ref[:, lanes], weights_ref, 2 * pair
        )
        weights_ref.send(pair)
        heads_ref[:, lanes] = heads
        inverse_ref[:, lanes] = inverse
    heads_ref.send()
    inverse_ref.send()
    other = dot(heads_ref[...], wo_ref[...], 1, 0)

    second = first_ref[...] + (own_ref[...] + other) + out_bias_ref[1:2, :]
    second_ref[...] = second
    second_ref.send()
    unit, _ = norm_unit(second)
    normed = (unit * gain_ref[2:3, :] + shift_ref[2:3, :]).astype(bf16)
    grad_y = live_gradient(cotangent_ref[...], text_ref[0], weight_ref[0])
    fc2_bias_grad_ref[...] = column_sum(grad_y)
    grad = grad_y.astype(bf16)
    part = fc2_theirs_ref.shape[0]
    for turn, (fc2_out, fc1_out) in enumerate(((fc2_theirs_ref, fc1_theirs_ref), (fc2_mine_ref, fc1_mine_ref))):
        side = 1 - core_ref[0] if turn == 0 else core_ref[0]
        for start in range(0, part, FF_BLOCK):
            here = pl.ds(pl.multiple_of(side * part + start, FF_BLOCK), FF_BLOCK)
            there = slice(start, start + FF_BLOCK)
            fc1 = fc1_ref[:, here]
            pre = dot(normed, fc1, 1, 0) + fc1_bias_ref[:, here]
            cdf = 0.5 * (1.0 + error_function(pre * 0.7071067811865476))
            inner = (pre * cdf).astype(bf16)
            slope = cdf + pre * (0.3989422804014327 * jnp.exp(-0.5 * pre * pre))
            fc2 = fc2_ref[here, :]
            grad_pre = (dot(grad, fc2, 1, 1) * slope).astype(bf16)
            fc1_bias_grad_ref[:, here] = column_sum(grad_pre.astype(f32))
            fc2_out[there, :] = dot(inner, grad, 0, 0)
            fc1_out[:, there] = dot(normed, grad_pre, 0, 0)
            mlp_term = dot(inner, fc2, 1, 0)
            normed_term = dot(grad_pre, fc1, 1, 1)
            if turn == 0 and start == 0:
                mlp_ref[...] = mlp_term
                normed_grad_ref[...] = normed_term
            else:
                mlp_ref[...] += mlp_term
                normed_grad_ref[...] += normed_term
        fc2_out.send()
        fc1_out.send()


def late_forward(
    audio_len, text_len, corpus_weight, core, gathered, normed, frames_in, bias, own, first, out_bias, gain, shift,
    fc1, fc1_bias, cotangent, fc2,
):
    rows, width = first.shape
    units = fc2.shape[0]
    columns = frames_in.shape[0]
    half = gathered.shape[1]
    full = shaped((rows, width), f32)
    proj = shaped((width, half), bf16)
    return call(
        late_forward_kernel,
        "late_forward",
        [
            shaped((rows, half), bf16),
            shaped((columns, half), bf16),
            shaped((columns, half), bf16),
            (shaped((half // HEAD_DIM, rows, columns), bf16), half // PAIR),
            shaped((rows, half), f32),
            shaped((rows, half), bf16),
            proj,
            proj,
            proj,
            shaped((half, width), bf16),
            full,
            full,
            shaped((units // 2, width), f32),
            shaped((width, units // 2), f32),
            shaped((units // 2, width), f32),
            shaped((width, units // 2), f32),
            full,
            shaped((1, units), f32),
            shaped((1, width), f32),
        ],
        4 * rows * width * half + 4 * columns * width * half + 12 * rows * (columns * half + width * units),
        (audio_len, text_len, corpus_weight, core),
        gathered, normed, frames_in, bias, own, first, out_bias, gain, shift, fc1, fc1_bias, cotangent, fc2,
    )


def projection_grads(core, normed, source, low, dq, dk, dv, heads, theirs_ref, mine_ref):
    part = theirs_ref.shape[1]
    for out_ref, side in ((theirs_ref, 1 - core), (mine_ref, core)):
        here = pl.ds(pl.multiple_of(side * part, PAIR), part)
        piece = source[:, here]
        out_ref[0] = dot(normed[:, here], dq[...], 0, 0)
        out_ref[1] = dot(piece, dk[...], 0, 1)
        out_ref[2] = dot(piece, dv[...], 0, 1)
        out_ref[3] = dot(heads[...], low[:, here], 0, 0)
        out_ref.send()


def cross_own_back_kernel(
    length_ref, weight_ref, core_ref, received_ref, partial_ref, second_ref, cotangent_ref, gain_ref,
    out_ref, q_ref, k_ref, v_ref, inverse_ref, heads_ref, weights_ref, proj_ref, normed_ref, frames_ref,
    grad_second_ref, low_ref, gain_grad_ref, shift_grad_ref, bias_grad_ref,
    dq_ref, dk_ref, dv_ref, term_ref, dq_sum_ref, dv_sum_ref, theirs_ref, mine_ref,
):
    incoming = partial_ref[...] + received_ref[...]
    unit, inverse = norm_unit(second_ref[...])
    gain_grad_ref[...] = column_sum(incoming * unit)
    shift_grad_ref[...] = column_sum(incoming)
    grad_second = live_gradient(cotangent_ref[...], length_ref[0], weight_ref[0]) + norm_backward(
        incoming, unit, inverse, gain_ref[2:3, :]
    )
    grad_second_ref[...] = grad_second
    grad_second_ref.send()
    low = grad_second.astype(bf16)
    low_ref[...] = low
    low_ref.send()
    bias_grad_ref[...] = column_sum(grad_second)
    grad_heads = dot(low, out_ref[1], 1, 1).astype(bf16)
    for pair in range(q_ref.shape[1] // PAIR):
        lanes = lanes_of(pair)
        dq, dk, dv = pair_backward(
            q_ref[:, lanes], k_ref[:, lanes], v_ref[:, lanes], weights_ref, 2 * pair,
            inverse_ref[:, lanes], heads_ref[:, lanes], grad_heads[:, lanes],
        )
        dq_ref[:, lanes] = dq
        dk_ref[lanes, :] = dk
        dv_ref[lanes, :] = dv
    dk_ref.send()
    dv_ref.send()
    projection_grads(
        core_ref[0], normed_ref, frames_ref, low_ref, dq_ref, dk_ref, dv_ref, heads_ref, theirs_ref, mine_ref
    )
    term_ref[...] = dot(dq_ref[...], proj_ref[0], 1, 1)
    dq_sum_ref[...] = column_sum(dq_ref[...].astype(f32))
    dv_sum_ref[...] = row_sums(dv_ref[...])


def cross_own_back(
    text_len, corpus_weight, core, cotangent, second, partial_normed, received, gain, out_proj, proj,
    q, k, v, weights, inverse, heads, normed, frames_in,
):
    rows, width = second.shape
    columns, half = k.shape
    vector = shaped((1, width), f32)
    grads = shaped((4, width // 2, half), f32)
    return call(
        cross_own_back_kernel,
        "cross_own_back",
        [
            shaped((rows, width), f32),
            shaped((rows, width), bf16),
            vector,
            vector,
            vector,
            shaped((rows, half), bf16),
            shaped((half, columns), bf16),
            shaped((half, columns), bf16),
            shaped((rows, width), f32),
            shaped((1, half), f32),
            shaped((8, half), f32),
            grads,
            grads,
        ],
        8 * rows * width * half + 4 * columns * width * half + 24 * rows * columns * half,
        (text_len, corpus_weight, core),
        received, partial_normed, second, cotangent, gain, (out_proj, 2, 1), q, k, v, inverse, heads,
        (weights, half // PAIR), (proj, 3, 0), normed, frames_in,
    )


def other_back_kernel(
    core_ref, low_in_ref, wo_ref, q_ref, k_ref, v_ref, inverse_ref, heads_ref, weights_ref, wq_ref,
    own_term_ref, first_ref, grad_second_ref, gain_ref,
    out_ref, self_q_ref, self_k_ref, self_v_ref, self_inverse_ref, self_heads_ref, self_weights_ref,
    proj_ref, hidden_ref, normed_ref,
    dk_ref, dv_ref, grad_first_ref, gain_grad_ref, shift_grad_ref, bias_grad_ref,
    term_ref, theirs_ref, mine_ref, self_gain_grad_ref, self_shift_grad_ref, dq_sum_ref, dv_sum_ref,
    low_ref, self_dq_ref, self_dk_ref, self_dv_ref,
):
    grad_heads = dot(low_in_ref[...], wo_ref[...], 1, 1).astype(bf16)
    pairs = q_ref.shape[1] // PAIR
    dqs = []
    for pair in range(pairs):
        lanes = lanes_of(pair)
        dq, dk, dv = pair_backward(
            q_ref[:, lanes], k_ref[:, lanes], v_ref[:, lanes], weights_ref, 2 * pair,
            inverse_ref[:, lanes], heads_ref[:, lanes], grad_heads[:, lanes],
        )
        dqs.append(dq)
        dk_ref[lanes, :] = dk
        dv_ref[lanes, :] = dv
    dk_ref.send()
    dv_ref.send()
    incoming = own_term_ref[...] + dot(jnp.concatenate(dqs, axis=1), wq_ref[...], 1, 1)
    unit, inverse = norm_unit(first_ref[...])
    gain_grad_ref[...] = column_sum(incoming * unit)
    shift_grad_ref[...] = column_sum(incoming)
    grad_first = grad_second_ref[...] + norm_backward(incoming, unit, inverse, gain_ref[1:2, :])
    grad_first_ref[...] = grad_first
    grad_first_ref.send()
    low = grad_first.astype(bf16)
    low_ref[...] = low
    bias_grad_ref[...] = column_sum(grad_first)

    grad_heads = dot(low, out_ref[0], 1, 1).astype(bf16)
    for pair in range(pairs):
        lanes = lanes_of(pair)
        dq, dk, dv = pair_backward(
            self_q_ref[:, lanes], self_k_ref[:, lanes], self_v_ref[:, lanes], self_weights_ref, 2 * pair,
            self_inverse_ref[:, lanes], self_heads_ref[:, lanes], grad_heads[:, lanes],
        )
        self_dq_ref[:, lanes] = dq
        self_dk_ref[lanes, :] = dk
        self_dv_ref[lanes, :] = dv
    projection_grads(
        core_ref[0], normed_ref, normed_ref, low_ref, self_dq_ref, self_dk_ref, self_dv_ref, self_heads_ref,
        theirs_ref, mine_ref,
    )
    incoming = dot(self_dq_ref[...], proj_ref[0], 1, 1) + (
        dot(self_dk_ref[...], proj_ref[1], 0, 1) + dot(self_dv_ref[...], proj_ref[2], 0, 1)
    )
    term_ref[...] = incoming
    term_ref.send()
    unit, _ = norm_unit(hidden_ref[...].astype(f32))
    self_gain_grad_ref[...] = column_sum(incoming * unit)
    self_shift_grad_ref[...] = column_sum(incoming)
    dq_sum_ref[...] = column_sum(self_dq_ref[...].astype(f32))
    dv_sum_ref[...] = row_sums(self_dv_ref[...])


def other_back(
    core, low, wo, wq, q, k, v, weights, inverse, heads, own_term, first, grad_second, gain,
    out_proj, proj, self_q, self_k, self_v, self_weights, self_inverse, self_heads, hidden, normed,
):
    rows, width = first.shape
    columns, half = k.shape
    vector = shaped((1, width), f32)
    grads = shaped((4, width // 2, half), f32)
    return call(
        other_back_kernel,
        "other_back",
        [
            shaped((half, columns), bf16),
            shaped((half, columns), bf16),
            shaped((rows, width), f32),
            vector,
            vector,
            vector,
            shaped((rows, width), f32),
            grads,
            grads,
            vector,
            vector,
            shaped((1, half), f32),
            shaped((8, half), f32),
            shaped((rows, width), bf16),
            shaped((rows, half), bf16),
            shaped((half, rows), bf16),
            shaped((half, rows), bf16),
        ],
        20 * rows * width * half + 24 * rows * (columns + rows) * half,
        (core,),
        low, wo, q, k, v, inverse, heads, (weights, half // PAIR), wq, own_term, first, grad_second, gain,
        (out_proj, 2, 0), self_q, self_k, self_v, self_inverse, self_heads, (self_weights, half // PAIR),
        (proj, 3), hidden, normed,
    )


def encoder_grad_kernel(dk0_ref, dv0_ref, dk1_ref, dv1_ref, proj_ref, wk1_ref, wv1_ref, out_ref):
    own = dot(dk0_ref[...], proj_ref[1], 0, 1) + dot(dv0_ref[...], proj_ref[2], 0, 1)
    other = dot(dk1_ref[...], wk1_ref[...], 0, 1) + dot(dv1_ref[...], wv1_ref[...], 0, 1)
    out_ref[:, 0, :] = own + other


def encoder_grad(dk0, dv0, dk1, dv1, proj, wk1, wv1, frames):
    half, padded = dk0.shape
    width = wk1.shape[0]
    grad_block = pl.BlockSpec((half, FRAME_BLOCK), lambda i: (0, i))
    weight = pl.BlockSpec(wk1.shape, lambda i: (0, 0))
    return pl.pallas_call(
        encoder_grad_kernel,
        grid=(padded // FRAME_BLOCK,),
        in_specs=[grad_block] * 4 + [pl.BlockSpec(proj.shape, lambda i: (0, 0, 0)), weight, weight],
        out_specs=pl.BlockSpec((FRAME_BLOCK, 1, width), lambda i: (i, 0, 0)),
        out_shape=shaped((frames, 1, width), f32),
        compiler_params=pltpu.CompilerParams(vmem_limit_bytes=VMEM_LIMIT),
        cost_estimate=pl.CostEstimate(
            flops=8 * half * padded * width, bytes_accessed=6 * frames * width, transcendentals=0
        ),
        name="encoder_grad",
    )(dk0, dv0, dk1, dv1, proj, wk1, wv1)


def swap(value):
    return lax.ppermute(value, "tensor", [(0, 1), (1, 0)])


def tie(*values):
    return lax.optimization_barrier(values)


class Scatter:
    def __init__(self, theirs, mine, turned=False):
        self.members = lax.axis_size("dp")
        self.bits = self.members.bit_length() - 1
        self.order = list(range(self.bits))
        if turned and self.bits > 2:
            self.order = [0] + self.order[2:] + [1]
        self.stage = 0
        self.theirs, self.mine = theirs, mine

    def launch(self):
        if self.stage == self.bits:
            return
        other = 1 << self.order[self.stage]
        self.received = lax.ppermute(self.theirs, "dp", [(i, i ^ other) for i in range(self.members)])

    def land(self):
        if self.stage == self.bits:
            return
        mine, received = self.mine, self.received
        if self.stage == 0:
            lead = mine.shape[:-2]
            self.lead = len(lead)
            cuts = self.bits - 1
            shape = lead + (2,) * cuts + (mine.shape[-2] >> cuts, mine.shape[-1])
            mine, received = mine.reshape(shape), received.reshape(shape)
        self.stage += 1
        if self.stage < self.bits:
            bit = self.order[self.stage]
            axis = self.lead + self.bits - 1 - bit
            side = (lax.axis_index("dp") >> bit) & 1

            def half(which):
                return lax.dynamic_index_in_dim(mine, which, axis, keepdims=True) + lax.dynamic_index_in_dim(
                    received, which, axis, keepdims=True
                )

            self.theirs = half(1 - side)
            self.mine = half(side)
        else:
            total = mine + received
            self.part = total.reshape(total.shape[: self.lead] + total.shape[-2:])

    def finish(self):
        while self.stage < self.bits:
            self.land()
            self.launch()
        return self.part


def place_kernel(moves, gathered_ref, *refs):
    outs, (held, in_sems, out_sems) = refs[:-3], refs[-3:]
    reads = [
        pltpu.make_async_copy(gathered_ref.at[i], held.at[i], in_sems.at[i]) for i in range(held.shape[0])
    ]
    for read in reads:
        read.start()
    writes = []
    for i, read in enumerate(reads):
        read.wait()
        for start, count, out, target in moves[i]:
            writes.append(
                pltpu.make_async_copy(
                    held.at[i, pl.ds(start, count)], outs[out].at[target], out_sems.at[len(writes)]
                )
            )
            writes[-1].start()
    for write in writes:
        write.wait()


def place(gathered, width, units):
    members, total, half = gathered.shape
    parts = members // 2
    rows = units // members
    count = width // members
    proj = shaped((3, width, half), f32)
    outs = [shaped((units, width), f32), shaped((width, units), f32), proj, proj, shaped((2, half, width), f32)]
    if count % 8 == 0:
        moves = []
        for i in range(members):
            q, c = i // 2, i % 2
            moves.append([])
            for j in range(2):
                columns = pl.ds(j * half, half)
                moves[i].append((j * rows, rows, 0, (pl.ds(c * width + q * rows, rows), columns)))
                columns = pl.ds(c * width + j * half, half)
                moves[i].append(((2 + j) * rows, rows, 1, (pl.ds(q * rows, rows), columns)))
            here = pl.ds(c * (width // 2) + q * count, count)
            for branch in range(2):
                start = 4 * rows + branch * 4 * count
                for a in range(3):
                    moves[i].append((start + a * count, count, 2 + branch, (a, here)))
                target = (1 - branch, pl.ds(q * count, count), pl.ds(c * half, half))
                moves[i].append((start + 3 * count, count, 4, target))
        anywhere = pl.BlockSpec(memory_space=pl.ANY)
        return pl.pallas_call(
            partial(place_kernel, moves),
            in_specs=[anywhere],
            out_specs=[anywhere] * len(outs),
            out_shape=outs,
            scratch_shapes=[
                pltpu.VMEM(gathered.shape, f32),
                pltpu.SemaphoreType.DMA((members,)),
                pltpu.SemaphoreType.DMA((sum(len(m) for m in moves),)),
            ],
            compiler_params=pltpu.CompilerParams(vmem_limit_bytes=VMEM_LIMIT),
            cost_estimate=pl.CostEstimate(flops=0, bytes_accessed=8 * gathered.size, transcendentals=0),
            name="place",
        )(gathered)
    split = gathered[:, : 4 * rows].reshape(parts, 2, 2, 2, rows, half)
    fc2 = split[:, :, 0].transpose(1, 0, 3, 2, 4).reshape(units, width)
    fc1 = split[:, :, 1].transpose(0, 3, 1, 2, 4).reshape(width, units)
    split = gathered[:, 4 * rows :].reshape(parts, 2, 2, 4, count, half)
    projections = split[:, :, :, :3].transpose(2, 3, 1, 0, 4, 5).reshape(2, 3, width, half)
    outputs = split[:, :, ::-1, 3].transpose(2, 0, 3, 1, 4).reshape(2, half, width)
    return fc2, fc1, projections[0], projections[1], outputs


def per_device(
    hidden,
    encoder,
    text_len,
    audio_len,
    corpus_weight,
    cotangent,
    norm_gain,
    norm_bias,
    self_proj,
    self_bias,
    cross_proj,
    cross_bias,
    out_proj,
    out_bias,
    fc1_weight,
    fc1_bias,
    fc2_weight,
    fc2_bias,
):
    sequences, frames, width = encoder.shape
    members = lax.axis_size("dp")
    me = lax.axis_index("dp")
    half = self_proj.shape[2]
    padded = -(-frames // FRAME_BLOCK) * FRAME_BLOCK
    core = (me & 1).astype(jnp.int32).reshape(1)

    proj_rows = cross_proj.reshape(-1, half)
    count = (proj_rows.shape[0] + width) // members
    turn = me - proj_rows.shape[0] // count
    per_block = half // count
    part = jnp.where(
        turn < 0,
        lax.dynamic_slice_in_dim(proj_rows, me * count, count, 0),
        lax.dynamic_slice(
            out_proj, (1, (turn % per_block) * count, (turn // per_block) * half), (1, count, half)
        )[0],
    )
    part = swap(part.astype(f32))
    hidden_in, part = tie(hidden, part)
    gathered = lax.all_gather(part, "dp", axis=0, tiled=True)

    normed_self, q_self, k_self, v_self, weights_self, inverse_self, heads_self, partial_self = self_forward(
        text_len, hidden_in, norm_gain, norm_bias, self_proj, self_bias, out_proj
    )
    received = swap(partial_self)
    other_bias = swap(cross_bias)

    frames_in = jnp.pad(encoder.reshape(frames, width), ((0, padded - frames), (0, 0)))
    k_own = dot(frames_in, cross_proj[1], 1, 0).astype(bf16)
    v_own = (dot(frames_in, cross_proj[2], 1, 0) + cross_bias[1]).astype(bf16)
    received, k_own, v_own = tie(received, k_own, v_own)
    first, normed_cross, q_own, weights_own, inverse_own, heads_own, term_own = cross_own(
        audio_len, hidden, partial_self, received, out_bias, norm_gain, norm_bias,
        cross_proj, cross_bias, k_own, v_own, out_proj,
    )
    gathered, normed_cross = tie(gathered, normed_cross)
    (
        q_other, k_other, v_other, weights_other, inverse_other, heads_other,
        wq_other, wk_other, wv_other, wo_other,
        second, partial_normed, fc2_theirs, fc1_theirs, fc2_mine, fc1_mine, partial_mlp,
        fc1_bias_grad, fc2_bias_grad,
    ) = late_forward(
        audio_len, text_len, corpus_weight, core, gathered, normed_cross, frames_in, other_bias, term_own, first,
        out_bias, norm_gain, norm_bias, fc1_weight, fc1_bias.reshape(1, -1), cotangent, fc2_weight,
    )
    received = swap(partial_normed)
    fc2_share = Scatter(fc2_theirs, fc2_mine)
    fc1_share = Scatter(fc1_theirs, fc1_mine, turned=True)
    fc2_share.launch()
    fc1_share.launch()
    fc2_share.land()
    fc2_share.launch()
    fc1_share.land()
    fc1_share.launch()

    (
        grad_second, second_low, gain_mlp, shift_mlp, bias_cross, dq_own, dk_own, dv_own, back_own,
        dq_cross_sum, dv_cross_sum, cross_theirs, cross_mine,
    ) = cross_own_back(
        text_len, corpus_weight, core, cotangent, second, partial_normed, received, norm_gain,
        out_proj, cross_proj, q_own, k_own, v_own, weights_own, inverse_own, heads_own, normed_cross, frames_in,
    )
    cross_theirs, fc2_share.received, fc1_share.received = tie(
        cross_theirs, fc2_share.received, fc1_share.received
    )
    cross_share = Scatter(cross_theirs, cross_mine)
    cross_share.launch()
    fc2_share.land()
    fc1_share.land()
    fc2_share.launch()
    fc1_share.launch()
    cross_share.received, fc2_share.theirs, fc1_share.theirs = tie(
        cross_share.received, fc2_share.theirs, fc1_share.theirs
    )
    cross_share.land()
    second_low, cross_share.theirs = tie(second_low, cross_share.theirs)
    cross_share.launch()

    (
        dk_other, dv_other, grad_first, gain_cross, shift_cross, bias_self, partial_normed,
        self_theirs, self_mine, gain_self, shift_self, dq_self_sum, dv_self_sum, *_,
    ) = other_back(
        core, second_low, wo_other, wq_other, q_other, k_other, v_other, weights_other, inverse_other, heads_other,
        back_own, first, grad_second, norm_gain, out_proj, self_proj, q_self, k_self, v_self, weights_self,
        inverse_self, heads_self, hidden, normed_self,
    )
    self_theirs, cross_share.received, fc1_share.received, fc2_share.received = tie(
        self_theirs, cross_share.received, fc1_share.received, fc2_share.received
    )
    self_share = Scatter(self_theirs, self_mine)
    self_share.launch()
    fc2_share.land()
    fc2_share.launch()
    cross_share.received, fc2_share.theirs = tie(cross_share.received, fc2_share.theirs)
    cross_share.land()
    self_share.land()
    self_share.theirs, cross_share.theirs, partial_normed, dk_own = tie(
        self_share.theirs, cross_share.theirs, partial_normed, dk_own
    )
    self_share.launch()
    cross_share.launch()
    received = swap(partial_normed)
    grad_encoder = encoder_grad(
        dk_own, dv_own, dk_other, dv_other, cross_proj, wk_other, wv_other, frames
    ).reshape(encoder.shape)
    cross_share.received, fc1_share.received, partial_normed, grad_encoder = tie(
        cross_share.received, fc1_share.received, partial_normed, grad_encoder
    )
    cross_share.land()
    fc1_share.land()
    cross_share.launch()
    self_share.received, cross_share.theirs = tie(self_share.received, cross_share.theirs)
    self_share.land()
    self_share.launch()
    fc1_share.theirs, self_share.theirs, hidden = tie(fc1_share.theirs, self_share.theirs, hidden)
    fc1_share.launch()
    cross_share.received, fc2_share.received, fc1_share.received, grad_encoder, _ = tie(
        cross_share.received, fc2_share.received, fc1_share.received, grad_encoder, self_share.theirs
    )
    cross_part = cross_share.finish()
    fc2_part = fc2_share.finish()
    fc1_part = fc1_share.finish()

    most = [fc2_part[:, :half], fc2_part[:, half:], fc1_part[:, :half], fc1_part[:, half:]]
    most = jnp.concatenate([item.reshape(-1, half) for item in (*most, cross_part)], axis=0)
    unit_self, root_self = norm_unit(hidden.astype(f32))
    grad_hidden = (
        grad_first + norm_backward(partial_normed + received, unit_self, root_self, norm_gain[0])
    ).astype(bf16)
    grad_hidden, most, self_share.received = tie(grad_hidden, most, self_share.received)
    self_part = self_share.finish()
    every = jnp.concatenate([most, self_part.reshape(-1, half)], axis=0)

    small = (
        gain_self,
        shift_self,
        gain_cross,
        gain_mlp,
        shift_cross,
        shift_mlp,
        dq_self_sum,
        dv_self_sum,
        dq_cross_sum,
        dv_cross_sum,
        bias_self,
        bias_cross,
        fc1_bias_grad,
        fc2_bias_grad,
    )
    *small, partial_mlp, every = tie(*small, partial_mlp, every)
    every = lax.all_gather(every, "dp", axis=0, tiled=False)
    small[7] = small[7][0:1]
    small[9] = small[9][0:1]
    norm_self = jnp.concatenate(small[0:2], axis=0)
    small = [norm_self + swap(norm_self)] + small[2:]
    flat = jnp.concatenate([item.reshape(-1, half) for item in small], axis=0)
    for bit in range(members.bit_length() - 1):
        flat = flat + lax.ppermute(flat, "dp", [(i, i ^ (1 << bit)) for i in range(members)])
    received_mlp = swap(partial_mlp)
    result = (second + (partial_mlp + received_mlp) + fc2_bias).astype(bf16)
    fc2_weight_grad, fc1_weight_grad, cross_proj_grad, self_proj_grad, out_proj_grad = place(
        every, width, fc2_weight.shape[0]
    )
    small_out = []
    offset = 0
    for item in small:
        count = item.size // half
        small_out.append(flat[offset : offset + count].reshape(item.shape))
        offset += count
    (
        norm_self, gain_cross, gain_mlp, shift_cross, shift_mlp, dq_self_sum, dv_self_sum, dq_cross_sum,
        dv_cross_sum, bias_self, bias_cross, fc1_bias_grad, fc2_bias_grad,
    ) = small_out
    return (
        result,
        grad_hidden,
        grad_encoder,
        jnp.concatenate([norm_self[0:1], gain_cross, gain_mlp], axis=0),
        jnp.concatenate([norm_self[1:2], shift_cross, shift_mlp], axis=0),
        self_proj_grad,
        jnp.concatenate([dq_self_sum, dv_self_sum], axis=0),
        cross_proj_grad,
        jnp.concatenate([dq_cross_sum, dv_cross_sum], axis=0),
        out_proj_grad,
        jnp.concatenate([bias_self, bias_cross], axis=0),
        fc1_weight_grad,
        fc1_bias_grad.reshape(-1),
        fc2_weight_grad,
        fc2_bias_grad.reshape(-1),
    )


def solution(mesh):
    placed = (
        P("dp", None),
        P("dp", None, None),
        P("dp"),
        P("dp"),
        P("dp"),
        P("dp", None),
        P(),
        P(),
        P(None, None, "tensor"),
        P(None, "tensor"),
        P(None, None, "tensor"),
        P(None, "tensor"),
        P(None, "tensor", None),
        P(),
        P(None, "tensor"),
        P("tensor"),
        P("tensor", None),
        P(),
    )
    return jax.shard_map(
        per_device,
        mesh=mesh,
        in_specs=placed,
        out_specs=(
            P("dp", None),
            P("dp", None),
            P("dp", None, None),
            P(),
            P(),
            P(None, None, "tensor"),
            P(None, "tensor"),
            P(None, None, "tensor"),
            P(None, "tensor"),
            P(None, "tensor", None),
            P(),
            P(None, "tensor"),
            P("tensor"),
            P("tensor", None),
            P(),
        ),
        check_vma=False,
    )
```
